256 devices in a mesh: row: 16 (over z, core), col: 16 (over x, y).
Axes of the slice: x: 4, y: 4, z: 8, core: 2. Of those that a mesh axis runs over, the one named last changes fastest.
Arguments:
- matrix: float32 [4, 16, 128, 4, 16, 128], P(None, 'row', None, None, 'col'), may hold values from 0 to 3.5, as said below
Outputs:
- factored: float32 [4, 16, 128, 4, 16, 128], P(None, 'row', None, None, 'col')
The draws below stay inside these ranges and needn't reach their ends.
Inputs may be any that keep to these rules, and one draw needn't show every extreme that they name: matrix is symmetric, and its smallest eigenvalue is at least 0.5.
All inputs are finite; a program needn't handle non-finite values.
Results may differ from the reference program's by a relative error of at most 0.00016.
Values sent between devices are 32-bit elements; how exact they have to be, the bound alone decides.
A program may use at most 64 MiB of HBM per device.

```python
import math
import jax
import jax.numpy as jnp
from jax import lax

NB = 128
ORDER = 8192
RB = 4
CB = 4
N_ROW = 16
N_COL = 16


def draw_matrix(key, part):
    key = jax.random.fold_in(key, 7)
    point_key, nugget_key = jax.random.split(key)
    points = jax.random.uniform(point_key, (ORDER, 3), jnp.float32)
    nugget = jnp.exp(jax.random.uniform(nugget_key, (ORDER,), jnp.float32, math.log(0.5), math.log(2.0)))
    long_radius = 0.3
    short_radius = 1.5 * (1.0 / ORDER) ** (1.0 / 3.0)
    columns_index = lax.iota(jnp.int32, ORDER)

    def one_block(start):
        near = lax.dynamic_slice_in_dim(points, start, NB, 0)
        offset = near[:, None, :] - points[None, :, :]
        distance = jnp.sqrt(offset[:, :, 0] ** 2 + offset[:, :, 1] ** 2 + offset[:, :, 2] ** 2)
        kernel = jnp.exp(-distance / long_radius) + 0.5 * jnp.exp(-distance / short_radius)
        row_index = start + lax.iota(jnp.int32, NB)
        on_diagonal = (row_index[:, None] == columns_index[None, :]).astype(jnp.float32)
        extra = lax.dynamic_slice_in_dim(nugget, start, NB, 0)
        return kernel + on_diagonal * extra[:, None]
    starts = lax.iota(jnp.int32, ORDER // NB) * NB
    square = lax.map(one_block, starts).reshape(ORDER, ORDER)
    return square.reshape(RB, N_ROW, NB, CB, N_COL, NB)


def setup_inputs(seed: int = 0) -> dict:
    arg_keys = jax.random.split(jax.random.key(seed), 2)
    return {
        "matrix": draw_matrix(jax.random.fold_in(arg_keys[1], 71), 0),
    }


def reference(matrix):
    square = matrix.reshape(ORDER, ORDER)
    for panel in range(2):
        first = panel * NB
        after = first + NB
        factor_tile = jnp.linalg.cholesky(square[first:after, first:after])
        beneath = square[after:, first:after]
        panel_tile = jax.scipy.linalg.solve_triangular(factor_tile, beneath.T, lower=True).T
        trailing = square[after:, after:] - jnp.dot(panel_tile, panel_tile.T, precision=lax.Precision.HIGHEST)
        top_strip = jnp.concatenate([square[first:after, :first], factor_tile, jnp.zeros((NB, ORDER - after), jnp.float32)], axis=1)
        bottom_strip = jnp.concatenate([square[after:, :first], panel_tile, trailing], axis=1)
        square = jnp.concatenate([square[:first], top_strip, bottom_strip], axis=0)
    return square.reshape(RB, N_ROW, NB, CB, N_COL, NB)
```

```python
import functools

import jax
import jax.numpy as jnp
from jax import lax
from jax.experimental import pallas as pl
from jax.experimental.pallas import tpu as pltpu
from jax.sharding import PartitionSpec as P

F32 = jnp.float32
MESH = pl.DeviceIdType.MESH
HIGHEST = lax.Precision.HIGHEST
NB = 128
LOOK = 2


def dot_nn(a, b):
    return jnp.dot(a, b, precision=HIGHEST, preferred_element_type=F32)


def dot_nt(a, b):
    return lax.dot_general(
        a, b, (((1,), (1,)), ((), ())), precision=HIGHEST, preferred_element_type=F32
    )


def row_splat(tile, k):
    return jnp.broadcast_to(tile[k : k + 1, :], (8, NB))


def lane_splat(tile, k):
    return jnp.broadcast_to(tile[:, k : k + 1], (8, NB))


def eliminate(rows, rows_identity, columns):
    sub = lax.broadcasted_iota(jnp.int32, (8, NB), 0)
    columns = list(columns)
    upper, inverse, solved = rows, rows_identity, rows_identity
    scale = jnp.ones((8, NB), F32)
    for k in range(8):
        pivot = row_splat(columns[k], k)
        over = 1.0 / pivot
        here = sub == k
        ratio = columns[k] * over
        below = jnp.where(sub > k, ratio, 0.0)
        for j in range(k + 1, 8):
            r = row_splat(columns[j], k)
            columns[j] = jnp.where(here, r * over, columns[j] - ratio * r)
        upper = upper - below * row_splat(upper, k)
        inverse = inverse - below * row_splat(inverse, k)
        r = row_splat(solved, k)
        solved = jnp.where(here, r * over, solved - ratio * r)
        scale = jnp.where(here, lax.rsqrt(pivot), scale)
    return upper * scale, inverse * scale, solved


def factor(work, solved_rows, upper, inverse):
    lane = lax.broadcasted_iota(jnp.int32, (8, NB), 1)
    sub = lax.broadcasted_iota(jnp.int32, (8, NB), 0)
    solved_rows[...] = jnp.zeros((NB, NB), F32)
    steps = NB // 8
    for t in range(steps):
        o = 8 * t
        rows = work[o : o + 8, :]
        columns = [lane_splat(rows, o + j) for j in range(8)]
        block = (lane >= o) & (lane < o + 8)
        rows_identity = jnp.where(block, (lane - o == sub).astype(F32), rows)
        up, inv, solved = eliminate(rows, rows_identity, columns)
        upper[o : o + 8, :] = jnp.where(lane >= o, up, 0.0)
        inverse[o : o + 8, :] = jnp.where(lane < o + 8, inv, 0.0)
        solved_rows[o : o + 8, :] = solved
        splats = [row_splat(solved, j) for j in range(8)]
        for i in range(t + 1, min(t + 1 + LOOK, steps)):
            tile = work[8 * i : 8 * i + 8, :]
            total = jnp.where(block, 0.0, tile)
            for j in range(8):
                total = total - lane_splat(tile, o + j) * splats[j]
            work[8 * i : 8 * i + 8, :] = total
        rest = 8 * (t + 1 + LOOK)
        if rest < NB:
            tiles = work[rest:, :]
            lanes = lax.broadcasted_iota(jnp.int32, (NB - rest, NB), 1)
            own = (lanes >= o) & (lanes < o + 8)
            work[rest:, :] = jnp.where(own, 0.0, tiles) - dot_nn(
                jnp.where(own, tiles, 0.0), solved_rows[...]
            )


def kernel(
    n,
    x_hbm,
    out_hbm,
    xv,
    panel,
    s0,
    s1,
    rbuf,
    cbuf,
    work,
    solved_rows,
    u0,
    w0,
    u1,
    w1,
    w10,
    ac,
    pr,
    pc,
    outv,
    load_sem,
    store_sem,
    s0_piece,
    s0_gather,
    s0_send_a,
    s0_send_b,
    s0_send_c,
    s1_piece,
    s1_gather,
    s1_send_a,
    s1_send_b,
    s1_send_c,
    r_piece,
    r_gather,
    r_send_a,
    r_send_b,
    c_piece,
    c_gather,
    c_send_a,
    c_send_b,
    c_pair,
    c_pair_send,
):
    r = lax.axis_index("row")
    c = lax.axis_index("col")

    def each(body, count=n - 1):
        def step(k, carry):
            body(k)
            return carry

        lax.fori_loop(1, count + 1, step, 0)

    def other(me, k):
        return lax.rem(me + k, n)

    def copy(src, dst, send, recv, row, col):
        return pltpu.make_async_remote_copy(
            src_ref=src,
            dst_ref=dst,
            send_sem=send,
            recv_sem=recv,
            device_id=(row, col),
            device_id_type=MESH,
        )

    load = pltpu.make_async_copy(x_hbm, xv, load_sem)
    load.start()
    barrier = pltpu.get_barrier_semaphore()

    def greet(k):
        pl.semaphore_signal(barrier, inc=1, device_id=(r, other(c, k)), device_id_type=MESH)
        pl.semaphore_signal(barrier, inc=1, device_id=(other(r, k), c), device_id_type=MESH)

    each(greet)
    load.wait()

    @pl.when(c < 2)
    def _():
        panel[...] = xv[pl.ds(0, 512, stride=4), :]

    pl.semaphore_wait(barrier, 2 * (n - 1))

    def s0_scatter(k):
        p = other(c, k)
        return copy(
            panel.at[pl.ds(pl.multiple_of(p * 8, 8), 8)], s0.at[p], s0_send_a.at[p], s0_piece, r, p
        )

    def s1_scatter(k):
        p = other(c, k)
        return copy(
            panel.at[pl.ds(pl.multiple_of(p * 8, 8), 8)],
            s1.at[p, c],
            s1_send_a.at[p],
            s1_piece.at[c],
            r,
            p,
        )

    def r_scatter(k):
        p = other(c, k)
        return copy(
            panel.at[pl.ds(pl.multiple_of(p * 32, 32), 32)],
            rbuf.at[p, c],
            r_send_a.at[p],
            r_piece.at[c],
            r,
            p,
        )

    def c_scatter(k):
        p = other(r, k)
        return copy(
            xv.at[pl.ds(pl.multiple_of(p * 32, 32), 32)],
            cbuf.at[lax.rem(p, 2), p // 2, r],
            c_send_a.at[p],
            c_piece.at[r],
            p,
            c,
        )

    def s0_down(k):
        p = other(r, k)
        return copy(s0.at[c], s0.at[c], s0_send_b.at[p], s0_piece, p, c)

    def s1_down(k):
        p = other(r, k)
        return copy(s1.at[c], s1.at[c], s1_send_b.at[p], s1_piece.at[0], p, c)

    def s0_across(k):
        p = other(c, k)
        return copy(s0.at[c], s0.at[c], s0_send_c.at[p], s0_gather.at[c], r, p)

    def s1_across(k):
        p = other(c, k)
        return copy(s1.at[c], s1.at[c], s1_send_c.at[p], s1_gather.at[c], r, p)

    def r_across(k):
        p = other(c, k)
        return copy(rbuf.at[c], rbuf.at[c], r_send_b.at[p], r_gather.at[c], r, p)

    parity = lax.rem(r, 2)
    pair = r + 1 - 2 * parity
    half = r // 2

    def c_down(k):
        p = lax.rem(r + 2 * k, n)
        return copy(
            cbuf.at[parity, half], cbuf.at[parity, half], c_send_b.at[p], c_gather.at[r], p, c
        )

    def c_across():
        return copy(cbuf.at[parity], cbuf.at[parity], c_pair_send, c_pair, pair, c)

    def start(make):
        return lambda k: make(k).start()

    def sent(make):
        return lambda k: make(k).wait_send()

    def arrive(buffer, sem):
        pltpu.make_async_copy(buffer, buffer, sem).wait()

    corner = jnp.logical_and(r == 0, c == 0)
    second = jnp.logical_and(r == 1, c < 2)

    def scatters():
        @pl.when(second)
        def _():
            each(start(s1_scatter))
            s1[c, c] = panel[pl.ds(pl.multiple_of(c * 8, 8), 8), :]

        @pl.when(c < 2)
        def _():
            each(start(r_scatter))
            rbuf[c, c] = panel[pl.ds(pl.multiple_of(c * 32, 32), 32), :]

        @pl.when(r < 2)
        def _():
            each(start(c_scatter))
            cbuf[parity, half, r] = xv[pl.ds(pl.multiple_of(r * 32, 32), 32), :]

    @pl.when(corner)
    def _():
        each(start(s0_scatter))
        s0[c] = panel[pl.ds(pl.multiple_of(c * 8, 8), 8), :]

    @pl.when(jnp.logical_not(corner))
    def _():
        scatters()
        arrive(s0.at[c], s0_piece)

    @pl.when(r == 0)
    def _():
        each(start(s0_down))

    each(start(s0_across))

    @pl.when(corner)
    def _():
        scatters()

    @pl.when(r == 1)
    def _():
        @pl.when(c != 0)
        def _():
            arrive(s1.at[c, 0], s1_piece.at[0])

        @pl.when(c != 1)
        def _():
            arrive(s1.at[c, 1], s1_piece.at[1])

        each(start(s1_down))

    @pl.when(r != 1)
    def _():
        arrive(s1.at[c], s1_piece.at[0])

    each(start(s1_across))

    @pl.when(c != 0)
    def _():
        arrive(rbuf.at[c, 0], r_piece.at[0])

    @pl.when(c != 1)
    def _():
        arrive(rbuf.at[c, 1], r_piece.at[1])

    each(start(r_across))

    @pl.when(r != 0)
    def _():
        arrive(cbuf.at[parity, half, 0], c_piece.at[0])

    @pl.when(r != 1)
    def _():
        arrive(cbuf.at[parity, half, 1], c_piece.at[1])

    each(start(c_down), n // 2 - 1)

    def s0_wait(k):
        p = other(c, k)
        arrive(s0.at[p], s0_gather.at[p])

    each(s0_wait)
    work[...] = s0[...].reshape(NB, NB)
    factor(work, solved_rows, u0, w0)

    def s1_wait(k):
        p = other(c, k)
        arrive(s1.at[p], s1_gather.at[p])

    each(s1_wait)
    l10 = dot_nt(s1[:, 0].reshape(NB, NB), w0[...])
    work[...] = s1[:, 1].reshape(NB, NB) - dot_nt(l10, l10)
    w10[...] = dot_nn(l10, w0[...])

    def c_wait(k):
        p = lax.rem(r + 2 * k, n)
        arrive(cbuf.at[parity, p // 2], c_gather.at[p])

    each(c_wait, n // 2 - 1)
    c_across().start()

    factor(work, solved_rows, u1, w1)
    w10[...] = -dot_nn(w1[...], w10[...])

    def r_wait(k):
        p = other(c, k)
        arrive(rbuf.at[p], r_gather.at[p])

    each(r_wait)
    r0 = rbuf[:, 0].reshape(4 * NB, NB)
    r1 = rbuf[:, 1].reshape(4 * NB, NB)
    pr[:, 0:NB] = dot_nt(r0, w0[...])
    pr[:, NB:] = dot_nt(r0, w10[...]) + dot_nt(r1, w1[...])

    c_across().wait()
    for p in range(n):
        for h in range(2):
            for b in range(4):
                ac[h * NB + 8 * p : h * NB + 8 * p + 8, b * NB : (b + 1) * NB] = cbuf[
                    p % 2, p // 2, h, pl.ds(b, 8, stride=4), :
                ]
    pc[0:NB, :] = dot_nn(w0[...], ac[0:NB, :])
    pc[NB:, :] = dot_nn(w10[...], ac[0:NB, :]) + dot_nn(w1[...], ac[NB:, :])

    for a in range(4):
        update = dot_nn(pr[a * NB : (a + 1) * NB, :], pc[...])
        for b in range(4):
            at = pl.ds(a * 512 + b, NB, stride=4)
            outv[at, :] = xv[at, :] - update[:, b * NB : (b + 1) * NB]

    @pl.when(c == 0)
    def _():
        for a in range(4):
            outv[pl.ds(a * 512, NB, stride=4), :] = pr[a * NB : (a + 1) * NB, 0:NB]

    @pl.when(c == 1)
    def _():
        for a in range(4):
            outv[pl.ds(a * 512, NB, stride=4), :] = pr[a * NB : (a + 1) * NB, NB:]

    @pl.when(r < 2)
    def _():
        keep = jnp.logical_and(r == 1, c == 0)
        first = outv[pl.ds(0, NB, stride=4), :]
        outv[0:512, :] = jnp.zeros((512, NB), F32)
        outv[pl.ds(0, NB, stride=4), :] = jnp.where(keep, first, 0.0)

        @pl.when(corner)
        def _():
            outv[pl.ds(0, NB, stride=4), :] = u0[...].T

        @pl.when(jnp.logical_and(r == 1, c == 1))
        def _():
            outv[pl.ds(0, NB, stride=4), :] = u1[...].T

    store = pltpu.make_async_copy(outv, out_hbm, store_sem)
    store.start()

    @pl.when(corner)
    def _():
        each(sent(s0_scatter))

    @pl.when(second)
    def _():
        each(sent(s1_scatter))

    @pl.when(c < 2)
    def _():
        each(sent(r_scatter))

    @pl.when(r < 2)
    def _():
        each(sent(c_scatter))

    @pl.when(r == 0)
    def _():
        each(sent(s0_down))

    @pl.when(r == 1)
    def _():
        each(sent(s1_down))

    each(sent(s0_across))
    each(sent(s1_across))
    each(sent(r_across))
    each(sent(c_down), n // 2 - 1)
    store.wait()


def per_device(matrix):
    n = lax.axis_size("row")
    flat = matrix.reshape(2048, NB)
    dma = pltpu.SemaphoreType.DMA
    square = pltpu.VMEM((NB, NB), F32)
    out = pl.pallas_call(
        functools.partial(kernel, n),
        out_shape=jax.ShapeDtypeStruct((2048, NB), F32),
        in_specs=[pl.BlockSpec(memory_space=pl.ANY)],
        out_specs=pl.BlockSpec(memory_space=pl.ANY),
        scratch_shapes=[
            pltpu.VMEM((2048, NB), F32),
            pltpu.VMEM((512, NB), F32),
            pltpu.VMEM((n, 8, NB), F32),
            pltpu.VMEM((n, 2, 8, NB), F32),
            pltpu.VMEM((n, 2, 32, NB), F32),
            pltpu.VMEM((2, n // 2, 2, 32, NB), F32),
            square,
            square,
            square,
            square,
            square,
            square,
            square,
            pltpu.VMEM((2 * NB, 4 * NB), F32),
            pltpu.VMEM((4 * NB, 2 * NB), F32),
            pltpu.VMEM((2 * NB, 4 * NB), F32),
            pltpu.VMEM((2048, NB), F32),
            dma,
            dma,
            dma,
            dma((n,)),
            dma((n,)),
            dma((n,)),
            dma((n,)),
            dma((2,)),
            dma((n,)),
            dma((n,)),
            dma((n,)),
            dma((n,)),
            dma((2,)),
            dma((n,)),
            dma((n,)),
            dma((n,)),
            dma((2,)),
            dma((n,)),
            dma((n,)),
            dma((n,)),
            dma,
            dma,
        ],
        compiler_params=pltpu.CompilerParams(
            collective_id=0, has_side_effects=True, vmem_limit_bytes=32 * 1024 * 1024
        ),
    )(flat)
    return out.reshape(matrix.shape)


def solution(mesh):
    specs = P(None, "row", None, None, "col", None)
    return jax.shard_map(
        per_device, mesh=mesh, in_specs=(specs,), out_specs=specs, check_vma=False
    )
```

```python
import functools

import jax
import jax.numpy as jnp
from jax import lax
from jax.experimental import pallas as pl
from jax.experimental.pallas import tpu as pltpu
from jax.sharding import PartitionSpec as P

F32 = jnp.float32
MESH = pl.DeviceIdType.MESH
HIGHEST = lax.Precision.HIGHEST
NB = 128
LOOK = 2


def dot_nn(a, b):
    return jnp.dot(a, b, precision=HIGHEST, preferred_element_type=F32)


def dot_nt(a, b):
    return lax.dot_general(
        a, b, (((1,), (1,)), ((), ())), precision=HIGHEST, preferred_element_type=F32
    )


def row_splat(tile, k):
    return jnp.broadcast_to(tile[k : k + 1, :], (8, NB))


def lane_splat(tile, k):
    return jnp.broadcast_to(tile[:, k : k + 1], (8, NB))


def eliminate(rows, rows_identity, columns):
    sub = lax.broadcasted_iota(jnp.int32, (8, NB), 0)
    columns = list(columns)
    upper, inverse, solved = rows, rows_identity, rows_identity
    scale = jnp.ones((8, NB), F32)
    for k in range(8):
        pivot = row_splat(columns[k], k)
        over = 1.0 / pivot
        here = sub == k
        ratio = columns[k] * over
        below = jnp.where(sub > k, ratio, 0.0)
        for j in range(k + 1, 8):
            r = row_splat(columns[j], k)
            columns[j] = jnp.where(here, r * over, columns[j] - ratio * r)
        upper = upper - below * row_splat(upper, k)
        inverse = inverse - below * row_splat(inverse, k)
        r = row_splat(solved, k)
        solved = jnp.where(here, r * over, solved - ratio * r)
        scale = jnp.where(here, lax.rsqrt(pivot), scale)
    return upper * scale, inverse * scale, solved


def factor(work, solved_rows, upper, inverse, between):
    lane = lax.broadcasted_iota(jnp.int32, (8, NB), 1)
    sub = lax.broadcasted_iota(jnp.int32, (8, NB), 0)
    solved_rows[...] = jnp.zeros((NB, NB), F32)
    steps = NB // 8
    for t in range(steps):
        if t in between:
            between[t]()
        o = 8 * t
        rows = work[o : o + 8, :]
        columns = [lane_splat(rows, o + j) for j in range(8)]
        block = (lane >= o) & (lane < o + 8)
        rows_identity = jnp.where(block, (lane - o == sub).astype(F32), rows)
        up, inv, solved = eliminate(rows, rows_identity, columns)
        upper[o : o + 8, :] = jnp.where(lane >= o, up, 0.0)
        inverse[o : o + 8, :] = jnp.where(lane < o + 8, inv, 0.0)
        solved_rows[o : o + 8, :] = solved
        splats = [row_splat(solved, j) for j in range(8)]
        for i in range(t + 1, min(t + 1 + LOOK, steps)):
            tile = work[8 * i : 8 * i + 8, :]
            total = jnp.where(block, 0.0, tile)
            for j in range(8):
                total = total - lane_splat(tile, o + j) * splats[j]
            work[8 * i : 8 * i + 8, :] = total
        rest = 8 * (t + 1 + LOOK)
        if rest < NB:
            tiles = work[rest:, :]
            lanes = lax.broadcasted_iota(jnp.int32, (NB - rest, NB), 1)
            own = (lanes >= o) & (lanes < o + 8)
            work[rest:, :] = jnp.where(own, 0.0, tiles) - dot_nn(
                jnp.where(own, tiles, 0.0), solved_rows[...]
            )


def kernel(
    n,
    x_hbm,
    out_hbm,
    xv,
    panel,
    lead,
    rbuf,
    cbuf,
    work,
    solved_rows,
    u0,
    w0,
    u1,
    w1,
    w10,
    ac,
    pr,
    pc,
    outv,
    load_sem,
    store_sem,
    s_root,
    s_recv,
    s_send,
    go_plane,
    go_line,
    r_piece,
    r_gather,
    r_send_a,
    r_send_b,
    c_piece,
    c_gather,
    c_send_a,
    c_send_b,
    c_pair,
    c_pair_send,
):
    r = lax.axis_index("row")
    c = lax.axis_index("col")

    def each(body, count=n - 1):
        def step(k, carry):
            body(k)
            return carry

        lax.fori_loop(1, count + 1, step, 0)

    def other(me, k):
        return lax.rem(me + k, n)

    def copy(src, dst, send, recv, row, col):
        return pltpu.make_async_remote_copy(
            src_ref=src,
            dst_ref=dst,
            send_sem=send,
            recv_sem=recv,
            device_id=(row, col),
            device_id_type=MESH,
        )

    def signal(sem, row, col):
        pl.semaphore_signal(sem, inc=1, device_id=(row, col), device_id_type=MESH)

    x = c // 4
    y = lax.rem(c, 4)
    odd = lax.rem(r, 2) == 1
    first_row, second_row, deep = r == 0, r == 1, r >= 2
    left = c < 2
    both = jnp.logical_and

    barrier = pltpu.get_barrier_semaphore()
    hub = jnp.where(deep, r, 1)
    line = jnp.where(left, 3, 1)

    @pl.when(both(first_row, jnp.logical_and(y == 0, x > 0)))
    def _():
        signal(barrier, 0, 0)

    @pl.when(both(first_row, y > 0))
    def _():
        signal(barrier, 0, 4 * x)

    @pl.when(both(first_row, c == 0))
    def _():
        signal(barrier, 0, 1)

    @pl.when(second_row)
    def _():
        signal(barrier, 0, c)

    for k in range(2):

        @pl.when(jnp.logical_not(both(r == hub, c == k)))
        def _():
            signal(barrier, hub, k)

    @pl.when(jnp.logical_or(both(left, r != 3), both(jnp.logical_not(left), r != 1)))
    def _():
        signal(barrier, line, c)

    load = pltpu.make_async_copy(x_hbm, xv, load_sem)
    load.start()
    load.wait()

    @pl.when(left)
    def _():
        panel[...] = xv[pl.ds(0, 512, stride=4), :]

    heard = jnp.where(
        first_row,
        jnp.where(c == 0, 7, jnp.where(c == 1, 2, jnp.where(y == 0, 4, 1))),
        jnp.where(
            second_row,
            jnp.where(left, 2 * n - 1, n - 1),
            jnp.where(left, jnp.where(r == 3, 2 * (n - 1), n - 1), 0),
        ),
    )

    @pl.when(heard > 0)
    def _():
        pl.semaphore_wait(barrier, heard)

    def r_scatter(k):
        p = other(c, k)
        return copy(
            panel.at[pl.ds(pl.multiple_of(p * 32, 32), 32)],
            rbuf.at[p, c],
            r_send_a.at[p],
            r_piece.at[c],
            r,
            p,
        )

    def c_scatter(k):
        p = other(r, k)
        return copy(
            xv.at[pl.ds(pl.multiple_of(p * 32, 32), 32)],
            cbuf.at[lax.rem(p, 2), p // 2, r],
            c_send_a.at[p],
            c_piece.at[r],
            p,
            c,
        )

    def r_across(k):
        p = other(c, k)
        return copy(rbuf.at[c], rbuf.at[c], r_send_b.at[p], r_gather.at[c], r, p)

    parity = lax.rem(r, 2)
    pair = r + 1 - 2 * parity
    half = r // 2

    def c_down(k):
        p = lax.rem(r + 2 * k, n)
        return copy(
            cbuf.at[parity, half], cbuf.at[parity, half], c_send_b.at[p], c_gather.at[r], p, c
        )

    def c_across():
        return copy(cbuf.at[parity], cbuf.at[parity], c_pair_send, c_pair, pair, c)

    def start(make):
        return lambda k: make(k).start()

    def sent(make):
        return lambda k: make(k).wait_send()

    def arrive(buffer, sem):
        pltpu.make_async_copy(buffer, buffer, sem).wait()

    def to_root(b):
        return copy(panel.at[pl.ds(0, NB)], lead.at[b], s_root, s_recv.at[b], 0, 0)

    def pass_on(b, act):
        def one(slot, row, col):
            act(copy(lead.at[b], lead.at[b], s_send.at[b, slot], s_recv.at[b], row, col))

        @pl.when(both(first_row, c == 0))
        def _():
            for k in range(1, 4):
                one(3 + k, 0, 4 * k)

        @pl.when(both(first_row, y == 0))
        def _():
            for k in range(1, 4):
                one(k, 0, c + k)

        @pl.when(first_row)
        def _():
            one(0, 1, c)

        @pl.when(second_row)
        def _():
            for k in range(7):
                one(k, 2 * k + 3, c)

        @pl.when(both(odd, deep))
        def _():
            one(0, r - 1, c)

    def forward(b):
        arrive(lead.at[b], s_recv.at[b])
        pass_on(b, lambda d: d.start())

    corner = both(first_row, c == 0)
    last = both(second_row, c == 1)

    @pl.when(both(first_row, c == 1))
    def _():
        to_root(1).start()

    @pl.when(last)
    def _():
        to_root(2).start()

    @pl.when(both(second_row, left))
    def _():
        signal(go_plane, 0, c)

    @pl.when(both(r == 3, left))
    def _():
        signal(go_line, 0, c)
        signal(go_line, 1, c)

    @pl.when(both(second_row, jnp.logical_not(left)))
    def _():
        signal(go_line, 0, c)

    def plane_scatter():
        each(start(r_scatter))
        rbuf[c, c] = panel[pl.ds(pl.multiple_of(c * 32, 32), 32), :]

    def line_scatter():
        each(start(c_scatter))
        cbuf[parity, half, r] = xv[pl.ds(pl.multiple_of(r * 32, 32), 32), :]

    @pl.when(both(r > 0, left))
    def _():
        plane_scatter()

    @pl.when(first_row)
    def _():
        @pl.when(c == 0)
        def _():
            lead[0] = panel[0:NB, :]
            pass_on(0, lambda d: d.start())

        @pl.when(c > 0)
        def _():
            forward(0)

        forward(1)

        @pl.when(left)
        def _():
            pl.semaphore_wait(go_plane, 1)
            plane_scatter()

        pl.semaphore_wait(go_line, 1)
        line_scatter()

    @pl.when(second_row)
    def _():
        @pl.when(left)
        def _():
            pl.semaphore_wait(go_line, 1)

        line_scatter()
        forward(0)
        forward(1)

    @pl.when(c != 0)
    def _():
        arrive(rbuf.at[c, 0], r_piece.at[0])

    @pl.when(c != 1)
    def _():
        arrive(rbuf.at[c, 1], r_piece.at[1])

    each(start(r_across))

    @pl.when(r != 0)
    def _():
        arrive(cbuf.at[parity, half, 0], c_piece.at[0])

    @pl.when(r != 1)
    def _():
        arrive(cbuf.at[parity, half, 1], c_piece.at[1])

    each(start(c_down), n // 2 - 1)

    @pl.when(deep)
    def _():
        forward(0)

    def midway():
        @pl.when(deep)
        def _():
            forward(1)

        @pl.when(jnp.logical_not(deep))
        def _():
            forward(2)

    work[...] = lead[0]
    factor(work, solved_rows, u0, w0, {8: midway})

    @pl.when(deep)
    def _():
        forward(2)

    u01 = dot_nn(w0[...], lead[1])
    l10 = u01.T
    work[...] = lead[2] - dot_nn(l10, u01)
    w10[...] = dot_nn(l10, w0[...])

    def c_wait(k):
        p = lax.rem(r + 2 * k, n)
        arrive(cbuf.at[parity, p // 2], c_gather.at[p])

    def pair_up():
        each(c_wait, n // 2 - 1)
        c_across().start()

    factor(work, solved_rows, u1, w1, {8: pair_up})
    w10[...] = -dot_nn(w1[...], w10[...])

    def r_wait(k):
        p = other(c, k)
        arrive(rbuf.at[p], r_gather.at[p])

    each(r_wait)
    r0 = rbuf[:, 0].reshape(4 * NB, NB)
    r1 = rbuf[:, 1].reshape(4 * NB, NB)
    pr[:, 0:NB] = dot_nt(r0, w0[...])
    pr[:, NB:] = dot_nt(r0, w10[...]) + dot_nt(r1, w1[...])

    c_across().wait()
    for p in range(n):
        for h in range(2):
            for b in range(4):
                ac[h * NB + 8 * p : h * NB + 8 * p + 8, b * NB : (b + 1) * NB] = cbuf[
                    p % 2, p // 2, h, pl.ds(b, 8, stride=4), :
                ]
    pc[0:NB, :] = dot_nn(w0[...], ac[0:NB, :])
    pc[NB:, :] = dot_nn(w10[...], ac[0:NB, :]) + dot_nn(w1[...], ac[NB:, :])

    for a in range(4):
        update = dot_nn(pr[a * NB : (a + 1) * NB, :], pc[...])
        for b in range(4):
            at = pl.ds(a * 512 + b, NB, stride=4)
            outv[at, :] = xv[at, :] - update[:, b * NB : (b + 1) * NB]

    @pl.when(c == 0)
    def _():
        for a in range(4):
            outv[pl.ds(a * 512, NB, stride=4), :] = pr[a * NB : (a + 1) * NB, 0:NB]

    @pl.when(c == 1)
    def _():
        for a in range(4):
            outv[pl.ds(a * 512, NB, stride=4), :] = pr[a * NB : (a + 1) * NB, NB:]

    @pl.when(r < 2)
    def _():
        keep = jnp.logical_and(r == 1, c == 0)
        first = outv[pl.ds(0, NB, stride=4), :]
        outv[0:512, :] = jnp.zeros((512, NB), F32)
        outv[pl.ds(0, NB, stride=4), :] = jnp.where(keep, first, 0.0)

        @pl.when(corner)
        def _():
            outv[pl.ds(0, NB, stride=4), :] = u0[...].T

        @pl.when(jnp.logical_and(r == 1, c == 1))
        def _():
            outv[pl.ds(0, NB, stride=4), :] = u1[...].T

    store = pltpu.make_async_copy(outv, out_hbm, store_sem)
    store.start()

    @pl.when(both(first_row, c == 1))
    def _():
        to_root(1).wait_send()

    @pl.when(last)
    def _():
        to_root(2).wait_send()

    for b in range(3):
        pass_on(b, lambda d: d.wait_send())

    @pl.when(left)
    def _():
        each(sent(r_scatter))

    @pl.when(r < 2)
    def _():
        each(sent(c_scatter))

    each(sent(r_across))
    each(sent(c_down), n // 2 - 1)
    store.wait()


def per_device(matrix):
    n = lax.axis_size("row")
    flat = matrix.reshape(2048, NB)
    dma = pltpu.SemaphoreType.DMA
    square = pltpu.VMEM((NB, NB), F32)
    out = pl.pallas_call(
        functools.partial(kernel, n),
        out_shape=jax.ShapeDtypeStruct((2048, NB), F32),
        in_specs=[pl.BlockSpec(memory_space=pl.ANY)],
        out_specs=pl.BlockSpec(memory_space=pl.ANY),
        scratch_shapes=[
            pltpu.VMEM((2048, NB), F32),
            pltpu.VMEM((512, NB), F32),
            pltpu.VMEM((3, NB, NB), F32),
            pltpu.VMEM((n, 2, 32, NB), F32),
            pltpu.VMEM((2, n // 2, 2, 32, NB), F32),
            square,
            square,
            square,
            square,
            square,
            square,
            square,
            pltpu.VMEM((2 * NB, 4 * NB), F32),
            pltpu.VMEM((4 * NB, 2 * NB), F32),
            pltpu.VMEM((2 * NB, 4 * NB), F32),
            pltpu.VMEM((2048, NB), F32),
            dma,
            dma,
            dma,
            dma((3,)),
            dma((3, 7)),
            pltpu.SemaphoreType.REGULAR,
            pltpu.SemaphoreType.REGULAR,
            dma((2,)),
            dma((n,)),
            dma((n,)),
            dma((n,)),
            dma((2,)),
            dma((n,)),
            dma((n,)),
            dma((n,)),
            dma,
            dma,
        ],
        compiler_params=pltpu.CompilerParams(
            collective_id=0, has_side_effects=True, vmem_limit_bytes=56 * 1024 * 1024
        ),
    )(flat)
    return out.reshape(matrix.shape)


def solution(mesh):
    specs = P(None, "row", None, None, "col", None)
    return jax.shard_map(
        per_device, mesh=mesh, in_specs=(specs,), out_specs=specs, check_vma=False
    )
```

```python
import functools

import jax
import jax.numpy as jnp
from jax import lax
from jax.experimental import pallas as pl
from jax.experimental.pallas import tpu as pltpu
from jax.sharding import PartitionSpec as P

F32 = jnp.float32
MESH = pl.DeviceIdType.MESH
HIGHEST = lax.Precision.HIGHEST
NB = 128
LOOK = 2
CHUNK = 64
CHUNKS = 512 // CHUNK


def dot_nn(a, b):
    return jnp.dot(a, b, precision=HIGHEST, preferred_element_type=F32)


def dot_nt(a, b):
    return lax.dot_general(
        a, b, (((1,), (1,)), ((), ())), precision=HIGHEST, preferred_element_type=F32
    )


def row_splat(tile, k):
    return jnp.broadcast_to(tile[k : k + 1, :], (8, NB))


def lane_splat(tile, k):
    return jnp.broadcast_to(tile[:, k : k + 1], (8, NB))


def eliminate(rows, rows_identity, columns):
    sub = lax.broadcasted_iota(jnp.int32, (8, NB), 0)
    columns = list(columns)
    upper, inverse, solved = rows, rows_identity, rows_identity
    scale = jnp.ones((8, NB), F32)
    for k in range(8):
        pivot = row_splat(columns[k], k)
        over = 1.0 / pivot
        here = sub == k
        ratio = columns[k] * over
        below = jnp.where(sub > k, ratio, 0.0)
        for j in range(k + 1, 8):
            r = row_splat(columns[j], k)
            columns[j] = jnp.where(here, r * over, columns[j] - ratio * r)
        upper = upper - below * row_splat(upper, k)
        inverse = inverse - below * row_splat(inverse, k)
        r = row_splat(solved, k)
        solved = jnp.where(here, r * over, solved - ratio * r)
        scale = jnp.where(here, lax.rsqrt(pivot), scale)
    return upper * scale, inverse * scale, solved


def factor(work, solved_rows, upper, inverse, between):
    lane = lax.broadcasted_iota(jnp.int32, (8, NB), 1)
    sub = lax.broadcasted_iota(jnp.int32, (8, NB), 0)
    solved_rows[...] = jnp.zeros((NB, NB), F32)
    steps = NB // 8
    for t in range(steps):
        if t in between:
            between[t]()
        o = 8 * t
        rows = work[o : o + 8, :]
        columns = [lane_splat(rows, o + j) for j in range(8)]
        block = (lane >= o) & (lane < o + 8)
        rows_identity = jnp.where(block, (lane - o == sub).astype(F32), rows)
        up, inv, solved = eliminate(rows, rows_identity, columns)
        upper[o : o + 8, :] = jnp.where(lane >= o, up, 0.0)
        inverse[o : o + 8, :] = jnp.where(lane < o + 8, inv, 0.0)
        solved_rows[o : o + 8, :] = solved
        splats = [row_splat(solved, j) for j in range(8)]
        for i in range(t + 1, min(t + 1 + LOOK, steps)):
            tile = work[8 * i : 8 * i + 8, :]
            total = jnp.where(block, 0.0, tile)
            for j in range(8):
                total = total - lane_splat(tile, o + j) * splats[j]
            work[8 * i : 8 * i + 8, :] = total
        rest = 8 * (t + 1 + LOOK)
        if rest < NB:
            tiles = work[rest:, :]
            lanes = lax.broadcasted_iota(jnp.int32, (NB - rest, NB), 1)
            own = (lanes >= o) & (lanes < o + 8)
            work[rest:, :] = jnp.where(own, 0.0, tiles) - dot_nn(
                jnp.where(own, tiles, 0.0), solved_rows[...]
            )


def gather_kernel(
    n,
    x_hbm,
    pr,
    pc,
    diag,
    xv,
    panel,
    lead,
    rbuf,
    cbuf,
    wbuf,
    wown,
    ac,
    work,
    solved_rows,
    u0,
    u1,
    w0,
    w1,
    w10,
    load_sem,
    lead_recv,
    lead_send,
    diag_recv,
    diag_send,
    go_plane,
    go_line,
    r_piece,
    r_gather,
    r_send_a,
    r_send_b,
    c_recv,
    c_send,
    c_pair,
    c_pair_send,
    w_piece,
    w_gather,
    w_send_a,
    w_send_b,
    w_send_c,
):
    r = lax.axis_index("row")
    c = lax.axis_index("col")
    z = r // 2
    core = lax.rem(r, 2)
    pair = r + 1 - 2 * core
    both, either, no = jnp.logical_and, jnp.logical_or, jnp.logical_not
    left = c < 2
    corner = both(r == 0, c == 0)
    last = both(r == 1, c == 1)
    hub = both(r == 1, c == 0)

    def span(first, end, body):
        def step(k, carry):
            body(k)
            return carry

        lax.fori_loop(first, end, step, 0)

    def each(body):
        span(1, n, body)

    def other(me, k):
        return lax.rem(me + k, n)

    def copy(src, dst, send, recv, row, col):
        return pltpu.make_async_remote_copy(
            src_ref=src,
            dst_ref=dst,
            send_sem=send,
            recv_sem=recv,
            device_id=(row, col),
            device_id_type=MESH,
        )

    def signal(sem, row, col):
        pl.semaphore_signal(sem, inc=1, device_id=(row, col), device_id_type=MESH)

    def arrive(buffer, sem):
        pltpu.make_async_copy(buffer, buffer, sem).wait()

    barrier = pltpu.get_barrier_semaphore()
    before = jnp.where(z < 5, r - 2, jnp.where(z < 7, r + 2, r - 14))
    signal(barrier, pair, c)

    @pl.when(z > 0)
    def _():
        signal(barrier, before, c)

    @pl.when(z != 4)
    def _():
        signal(barrier, 8, c)

    for k in range(2):

        @pl.when(both(z > 0, c != k))
        def _():
            signal(barrier, r, k)

    @pl.when(both(z == 0, c != 0))
    def _():
        signal(barrier, 1, 0)

    @pl.when(corner)
    def _():
        signal(barrier, 1, 1)

    load = pltpu.make_async_copy(x_hbm, xv, load_sem)
    load.start()
    load.wait()

    @pl.when(left)
    def _():
        panel[...] = xv[pl.ds(0, 512, stride=4), :]

    def enter():
        after = jnp.where(z == 0, 2, jnp.where(either(z == 4, z == 5), 0, 1))
        heard = (
            1
            + after
            + jnp.where(r == 8, n - 2, 0)
            + jnp.where(both(z > 0, left), n - 1, 0)
            + jnp.where(hub, 2 * (n - 1), 0)
            + jnp.where(last, 1, 0)
        )
        pl.semaphore_wait(barrier, heard)

    def to_corner(b):
        return copy(panel.at[pl.ds(0, NB)], lead.at[b], lead_send, lead_recv.at[b], 0, 0)

    def r_scatter(k):
        p = other(c, k)
        return copy(
            panel.at[pl.ds(pl.multiple_of(p * 32, 32), 32)],
            rbuf.at[p, c],
            r_send_a.at[p],
            r_piece.at[c],
            r,
            p,
        )

    def r_across(k):
        p = other(c, k)
        return copy(rbuf.at[c], rbuf.at[c], r_send_b.at[p], r_gather.at[c], r, p)

    def plane_scatter():
        each(lambda k: r_scatter(k).start())
        rbuf[c, c] = panel[pl.ds(pl.multiple_of(c * 32, 32), 32), :]

    def plane_gather():
        @pl.when(c != 0)
        def _():
            arrive(rbuf.at[c, 0], r_piece.at[0])

        @pl.when(c != 1)
        def _():
            arrive(rbuf.at[c, 1], r_piece.at[1])

        each(lambda k: r_across(k).start())

    def chunk(k):
        return cbuf.at[core, pl.ds(pl.multiple_of(k * CHUNK, CHUNK), CHUNK)]

    def first_chunk(k):
        return xv.at[pl.ds(pl.multiple_of(k * CHUNK, CHUNK), CHUNK)]

    def c_next(k, way, src):
        there = lax.rem(r + 2 + way * (n - 4), n)
        return copy(src, chunk(k), c_send.at[way, k], c_recv.at[k], there, c)

    def c_beside(k, src):
        return copy(src, chunk(k), c_pair_send.at[k], c_pair.at[k], pair, c)

    def line_start(k):
        c_next(k, 0, first_chunk(k)).start()
        c_next(k, 1, first_chunk(k)).start()
        c_beside(k, first_chunk(k)).start()

    up = both(z >= 1, z <= 3)
    down = z >= 6

    def line_relay(k):
        arrive(chunk(k), c_recv.at[k])

        @pl.when(up)
        def _():
            c_next(k, 0, chunk(k)).start()

        @pl.when(down)
        def _():
            c_next(k, 1, chunk(k)).start()

        c_beside(k, chunk(k)).start()

    def w_copy(send, recv, row, col):
        return copy(wbuf.at[c], wbuf.at[c], send, recv, row, col)

    def w_scatter(k):
        p = other(c, k)
        return copy(wown.at[p], wbuf.at[p], w_send_a.at[p], w_piece, r, p)

    def w_down(k):
        p = other(r, k)
        return w_copy(w_send_b.at[p], w_piece, p, c)

    def w_across(k):
        p = other(c, k)
        return w_copy(w_send_c.at[p], w_gather.at[c], r, p)

    def diagonal():
        return copy(u1, diag, diag_send, diag_recv, 1, 1)

    def pass_w():
        @pl.when(r == 0)
        def _():
            pl.semaphore_wait(go_line, 1)
            each(lambda k: w_down(k).start())

        each(lambda k: w_across(k).start())

    @pl.when(corner)
    def _():
        work[...] = panel[0:NB, :]
        factor(work, solved_rows, u0, w0, {})
        enter()
        span(0, CHUNKS, line_start)
        pl.semaphore_wait(go_plane, 1)
        plane_scatter()
        arrive(lead.at[0], lead_recv.at[0])
        l10 = dot_nt(lead[0], w0[...])
        w10[...] = dot_nn(l10, w0[...])
        arrive(lead.at[1], lead_recv.at[1])
        work[...] = lead[1] - dot_nt(l10, l10)
        factor(work, solved_rows, u1, w1, {})
        wown[:, 0] = w0[...].reshape(n, 8, NB)
        wown[:, 1] = -dot_nn(w1[...], w10[...]).reshape(n, 8, NB)
        wown[:, 2] = w1[...].reshape(n, 8, NB)
        wbuf[0] = wown[0]
        each(lambda k: w_scatter(k).start())
        pass_w()
        diagonal().start()
        plane_gather()
        diag[...] = u0[...]

    @pl.when(no(corner))
    def _():
        enter()

        @pl.when(hub)
        def _():
            to_corner(0).start()
            signal(go_plane, 0, 0)
            signal(go_plane, 0, 1)
            signal(go_plane, 1, 1)

        @pl.when(last)
        def _():
            to_corner(1).start()

        @pl.when(r == 8)
        def _():
            signal(go_line, 0, c)

        @pl.when(z == 0)
        def _():
            span(0, CHUNKS, line_start)

        @pl.when(left)
        def _():
            @pl.when(both(z == 0, no(hub)))
            def _():
                pl.semaphore_wait(go_plane, 1)

            plane_scatter()

        early = jnp.where(z == 1, CHUNKS // 2, jnp.where(z == 2, 1, 0))
        mid = jnp.where(z == 4, CHUNKS // 2, jnp.where(z == 5, 5, CHUNKS))

        @pl.when(z > 0)
        def _():
            span(0, early, line_relay)

        plane_gather()

        @pl.when(z > 0)
        def _():
            span(early, mid, line_relay)

        arrive(wbuf.at[c], w_piece)
        pass_w()

        @pl.when(z > 0)
        def _():
            span(mid, CHUNKS, line_relay)

    @pl.when(z == 0)
    def _():
        cbuf[core] = xv[0:512, :]

    def w_wait(k):
        p = other(c, k)
        arrive(wbuf.at[p], w_gather.at[p])

    def r_wait(k):
        p = other(c, k)
        arrive(rbuf.at[p], r_gather.at[p])

    def c_wait(k):
        arrive(cbuf.at[1 - core, pl.ds(pl.multiple_of(k * CHUNK, CHUNK), CHUNK)], c_pair.at[k])

    span(0, CHUNKS, c_wait)
    for h in range(2):
        for b in range(4):
            ac[h * NB : (h + 1) * NB, b * NB : (b + 1) * NB] = cbuf[h, pl.ds(b, NB, stride=4), :]
    each(r_wait)
    each(w_wait)
    w00 = wbuf[:, 0].reshape(NB, NB)
    w01 = wbuf[:, 1].reshape(NB, NB)
    w11 = wbuf[:, 2].reshape(NB, NB)
    r0 = rbuf[:, 0].reshape(4 * NB, NB)
    r1 = rbuf[:, 1].reshape(4 * NB, NB)
    pr[:, 0:NB] = dot_nt(r0, w00)
    pr[:, NB:] = dot_nt(r0, w01) + dot_nt(r1, w11)
    pc[0:NB, :] = dot_nn(w00, ac[0:NB, :])
    pc[NB:, :] = dot_nn(w01, ac[0:NB, :]) + dot_nn(w11, ac[NB:, :])

    @pl.when(last)
    def _():
        arrive(diag, diag_recv)

    @pl.when(corner)
    def _():
        each(lambda k: w_scatter(k).wait_send())
        diagonal().wait_send()

    @pl.when(hub)
    def _():
        to_corner(0).wait_send()

    @pl.when(last)
    def _():
        to_corner(1).wait_send()

    @pl.when(left)
    def _():
        each(lambda k: r_scatter(k).wait_send())

    @pl.when(r == 0)
    def _():
        each(lambda k: w_down(k).wait_send())

    @pl.when(either(z == 0, up))
    def _():
        span(0, CHUNKS, lambda k: c_next(k, 0, chunk(k)).wait_send())

    @pl.when(either(z == 0, down))
    def _():
        span(0, CHUNKS, lambda k: c_next(k, 1, chunk(k)).wait_send())

    span(0, CHUNKS, lambda k: c_beside(k, chunk(k)).wait_send())
    each(lambda k: r_across(k).wait_send())
    each(lambda k: w_across(k).wait_send())


def update_kernel(x, pr, pc, diag, out):
    a = pl.program_id(0)
    r = lax.axis_index("row")
    c = lax.axis_index("col")
    both = jnp.logical_and
    top = both(a == 0, r < 2)

    def put(b, value):
        out[pl.ds(b, NB, stride=4), :] = value

    @pl.when(top)
    def _():
        out[...] = jnp.zeros((512, NB), F32)

        @pl.when(both(r == 1, c == 0))
        def _():
            put(0, pr[:, 0:NB])

        @pl.when(both(r == c, c < 2))
        def _():
            put(0, diag[...].T)

    @pl.when(jnp.logical_not(top))
    def _():
        update = dot_nn(pr[...], pc[...])
        for b in range(4):
            put(b, x[pl.ds(b, NB, stride=4), :] - update[:, b * NB : (b + 1) * NB])

        @pl.when(c == 0)
        def _():
            put(0, pr[:, 0:NB])

        @pl.when(c == 1)
        def _():
            put(0, pr[:, NB:])


def per_device(matrix):
    n = lax.axis_size("row")
    flat = matrix.reshape(2048, NB)
    dma = pltpu.SemaphoreType.DMA
    square = pltpu.VMEM((NB, NB), F32)
    whole = pl.BlockSpec(memory_space=pltpu.VMEM)
    pr, pc, diag = pl.pallas_call(
        functools.partial(gather_kernel, n),
        out_shape=[
            jax.ShapeDtypeStruct((4 * NB, 2 * NB), F32),
            jax.ShapeDtypeStruct((2 * NB, 4 * NB), F32),
            jax.ShapeDtypeStruct((NB, NB), F32),
        ],
        in_specs=[pl.BlockSpec(memory_space=pl.ANY)],
        out_specs=[whole] * 3,
        scratch_shapes=[
            pltpu.VMEM((2048, NB), F32),
            pltpu.VMEM((512, NB), F32),
            pltpu.VMEM((2, NB, NB), F32),
            pltpu.VMEM((n, 2, 32, NB), F32),
            pltpu.VMEM((2, 512, NB), F32),
            pltpu.VMEM((n, 3, 8, NB), F32),
            pltpu.VMEM((n, 3, 8, NB), F32),
            pltpu.VMEM((2 * NB, 4 * NB), F32),
            square,
            square,
            square,
            square,
            square,
            square,
            square,
            dma,
            dma((2,)),
            dma,
            dma,
            dma,
            pltpu.SemaphoreType.REGULAR,
            pltpu.SemaphoreType.REGULAR,
            dma((2,)),
            dma((n,)),
            dma((n,)),
            dma((n,)),
            dma((CHUNKS,)),
            dma((2, CHUNKS)),
            dma((CHUNKS,)),
            dma((CHUNKS,)),
            dma,
            dma((n,)),
            dma((n,)),
            dma((n,)),
            dma((n,)),
        ],
        compiler_params=pltpu.CompilerParams(
            collective_id=0, has_side_effects=True, vmem_limit_bytes=56 * 1024 * 1024
        ),
    )(flat)
    out = pl.pallas_call(
        update_kernel,
        out_shape=jax.ShapeDtypeStruct((2048, NB), F32),
        grid=(4,),
        in_specs=[
            pl.BlockSpec((512, NB), lambda a: (a, 0)),
            pl.BlockSpec((NB, 2 * NB), lambda a: (a, 0)),
            pl.BlockSpec((2 * NB, 4 * NB), lambda a: (0, 0)),
            pl.BlockSpec((NB, NB), lambda a: (0, 0)),
        ],
        out_specs=pl.BlockSpec((512, NB), lambda a: (a, 0)),
    )(flat, pr, pc, diag)
    return out.reshape(matrix.shape)


def solution(mesh):
    specs = P(None, "row", None, None, "col", None)
    return jax.shard_map(
        per_device, mesh=mesh, in_specs=(specs,), out_specs=specs, check_vma=False
    )
```

```python
import functools

import jax
import jax.numpy as jnp
from jax import lax
from jax.experimental import pallas as pl
from jax.experimental.pallas import tpu as pltpu
from jax.sharding import PartitionSpec as P

F32 = jnp.float32
MESH = pl.DeviceIdType.MESH
HIGHEST = lax.Precision.HIGHEST
NB = 128
LOOK = 2
CHUNK = 64
CHUNKS = 512 // CHUNK


def dot_nn(a, b):
    return jnp.dot(a, b, precision=HIGHEST, preferred_element_type=F32)


def dot_nt(a, b):
    return lax.dot_general(
        a, b, (((1,), (1,)), ((), ())), precision=HIGHEST, preferred_element_type=F32
    )


def row_splat(tile, k):
    return jnp.broadcast_to(tile[k : k + 1, :], (8, NB))


def lane_splat(tile, k):
    return jnp.broadcast_to(tile[:, k : k + 1], (8, NB))


def eliminate(rows, rows_identity, columns):
    sub = lax.broadcasted_iota(jnp.int32, (8, NB), 0)
    columns = list(columns)
    upper, inverse, solved = rows, rows_identity, rows_identity
    scale = jnp.ones((8, NB), F32)
    for k in range(8):
        pivot = row_splat(columns[k], k)
        over = 1.0 / pivot
        here = sub == k
        ratio = columns[k] * over
        below = jnp.where(sub > k, ratio, 0.0)
        for j in range(k + 1, 8):
            r = row_splat(columns[j], k)
            columns[j] = jnp.where(here, r * over, columns[j] - ratio * r)
        upper = upper - below * row_splat(upper, k)
        inverse = inverse - below * row_splat(inverse, k)
        r = row_splat(solved, k)
        solved = jnp.where(here, r * over, solved - ratio * r)
        scale = jnp.where(here, lax.rsqrt(pivot), scale)
    return upper * scale, inverse * scale, solved


def factor(work, solved_rows, upper, inverse, between):
    lane = lax.broadcasted_iota(jnp.int32, (8, NB), 1)
    sub = lax.broadcasted_iota(jnp.int32, (8, NB), 0)
    solved_rows[...] = jnp.zeros((NB, NB), F32)
    steps = NB // 8
    for t in range(steps):
        if t in between:
            between[t]()
        o = 8 * t
        rows = work[o : o + 8, :]
        columns = [lane_splat(rows, o + j) for j in range(8)]
        block = (lane >= o) & (lane < o + 8)
        rows_identity = jnp.where(block, (lane - o == sub).astype(F32), rows)
        up, inv, solved = eliminate(rows, rows_identity, columns)
        upper[o : o + 8, :] = jnp.where(lane >= o, up, 0.0)
        inverse[o : o + 8, :] = jnp.where(lane < o + 8, inv, 0.0)
        solved_rows[o : o + 8, :] = solved
        splats = [row_splat(solved, j) for j in range(8)]
        for i in range(t + 1, min(t + 1 + LOOK, steps)):
            tile = work[8 * i : 8 * i + 8, :]
            total = jnp.where(block, 0.0, tile)
            for j in range(8):
                total = total - lane_splat(tile, o + j) * splats[j]
            work[8 * i : 8 * i + 8, :] = total
        rest = 8 * (t + 1 + LOOK)
        if rest < NB:
            tiles = work[rest:, :]
            lanes = lax.broadcasted_iota(jnp.int32, (NB - rest, NB), 1)
            own = (lanes >= o) & (lanes < o + 8)
            work[rest:, :] = jnp.where(own, 0.0, tiles) - dot_nn(
                jnp.where(own, tiles, 0.0), solved_rows[...]
            )


def gather_kernel(
    n,
    x_hbm,
    pr,
    pc,
    diag,
    xv,
    panel,
    lead,
    rbuf,
    cbuf,
    wbuf,
    wown,
    ac,
    work,
    solved_rows,
    u0,
    u1,
    w0,
    w1,
    w10,
    load_sem,
    lead_recv,
    lead_send,
    diag_recv,
    diag_send,
    go_plane,
    go_line,
    r_piece,
    r_gather,
    r_send_a,
    r_send_b,
    c_recv,
    c_send,
    c_pair,
    c_pair_send,
    w_piece,
    w_gather,
    w_send_a,
    w_send_b,
    w_send_c,
):
    r = lax.axis_index("row")
    c = lax.axis_index("col")
    z = r // 2
    core = lax.rem(r, 2)
    pair = r + 1 - 2 * core
    both, either, no = jnp.logical_and, jnp.logical_or, jnp.logical_not
    left = c < 2
    corner = both(r == 0, c == 0)
    last = both(r == 1, c == 1)

    def span(first, end, body):
        def step(k, carry):
            body(k)
            return carry

        lax.fori_loop(first, end, step, 0)

    def each(body):
        span(1, n, body)

    def other(me, k):
        return lax.rem(me + k, n)

    def copy(src, dst, send, recv, row, col):
        return pltpu.make_async_remote_copy(
            src_ref=src,
            dst_ref=dst,
            send_sem=send,
            recv_sem=recv,
            device_id=(row, col),
            device_id_type=MESH,
        )

    def signal(sem, row, col):
        pl.semaphore_signal(sem, inc=1, device_id=(row, col), device_id_type=MESH)

    def arrive(buffer, sem):
        pltpu.make_async_copy(buffer, buffer, sem).wait()

    barrier = pltpu.get_barrier_semaphore()
    before = jnp.where(z < 5, r - 2, jnp.where(z < 7, r + 2, r - 14))
    before = jnp.where(both(r == n - 1, left), 0, before)
    signal(barrier, pair, c)

    @pl.when(z > 0)
    def _():
        signal(barrier, before, c)

    @pl.when(z != 4)
    def _():
        signal(barrier, 8, c)

    for k in range(2):

        @pl.when(c != k)
        def _():
            signal(barrier, jnp.where(z > 0, r, 0), k)

    @pl.when(corner)
    def _():
        signal(barrier, 1, 1)

    top = pltpu.make_async_copy(x_hbm.at[pl.ds(0, 512)], xv.at[pl.ds(0, 512)], load_sem.at[0])
    below = pltpu.make_async_copy(
        x_hbm.at[pl.ds(512, 1536)], xv.at[pl.ds(512, 1536)], load_sem.at[1]
    )
    top.start()
    below.start()
    top.wait()

    @pl.when(left)
    def _():
        panel[0:NB, :] = xv[pl.ds(0, NB, stride=4), :]

    def load_rest():
        below.wait()

        @pl.when(left)
        def _():
            panel[NB:, :] = xv[pl.ds(512, 384, stride=4), :]

    def enter():
        after = jnp.where(z == 0, 2, jnp.where(either(z == 4, z == 5), 0, 1))
        heard = (
            1
            + after
            + jnp.where(r == 8, n - 2, 0)
            + jnp.where(both(z > 0, left), n - 1, 0)
            + jnp.where(both(r == 0, left), 2 * (n - 1) + 1, 0)
            - jnp.where(both(r == 1, left), 1, 0)
            + jnp.where(last, 1, 0)
        )
        pl.semaphore_wait(barrier, heard)

    def to_corner(b):
        return copy(panel.at[pl.ds(0, NB)], lead.at[b], lead_send, lead_recv.at[b], 0, 0)

    def r_scatter(k):
        p = other(c, k)
        return copy(
            panel.at[pl.ds(pl.multiple_of(p * 32, 32), 32)],
            rbuf.at[p, c],
            r_send_a.at[p],
            r_piece.at[c],
            r,
            p,
        )

    def r_across(k):
        p = other(c, k)
        return copy(rbuf.at[c], rbuf.at[c], r_send_b.at[p], r_gather.at[c], r, p)

    def plane_scatter():
        each(lambda k: r_scatter(k).start())
        rbuf[c, c] = panel[pl.ds(pl.multiple_of(c * 32, 32), 32), :]

    def plane_gather():
        @pl.when(c != 0)
        def _():
            arrive(rbuf.at[c, 0], r_piece.at[0])

        @pl.when(c != 1)
        def _():
            arrive(rbuf.at[c, 1], r_piece.at[1])

        each(lambda k: r_across(k).start())

    def chunk(k):
        return cbuf.at[core, pl.ds(pl.multiple_of(k * CHUNK, CHUNK), CHUNK)]

    def first_chunk(k):
        return xv.at[pl.ds(pl.multiple_of(k * CHUNK, CHUNK), CHUNK)]

    def c_next(k, way, src):
        there = lax.rem(r + 2 + way * (n - 4), n)
        return copy(src, chunk(k), c_send.at[way, k], c_recv.at[k], there, c)

    def c_beside(k, src):
        return copy(src, chunk(k), c_pair_send.at[k], c_pair.at[k], pair, c)

    def line_up(k):
        c_next(k, 0, first_chunk(k)).start()
        c_beside(k, first_chunk(k)).start()

    def line_down(k):
        c_next(k, 1, first_chunk(k)).start()

    up = both(z >= 1, z <= 3)
    down = z >= 6

    def line_relay(k):
        arrive(chunk(k), c_recv.at[k])

        @pl.when(up)
        def _():
            c_next(k, 0, chunk(k)).start()

        @pl.when(down)
        def _():
            c_next(k, 1, chunk(k)).start()

        c_beside(k, chunk(k)).start()

    def w_copy(send, recv, row, col):
        return copy(wbuf.at[c], wbuf.at[c], send, recv, row, col)

    def w_scatter(p):
        return copy(wown.at[p], wbuf.at[p], w_send_a.at[p], w_piece, 1, p)

    def w_down(k):
        p = other(r, lax.rem(k + 6, n - 1) + 1)
        return w_copy(w_send_b.at[p], w_piece, p, c)

    def w_across(k):
        p = other(c, k)
        return w_copy(w_send_c.at[p], w_gather.at[c], r, p)

    def diagonal():
        return copy(u1, diag, diag_send, diag_recv, 1, 1)

    def pass_w():
        arrive(wbuf.at[c], w_piece)

        @pl.when(r == 1)
        def _():
            pl.semaphore_wait(go_line, 1)
            each(lambda k: w_down(k).start())

        each(lambda k: w_across(k).start())

    @pl.when(corner)
    def _():
        work[...] = panel[0:NB, :]
        factor(work, solved_rows, u0, w0, {})
        load_rest()
        arrive(lead.at[0], lead_recv.at[0])
        l10 = dot_nt(lead[0], w0[...])
        w10[...] = dot_nn(l10, w0[...])
        arrive(lead.at[1], lead_recv.at[1])
        work[...] = lead[1] - dot_nt(l10, l10)
        enter()
        signal(go_plane, 1, 0)
        sends = [
            copy(
                panel.at[pl.ds(32 * p, 32)], rbuf.at[p, 0], r_send_a.at[p], r_piece.at[0], 0, p
            )
            for p in range(1, n)
        ]
        for k in range(CHUNKS):
            at = pl.ds(k * CHUNK, CHUNK)
            for way, row in ((0, 2), (1, n - 2)):
                sends.append(
                    copy(
                        xv.at[at], cbuf.at[0, at], c_send.at[way, k], c_recv.at[k], row, 0
                    )
                )
            sends.append(copy(xv.at[at], cbuf.at[0, at], c_pair_send.at[k], c_pair.at[k], 1, 0))
        each_step = -(-len(sends) // 14)

        def some(t):
            def issue():
                for d in sends[t * each_step : (t + 1) * each_step]:
                    d.start()

            return issue

        factor(work, solved_rows, u1, w1, {t: some(t) for t in range(14)})
        wown[:, 0] = w0[...].reshape(n, 8, NB)
        wown[:, 1] = -dot_nn(w1[...], w10[...]).reshape(n, 8, NB)
        wown[:, 2] = w1[...].reshape(n, 8, NB)
        span(0, n, lambda p: w_scatter(p).start())
        diagonal().start()
        rbuf[0, 0] = panel[0:32, :]
        plane_gather()
        pass_w()
        diag[...] = u0[...]

    @pl.when(no(corner))
    def _():
        enter()

        @pl.when(both(r == 1, c == 0))
        def _():
            to_corner(0).start()

        @pl.when(last)
        def _():
            to_corner(1).start()

        @pl.when(r == 8)
        def _():
            signal(go_line, 1, c)

        @pl.when(both(r == 0, c == 1))
        def _():
            signal(go_plane, 1, 1)

        @pl.when(z == 0)
        def _():
            span(0, CHUNKS, line_up)

        load_rest()

        @pl.when(both(r == 1, left))
        def _():
            pl.semaphore_wait(go_plane, 1)

        @pl.when(z == 0)
        def _():
            span(0, CHUNKS, line_down)

        @pl.when(left)
        def _():
            plane_scatter()

        early = jnp.where(z == 1, CHUNKS // 2, jnp.where(z == 2, 1, 0))
        mid = jnp.where(z == 4, CHUNKS // 2, jnp.where(z == 5, 5, CHUNKS))

        @pl.when(z > 0)
        def _():
            span(0, early, line_relay)

        plane_gather()

        @pl.when(z > 0)
        def _():
            span(early, mid, line_relay)

        pass_w()

        @pl.when(z > 0)
        def _():
            span(mid, CHUNKS, line_relay)

    @pl.when(z == 0)
    def _():
        cbuf[core] = xv[0:512, :]

    def w_wait(k):
        p = other(c, k)
        arrive(wbuf.at[p], w_gather.at[p])

    def r_wait(k):
        p = other(c, k)
        arrive(rbuf.at[p], r_gather.at[p])

    def c_wait(k):
        arrive(cbuf.at[1 - core, pl.ds(pl.multiple_of(k * CHUNK, CHUNK), CHUNK)], c_pair.at[k])

    span(0, CHUNKS, c_wait)
    for h in range(2):
        for b in range(4):
            ac[h * NB : (h + 1) * NB, b * NB : (b + 1) * NB] = cbuf[h, pl.ds(b, NB, stride=4), :]
    each(r_wait)
    each(w_wait)
    w00 = wbuf[:, 0].reshape(NB, NB)
    w01 = wbuf[:, 1].reshape(NB, NB)
    w11 = wbuf[:, 2].reshape(NB, NB)
    r0 = rbuf[:, 0].reshape(4 * NB, NB)
    r1 = rbuf[:, 1].reshape(4 * NB, NB)
    rows = jnp.concatenate([r0, r1], axis=1)
    lower = jnp.concatenate(
        [
            jnp.concatenate([w00, jnp.zeros((NB, NB), F32)], axis=1),
            jnp.concatenate([w01, w11], axis=1),
        ],
        axis=0,
    )
    pr[...] = dot_nt(rows, lower)
    pc[...] = dot_nn(lower, ac[...])

    @pl.when(last)
    def _():
        arrive(diag, diag_recv)

    @pl.when(corner)
    def _():
        span(0, n, lambda p: w_scatter(p).wait_send())
        diagonal().wait_send()

    @pl.when(both(r == 1, c == 0))
    def _():
        to_corner(0).wait_send()

    @pl.when(last)
    def _():
        to_corner(1).wait_send()

    @pl.when(left)
    def _():
        each(lambda k: r_scatter(k).wait_send())

    @pl.when(r == 1)
    def _():
        each(lambda k: w_down(k).wait_send())

    @pl.when(either(z == 0, up))
    def _():
        span(0, CHUNKS, lambda k: c_next(k, 0, chunk(k)).wait_send())

    @pl.when(either(z == 0, down))
    def _():
        span(0, CHUNKS, lambda k: c_next(k, 1, chunk(k)).wait_send())

    span(0, CHUNKS, lambda k: c_beside(k, chunk(k)).wait_send())
    each(lambda k: r_across(k).wait_send())
    each(lambda k: w_across(k).wait_send())


def update_kernel(x, pr, pc, diag, out, parts, sems):
    r = lax.axis_index("row")
    c = lax.axis_index("col")
    both = jnp.logical_and

    def store(a):
        return pltpu.make_async_copy(parts.at[a], out.at[pl.ds(a * 512, 512)], sems.at[a])

    for a in range(4):
        at = slice(a * NB, (a + 1) * NB)

        def put(b, value):
            parts[a, pl.ds(b, NB, stride=4), :] = value

        def update():
            delta = dot_nn(pr[at, :], pc[...])
            for b in range(4):
                put(b, x[pl.ds(a * 512 + b, NB, stride=4), :] - delta[:, b * NB : (b + 1) * NB])

            @pl.when(c == 0)
            def _():
                put(0, pr[at, 0:NB])

            @pl.when(c == 1)
            def _():
                put(0, pr[at, NB:])

        if a > 0:
            update()
        else:

            @pl.when(r < 2)
            def _():
                parts[0] = jnp.zeros((512, NB), F32)

                @pl.when(both(r == 1, c == 0))
                def _():
                    put(0, pr[at, 0:NB])

                @pl.when(both(r == c, c < 2))
                def _():
                    put(0, diag[...].T)

            @pl.when(r >= 2)
            def _():
                update()

        store(a).start()

    for a in range(4):
        store(a).wait()


def per_device(matrix):
    n = lax.axis_size("row")
    flat = matrix.reshape(2048, NB)
    dma = pltpu.SemaphoreType.DMA
    square = pltpu.VMEM((NB, NB), F32)
    whole = pl.BlockSpec(memory_space=pltpu.VMEM)
    flat = pltpu.with_memory_space_constraint(flat, pltpu.HBM)
    pr, pc, diag, x = pl.pallas_call(
        functools.partial(gather_kernel, n),
        out_shape=[
            pltpu.VMEM((4 * NB, 2 * NB), F32),
            pltpu.VMEM((2 * NB, 4 * NB), F32),
            square,
            pltpu.VMEM((2048, NB), F32),
        ],
        in_specs=[pl.BlockSpec(memory_space=pl.ANY)],
        out_specs=[whole] * 4,
        scratch_shapes=[
            pltpu.VMEM((512, NB), F32),
            pltpu.VMEM((2, NB, NB), F32),
            pltpu.VMEM((n, 2, 32, NB), F32),
            pltpu.VMEM((2, 512, NB), F32),
            pltpu.VMEM((n, 3, 8, NB), F32),
            pltpu.VMEM((n, 3, 8, NB), F32),
            pltpu.VMEM((2 * NB, 4 * NB), F32),
            square,
            square,
            square,
            square,
            square,
            square,
            square,
            dma((2,)),
            dma((2,)),
            dma,
            dma,
            dma,
            pltpu.SemaphoreType.REGULAR,
            pltpu.SemaphoreType.REGULAR,
            dma((2,)),
            dma((n,)),
            dma((n,)),
            dma((n,)),
            dma((CHUNKS,)),
            dma((2, CHUNKS)),
            dma((CHUNKS,)),
            dma((CHUNKS,)),
            dma,
            dma((n,)),
            dma((n,)),
            dma((n,)),
            dma((n,)),
        ],
        compiler_params=pltpu.CompilerParams(
            collective_id=0, has_side_effects=True, vmem_limit_bytes=24 * 1024 * 1024
        ),
    )(flat)
    out = pl.pallas_call(
        update_kernel,
        out_shape=pltpu.HBM((2048, NB), F32),
        in_specs=[whole] * 4,
        out_specs=pl.BlockSpec(memory_space=pltpu.HBM),
        scratch_shapes=[pltpu.VMEM((4, 512, NB), F32), dma((4,))],
        compiler_params=pltpu.CompilerParams(vmem_limit_bytes=24 * 1024 * 1024),
    )(x, pr, pc, diag)
    return out.reshape(matrix.shape)


def solution(mesh):
    specs = P(None, "row", None, None, "col", None)
    return jax.shard_map(
        per_device, mesh=mesh, in_specs=(specs,), out_specs=specs, check_vma=False
    )
```

```python
import functools

import jax
import jax.numpy as jnp
from jax import lax
from jax.experimental import pallas as pl
from jax.experimental.pallas import tpu as pltpu
from jax.sharding import PartitionSpec as P

F32 = jnp.float32
MESH = pl.DeviceIdType.MESH
HIGHEST = lax.Precision.HIGHEST
NB = 128
LOOK = 2
CHUNK = 64
CHUNKS = 512 // CHUNK


def dot_nn(a, b):
    return jnp.dot(a, b, precision=HIGHEST, preferred_element_type=F32)


def dot_nt(a, b):
    return lax.dot_general(
        a, b, (((1,), (1,)), ((), ())), precision=HIGHEST, preferred_element_type=F32
    )


def row_splat(tile, k):
    return jnp.broadcast_to(tile[k : k + 1, :], (8, NB))


def lane_splat(tile, k):
    return jnp.broadcast_to(tile[:, k : k + 1], (8, NB))


def eliminate(rows, rows_identity, columns):
    sub = lax.broadcasted_iota(jnp.int32, (8, NB), 0)
    columns = list(columns)
    upper, inverse, solved = rows, rows_identity, rows_identity
    scale = jnp.ones((8, NB), F32)
    for k in range(8):
        pivot = row_splat(columns[k], k)
        over = 1.0 / pivot
        here = sub == k
        ratio = columns[k] * over
        below = jnp.where(sub > k, ratio, 0.0)
        for j in range(k + 1, 8):
            r = row_splat(columns[j], k)
            columns[j] = jnp.where(here, r * over, columns[j] - ratio * r)
        upper = upper - below * row_splat(upper, k)
        inverse = inverse - below * row_splat(inverse, k)
        r = row_splat(solved, k)
        solved = jnp.where(here, r * over, solved - ratio * r)
        scale = jnp.where(here, lax.rsqrt(pivot), scale)
    return upper * scale, inverse * scale, solved


def factor(work, solved_rows, upper, inverse):
    lane = lax.broadcasted_iota(jnp.int32, (8, NB), 1)
    sub = lax.broadcasted_iota(jnp.int32, (8, NB), 0)
    solved_rows[...] = jnp.zeros((NB, NB), F32)
    steps = NB // 8
    for t in range(steps):
        o = 8 * t
        rows = work[o : o + 8, :]
        columns = [lane_splat(rows, o + j) for j in range(8)]
        block = (lane >= o) & (lane < o + 8)
        rows_identity = jnp.where(block, (lane - o == sub).astype(F32), rows)
        up, inv, solved = eliminate(rows, rows_identity, columns)
        upper[o : o + 8, :] = jnp.where(lane >= o, up, 0.0)
        inverse[o : o + 8, :] = jnp.where(lane < o + 8, inv, 0.0)
        solved_rows[o : o + 8, :] = solved
        splats = [row_splat(solved, j) for j in range(8)]
        for i in range(t + 1, min(t + 1 + LOOK, steps)):
            tile = work[8 * i : 8 * i + 8, :]
            total = jnp.where(block, 0.0, tile)
            for j in range(8):
                total = total - lane_splat(tile, o + j) * splats[j]
            work[8 * i : 8 * i + 8, :] = total
        rest = 8 * (t + 1 + LOOK)
        if rest < NB:
            tiles = work[rest:, :]
            lanes = lax.broadcasted_iota(jnp.int32, (NB - rest, NB), 1)
            own = (lanes >= o) & (lanes < o + 8)
            work[rest:, :] = jnp.where(own, 0.0, tiles) - dot_nn(
                jnp.where(own, tiles, 0.0), solved_rows[...]
            )


def gather_kernel(
    n,
    x_hbm,
    pr,
    pc,
    diag,
    xv,
    panel,
    lead,
    rbuf,
    cbuf,
    wbuf,
    wown,
    ac,
    work,
    solved_rows,
    upper,
    inverse,
    w10,
    handed,
    load_sem,
    lead_recv,
    lead_send,
    diag_recv,
    diag_send,
    go_plane,
    go_line,
    go_down,
    hand_recv,
    hand_send,
    hand_rows,
    hand_line,
    r_piece,
    r_gather,
    r_send_a,
    r_send_b,
    c_recv,
    c_send,
    c_pair,
    c_pair_send,
    w_piece,
    w_gather,
    w_send_a,
    w_send_b,
    w_send_c,
):
    r = lax.axis_index("row")
    c = lax.axis_index("col")
    z = r // 2
    core = lax.rem(r, 2)
    pair = r + 1 - 2 * core
    both, either, no = jnp.logical_and, jnp.logical_or, jnp.logical_not
    left = c < 2
    corner = both(r == 0, c == 0)
    last = both(r == 1, c == 1)

    def span(first, end, body):
        def step(k, carry):
            body(k)
            return carry

        lax.fori_loop(first, end, step, 0)

    def each(body):
        span(1, n, body)

    def other(me, k):
        return lax.rem(me + k, n)

    def copy(src, dst, send, recv, row, col):
        return pltpu.make_async_remote_copy(
            src_ref=src,
            dst_ref=dst,
            send_sem=send,
            recv_sem=recv,
            device_id=(row, col),
            device_id_type=MESH,
        )

    def signal(sem, row, col):
        pl.semaphore_signal(sem, inc=1, device_id=(row, col), device_id_type=MESH)

    def arrive(buffer, sem):
        pltpu.make_async_copy(buffer, buffer, sem).wait()

    hub = both(r == 1, c == 0)
    barrier = pltpu.get_barrier_semaphore()
    before = jnp.where(z < 5, r - 2, jnp.where(z < 7, r + 2, r - 2))
    signal(barrier, pair, c)

    @pl.when(z > 0)
    def _():
        signal(barrier, before, c)

    @pl.when(z != 4)
    def _():
        signal(barrier, 8, c)

    @pl.when(either(hub, both(z == 0, c != 0)))
    def _():
        signal(barrier, r + 12, c)

    @pl.when(hub)
    def _():
        signal(barrier, 12, c)

    for k in range(2):

        @pl.when(c != k)
        def _():
            signal(barrier, jnp.where(z > 0, r, 0), k)

    @pl.when(corner)
    def _():
        signal(barrier, 1, 1)

    top = pltpu.make_async_copy(x_hbm.at[pl.ds(0, 512)], xv.at[pl.ds(0, 512)], load_sem.at[0])
    below = pltpu.make_async_copy(
        x_hbm.at[pl.ds(512, 1536)], xv.at[pl.ds(512, 1536)], load_sem.at[1]
    )
    top.start()
    below.start()
    top.wait()

    @pl.when(left)
    def _():
        panel[0:NB, :] = xv[pl.ds(0, NB, stride=4), :]

    def load_rest():
        below.wait()

        @pl.when(left)
        def _():
            panel[NB:, :] = xv[pl.ds(512, 384, stride=4), :]

    def enter():
        after = jnp.where(either(z == 4, z == 5), 0, jnp.where(z == 6, 3, 1))
        heard = (
            1
            + after
            + jnp.where(r == 8, n - 2, 0)
            + jnp.where(both(z > 0, left), n - 1, 0)
            + jnp.where(both(r == 0, left), 2 * (n - 1), 0)
            + jnp.where(last, 1, 0)
        )
        pl.semaphore_wait(barrier, heard)

    def to_corner(b):
        return copy(panel.at[pl.ds(0, NB)], lead.at[b], lead_send, lead_recv.at[b], 0, 0)

    def r_scatter(k):
        p = other(c, k)
        return copy(
            panel.at[pl.ds(pl.multiple_of(p * 32, 32), 32)],
            rbuf.at[p, c],
            r_send_a.at[p],
            r_piece.at[c],
            r,
            p,
        )

    def r_across(k):
        p = other(c, k)
        return copy(rbuf.at[c], rbuf.at[c], r_send_b.at[p], r_gather.at[c], r, p)

    def plane_scatter():
        each(lambda k: r_scatter(k).start())
        rbuf[c, c] = panel[pl.ds(pl.multiple_of(c * 32, 32), 32), :]

    def plane_gather():
        @pl.when(c != 0)
        def _():
            arrive(rbuf.at[c, 0], r_piece.at[0])

        @pl.when(c != 1)
        def _():
            arrive(rbuf.at[c, 1], r_piece.at[1])

        each(lambda k: r_across(k).start())

    def chunk(k):
        return cbuf.at[core, pl.ds(pl.multiple_of(k * CHUNK, CHUNK), CHUNK)]

    def first_chunk(k):
        return xv.at[pl.ds(pl.multiple_of(k * CHUNK, CHUNK), CHUNK)]

    def c_next(k, way, src):
        there = lax.rem(r + 2 + way * (n - 4), n)
        return copy(src, chunk(k), c_send.at[way, k], c_recv.at[k], there, c)

    def c_beside(k, src):
        return copy(src, chunk(k), c_pair_send.at[k], c_pair.at[k], pair, c)

    def line_up(k):
        c_next(k, 0, first_chunk(k)).start()
        c_beside(k, first_chunk(k)).start()

    def line_down(k):
        c_next(k, 1, first_chunk(k)).start()

    up = both(z >= 1, z <= 3)
    down = z >= 6

    def line_relay(k):
        arrive(chunk(k), c_recv.at[k])

        @pl.when(up)
        def _():
            c_next(k, 0, chunk(k)).start()

        @pl.when(down)
        def _():
            c_next(k, 1, chunk(k)).start()

        c_beside(k, chunk(k)).start()

    def w_copy(send, recv, row, col):
        return copy(wbuf.at[c], wbuf.at[c], send, recv, row, col)

    def w_scatter(p):
        return copy(wown.at[p], wbuf.at[p], w_send_a.at[p], w_piece, 1, p)

    def w_down(k):
        p = other(r, k)
        return w_copy(w_send_b.at[p], w_piece, p, c)

    def w_across(k):
        p = other(c, k)
        return w_copy(w_send_c.at[p], w_gather.at[c], r, p)

    def diagonal():
        return copy(upper.at[1], diag, diag_send, diag_recv, 1, 1)

    def pass_w():
        arrive(wbuf.at[c], w_piece)

        @pl.when(r == 1)
        def _():
            pl.semaphore_wait(go_line, 1)
            each(lambda k: w_down(k).start())

        each(lambda k: w_across(k).start())

    def hand(b):
        src = panel if b == 0 else xv.at[pl.ds(0, 512)]
        dst = handed if b == 0 else cbuf.at[0]
        return copy(src, dst, hand_send.at[b], hand_recv.at[b], 1, 0)

    def hand_scatter(p):
        return copy(
            handed.at[pl.ds(pl.multiple_of(p * 32, 32), 32)],
            rbuf.at[p, 0],
            hand_rows.at[p],
            r_piece.at[0],
            0,
            p,
        )

    def hand_next(k, way):
        at = cbuf.at[0, pl.ds(pl.multiple_of(k * CHUNK, CHUNK), CHUNK)]
        return copy(at, at, hand_line.at[way, k], c_recv.at[k], 2 + way * (n - 4), 0)

    def middle():
        load_rest()
        arrive(lead.at[0], lead_recv.at[0])
        w0 = inverse[0]
        l10 = dot_nt(lead[0], w0)
        w10[...] = dot_nn(l10, w0)
        arrive(lead.at[1], lead_recv.at[1])
        work[...] = lead[1] - dot_nt(l10, l10)
        enter()
        signal(go_plane, 1, 0)
        hand(0).start()
        hand(1).start()

    @pl.when(corner)
    def _():
        work[...] = panel[0:NB, :]

        def block(b, carry):
            factor(work, solved_rows, upper.at[b], inverse.at[b])

            @pl.when(b == 0)
            def _():
                middle()

            return carry

        lax.fori_loop(0, 2, block, 0)
        wown[:, 0] = inverse[0].reshape(n, 8, NB)
        wown[:, 1] = -dot_nn(inverse[1], w10[...]).reshape(n, 8, NB)
        wown[:, 2] = inverse[1].reshape(n, 8, NB)
        span(0, n, lambda p: w_scatter(p).start())
        diagonal().start()
        rbuf[0, 0] = panel[0:32, :]
        plane_gather()
        pass_w()
        diag[...] = upper[0]

    @pl.when(no(corner))
    def _():
        enter()

        @pl.when(hub)
        def _():
            to_corner(0).start()

        @pl.when(last)
        def _():
            to_corner(1).start()

        @pl.when(r == 8)
        def _():
            signal(go_line, 1, c)

        @pl.when(z == 6)
        def _():
            signal(go_down, jnp.where(c == 0, 1, r - 12), c)

        @pl.when(both(r == 0, c == 1))
        def _():
            signal(go_plane, 1, 1)

        @pl.when(z == 0)
        def _():
            span(0, CHUNKS, line_up)

        load_rest()

        @pl.when(both(r == 1, left))
        def _():
            pl.semaphore_wait(go_plane, 1)

        @pl.when(left)
        def _():
            plane_scatter()

        @pl.when(hub)
        def _():
            arrive(handed, hand_recv.at[0])
            each(lambda p: hand_scatter(p).start())
            arrive(cbuf.at[0], hand_recv.at[1])
            span(0, CHUNKS, lambda k: hand_next(k, 0).start())
            pl.semaphore_wait(go_down, 2)
            span(0, CHUNKS, lambda k: hand_next(k, 1).start())

        @pl.when(z == 0)
        def _():
            @pl.when(no(hub))
            def _():
                pl.semaphore_wait(go_down, 1)

            span(0, CHUNKS, line_down)

        early = jnp.where(z == 1, CHUNKS // 2, jnp.where(z == 2, 1, 0))
        mid = jnp.where(z == 4, CHUNKS // 2, jnp.where(z == 5, 5, CHUNKS))

        @pl.when(z > 0)
        def _():
            span(0, early, line_relay)

        plane_gather()

        @pl.when(z > 0)
        def _():
            span(early, mid, line_relay)

        pass_w()

        @pl.when(z > 0)
        def _():
            span(mid, CHUNKS, line_relay)

    @pl.when(z == 0)
    def _():
        cbuf[core] = xv[0:512, :]

    def w_wait(k):
        p = other(c, k)
        arrive(wbuf.at[p], w_gather.at[p])

    def r_wait(k):
        p = other(c, k)
        arrive(rbuf.at[p], r_gather.at[p])

    def c_wait(k):
        arrive(cbuf.at[1 - core, pl.ds(pl.multiple_of(k * CHUNK, CHUNK), CHUNK)], c_pair.at[k])

    @pl.when(no(hub))
    def _():
        span(0, CHUNKS, c_wait)

    for h in range(2):
        for b in range(4):
            ac[h * NB : (h + 1) * NB, b * NB : (b + 1) * NB] = cbuf[h, pl.ds(b, NB, stride=4), :]
    each(r_wait)
    each(w_wait)
    w00 = wbuf[:, 0].reshape(NB, NB)
    w01 = wbuf[:, 1].reshape(NB, NB)
    w11 = wbuf[:, 2].reshape(NB, NB)
    r0 = rbuf[:, 0].reshape(4 * NB, NB)
    r1 = rbuf[:, 1].reshape(4 * NB, NB)
    rows = jnp.concatenate([r0, r1], axis=1)
    lower = jnp.concatenate(
        [
            jnp.concatenate([w00, jnp.zeros((NB, NB), F32)], axis=1),
            jnp.concatenate([w01, w11], axis=1),
        ],
        axis=0,
    )
    pr[...] = dot_nt(rows, lower)
    pc[...] = dot_nn(lower, ac[...])

    @pl.when(last)
    def _():
        arrive(diag, diag_recv)

    @pl.when(corner)
    def _():
        span(0, n, lambda p: w_scatter(p).wait_send())
        diagonal().wait_send()
        hand(0).wait_send()
        hand(1).wait_send()

    @pl.when(hub)
    def _():
        to_corner(0).wait_send()
        each(lambda p: hand_scatter(p).wait_send())
        span(0, CHUNKS, lambda k: hand_next(k, 0).wait_send())
        span(0, CHUNKS, lambda k: hand_next(k, 1).wait_send())

    @pl.when(last)
    def _():
        to_corner(1).wait_send()

    @pl.when(both(left, no(corner)))
    def _():
        each(lambda k: r_scatter(k).wait_send())

    @pl.when(r == 1)
    def _():
        each(lambda k: w_down(k).wait_send())

    @pl.when(either(both(z == 0, no(corner)), up))
    def _():
        span(0, CHUNKS, lambda k: c_next(k, 0, chunk(k)).wait_send())

    @pl.when(either(both(z == 0, no(corner)), down))
    def _():
        span(0, CHUNKS, lambda k: c_next(k, 1, chunk(k)).wait_send())

    @pl.when(no(corner))
    def _():
        span(0, CHUNKS, lambda k: c_beside(k, chunk(k)).wait_send())

    each(lambda k: r_across(k).wait_send())
    each(lambda k: w_across(k).wait_send())


def update_kernel(x, pr, pc, diag, out, parts, sems):
    r = lax.axis_index("row")
    c = lax.axis_index("col")
    both = jnp.logical_and

    def store(a):
        return pltpu.make_async_copy(parts.at[a], out.at[pl.ds(a * 512, 512)], sems.at[a])

    for a in range(4):
        at = slice(a * NB, (a + 1) * NB)

        def put(b, value):
            parts[a, pl.ds(b, NB, stride=4), :] = value

        def update():
            delta = dot_nn(pr[at, :], pc[...])
            for b in range(4):
                put(b, x[pl.ds(a * 512 + b, NB, stride=4), :] - delta[:, b * NB : (b + 1) * NB])

            @pl.when(c == 0)
            def _():
                put(0, pr[at, 0:NB])

            @pl.when(c == 1)
            def _():
                put(0, pr[at, NB:])

        if a > 0:
            update()
        else:

            @pl.when(r < 2)
            def _():
                parts[0] = jnp.zeros((512, NB), F32)

                @pl.when(both(r == 1, c == 0))
                def _():
                    put(0, pr[at, 0:NB])

                @pl.when(both(r == c, c < 2))
                def _():
                    put(0, diag[...].T)

            @pl.when(r >= 2)
            def _():
                update()

        store(a).start()

    for a in range(4):
        store(a).wait()


def per_device(matrix):
    n = lax.axis_size("row")
    flat = matrix.reshape(2048, NB)
    dma = pltpu.SemaphoreType.DMA
    square = pltpu.VMEM((NB, NB), F32)
    whole = pl.BlockSpec(memory_space=pltpu.VMEM)
    flat = pltpu.with_memory_space_constraint(flat, pltpu.HBM)
    pr, pc, diag, x = pl.pallas_call(
        functools.partial(gather_kernel, n),
        out_shape=[
            pltpu.VMEM((4 * NB, 2 * NB), F32),
            pltpu.VMEM((2 * NB, 4 * NB), F32),
            square,
            pltpu.VMEM((2048, NB), F32),
        ],
        in_specs=[pl.BlockSpec(memory_space=pl.ANY)],
        out_specs=[whole] * 4,
        scratch_shapes=[
            pltpu.VMEM((512, NB), F32),
            pltpu.VMEM((2, NB, NB), F32),
            pltpu.VMEM((n, 2, 32, NB), F32),
            pltpu.VMEM((2, 512, NB), F32),
            pltpu.VMEM((n, 3, 8, NB), F32),
            pltpu.VMEM((n, 3, 8, NB), F32),
            pltpu.VMEM((2 * NB, 4 * NB), F32),
            square,
            square,
            pltpu.VMEM((2, NB, NB), F32),
            pltpu.VMEM((2, NB, NB), F32),
            square,
            pltpu.VMEM((512, NB), F32),
            dma((2,)),
            dma((2,)),
            dma,
            dma,
            dma,
            pltpu.SemaphoreType.REGULAR,
            pltpu.SemaphoreType.REGULAR,
            pltpu.SemaphoreType.REGULAR,
            dma((2,)),
            dma((2,)),
            dma((n,)),
            dma((2, CHUNKS)),
            dma((2,)),
            dma((n,)),
            dma((n,)),
            dma((n,)),
            dma((CHUNKS,)),
            dma((2, CHUNKS)),
            dma((CHUNKS,)),
            dma((CHUNKS,)),
            dma,
            dma((n,)),
            dma((n,)),
            dma((n,)),
            dma((n,)),
        ],
        compiler_params=pltpu.CompilerParams(
            collective_id=0, has_side_effects=True, vmem_limit_bytes=24 * 1024 * 1024
        ),
    )(flat)
    out = pl.pallas_call(
        update_kernel,
        out_shape=pltpu.HBM((2048, NB), F32),
        in_specs=[whole] * 4,
        out_specs=pl.BlockSpec(memory_space=pltpu.HBM),
        scratch_shapes=[pltpu.VMEM((4, 512, NB), F32), dma((4,))],
        compiler_params=pltpu.CompilerParams(vmem_limit_bytes=24 * 1024 * 1024),
    )(x, pr, pc, diag)
    return out.reshape(matrix.shape)


def solution(mesh):
    specs = P(None, "row", None, None, "col", None)
    return jax.shard_map(
        per_device, mesh=mesh, in_specs=(specs,), out_specs=specs, check_vma=False
    )
```

```python
import functools

import jax
import jax.numpy as jnp
from jax import lax
from jax.experimental import pallas as pl
from jax.experimental.pallas import tpu as pltpu
from jax.sharding import PartitionSpec as P

F32 = jnp.float32
MESH = pl.DeviceIdType.MESH
HIGHEST = lax.Precision.HIGHEST
NB = 128
LOOK = 2
CHUNK = 64
CHUNKS = 512 // CHUNK
EARLY = (0, 6, 4, 2, 0, 0, 0, 1)
MID = (0, 8, 8, 8, 6, 0, 2, 4)


def dot_nn(a, b):
    return jnp.dot(a, b, precision=HIGHEST, preferred_element_type=F32)


def dot_nt(a, b):
    return lax.dot_general(
        a, b, (((1,), (1,)), ((), ())), precision=HIGHEST, preferred_element_type=F32
    )


def row_splat(tile, k):
    return jnp.broadcast_to(tile[k : k + 1, :], (8, NB))


def lane_splat(tile, k):
    return jnp.broadcast_to(tile[:, k : k + 1], (8, NB))


def eliminate(rows, rows_identity, columns):
    sub = lax.broadcasted_iota(jnp.int32, (8, NB), 0)
    columns = list(columns)
    upper, inverse, solved = rows, rows_identity, rows_identity
    scale = jnp.ones((8, NB), F32)
    for k in range(8):
        pivot = row_splat(columns[k], k)
        over = 1.0 / pivot
        here = sub == k
        ratio = columns[k] * over
        below = jnp.where(sub > k, ratio, 0.0)
        for j in range(k + 1, 8):
            r = row_splat(columns[j], k)
            columns[j] = jnp.where(here, r * over, columns[j] - ratio * r)
        upper = upper - below * row_splat(upper, k)
        inverse = inverse - below * row_splat(inverse, k)
        r = row_splat(solved, k)
        solved = jnp.where(here, r * over, solved - ratio * r)
        scale = jnp.where(here, lax.rsqrt(pivot), scale)
    return upper * scale, inverse * scale, solved


def factor(work, solved_rows, upper, inverse):
    lane = lax.broadcasted_iota(jnp.int32, (8, NB), 1)
    sub = lax.broadcasted_iota(jnp.int32, (8, NB), 0)
    solved_rows[...] = jnp.zeros((NB, NB), F32)
    steps = NB // 8
    for t in range(steps):
        o = 8 * t
        rows = work[o : o + 8, :]
        columns = [lane_splat(rows, o + j) for j in range(8)]
        block = (lane >= o) & (lane < o + 8)
        rows_identity = jnp.where(block, (lane - o == sub).astype(F32), rows)
        up, inv, solved = eliminate(rows, rows_identity, columns)
        upper[o : o + 8, :] = jnp.where(lane >= o, up, 0.0)
        inverse[o : o + 8, :] = jnp.where(lane < o + 8, inv, 0.0)
        solved_rows[o : o + 8, :] = solved
        splats = [row_splat(solved, j) for j in range(8)]
        for i in range(t + 1, min(t + 1 + LOOK, steps)):
            tile = work[8 * i : 8 * i + 8, :]
            total = jnp.where(block, 0.0, tile)
            for j in range(8):
                total = total - lane_splat(tile, o + j) * splats[j]
            work[8 * i : 8 * i + 8, :] = total
        rest = 8 * (t + 1 + LOOK)
        if rest < NB:
            tiles = work[rest:, :]
            lanes = lax.broadcasted_iota(jnp.int32, (NB - rest, NB), 1)
            own = (lanes >= o) & (lanes < o + 8)
            work[rest:, :] = jnp.where(own, 0.0, tiles) - dot_nn(
                jnp.where(own, tiles, 0.0), solved_rows[...]
            )


def gather_kernel(
    n,
    x_hbm,
    pr,
    pc,
    diag,
    xv,
    panel,
    lead,
    rbuf,
    cbuf,
    wbuf,
    wown,
    ac,
    work,
    solved_rows,
    upper,
    inverse,
    w10,
    handed,
    load_sem,
    lead_recv,
    lead_send,
    diag_recv,
    diag_send,
    go_plane,
    go_line,
    go_down,
    hand_recv,
    hand_send,
    hand_rows,
    hand_line,
    r_piece,
    r_gather,
    r_send_a,
    r_send_b,
    c_recv,
    c_send,
    c_pair,
    c_pair_send,
    w_piece,
    w_gather,
    w_send_a,
    w_send_b,
    w_send_c,
    w_pair,
    w_pair_send,
):
    r = lax.axis_index("row")
    c = lax.axis_index("col")
    z = r // 2
    core = lax.rem(r, 2)
    pair = r + 1 - 2 * core
    both, either, no = jnp.logical_and, jnp.logical_or, jnp.logical_not
    left = c < 2
    corner = both(r == 0, c == 0)
    last = both(r == 1, c == 1)

    def span(first, end, body):
        def step(k, carry):
            body(k)
            return carry

        lax.fori_loop(first, end, step, 0)

    def each(body):
        span(1, n, body)

    def other(me, k):
        return lax.rem(me + k, n)

    def copy(src, dst, send, recv, row, col):
        return pltpu.make_async_remote_copy(
            src_ref=src,
            dst_ref=dst,
            send_sem=send,
            recv_sem=recv,
            device_id=(row, col),
            device_id_type=MESH,
        )

    def signal(sem, row, col):
        pl.semaphore_signal(sem, inc=1, device_id=(row, col), device_id_type=MESH)

    def arrive(buffer, sem):
        pltpu.make_async_copy(buffer, buffer, sem).wait()

    hub = both(r == 1, c == 0)
    barrier = pltpu.get_barrier_semaphore()
    door = jnp.where(left, 2, 12)
    before = jnp.where(z < 5, r - 2, jnp.where(z < 7, r + 2, door + core))
    signal(barrier, pair, c)

    @pl.when(z > 0)
    def _():
        signal(barrier, before, c)

    @pl.when(z != 4)
    def _():
        signal(barrier, 8, c)

    @pl.when(either(hub, both(z == 0, c != 0)))
    def _():
        signal(barrier, door + core, c)

    @pl.when(hub)
    def _():
        signal(barrier, door, c)

    for k in range(2):

        @pl.when(c != k)
        def _():
            signal(barrier, jnp.where(z > 0, r, 0), k)

    @pl.when(corner)
    def _():
        signal(barrier, 1, 1)

    top = pltpu.make_async_copy(x_hbm.at[pl.ds(0, 512)], xv.at[pl.ds(0, 512)], load_sem.at[0])
    below = pltpu.make_async_copy(
        x_hbm.at[pl.ds(512, 1536)], xv.at[pl.ds(512, 1536)], load_sem.at[1]
    )
    top.start()
    below.start()
    top.wait()

    @pl.when(left)
    def _():
        panel[0:NB, :] = xv[pl.ds(0, NB, stride=4), :]

    def load_rest():
        below.wait()

        @pl.when(left)
        def _():
            panel[NB:, :] = xv[pl.ds(512, 384, stride=4), :]

    def enter():
        after = jnp.where(either(z == 4, z == 5), 0, 1)
        heard = (
            1
            + after
            + jnp.where(z == door // 2, 2, 0)
            + jnp.where(r == 8, n - 2, 0)
            + jnp.where(both(z > 0, left), n - 1, 0)
            + jnp.where(both(r == 0, left), 2 * (n - 1), 0)
            + jnp.where(last, 1, 0)
        )
        pl.semaphore_wait(barrier, heard)

    def to_corner(b):
        return copy(panel.at[pl.ds(0, NB)], lead.at[b], lead_send, lead_recv.at[b], 0, 0)

    def r_scatter(k):
        p = other(c, k)
        return copy(
            panel.at[pl.ds(pl.multiple_of(p * 32, 32), 32)],
            rbuf.at[p, c],
            r_send_a.at[p],
            r_piece.at[c],
            r,
            p,
        )

    def r_across(k):
        p = other(c, k)
        return copy(rbuf.at[c], rbuf.at[c], r_send_b.at[p], r_gather.at[c], r, p)

    def plane_scatter():
        each(lambda k: r_scatter(k).start())
        rbuf[c, c] = panel[pl.ds(pl.multiple_of(c * 32, 32), 32), :]

    def plane_gather():
        @pl.when(c != 0)
        def _():
            arrive(rbuf.at[c, 0], r_piece.at[0])

        @pl.when(c != 1)
        def _():
            arrive(rbuf.at[c, 1], r_piece.at[1])

        each(lambda k: r_across(k).start())

    def chunk(k):
        return cbuf.at[core, pl.ds(pl.multiple_of(k * CHUNK, CHUNK), CHUNK)]

    def first_chunk(k):
        return xv.at[pl.ds(pl.multiple_of(k * CHUNK, CHUNK), CHUNK)]

    def c_next(k, way, src):
        there = lax.rem(r + 2 + way * (n - 4), n)
        return copy(src, chunk(k), c_send.at[way, k], c_recv.at[k], there, c)

    def c_beside(k, src):
        return copy(src, chunk(k), c_pair_send.at[k], c_pair.at[k], pair, c)

    def line_up(k):
        c_next(k, 0, first_chunk(k)).start()
        c_beside(k, first_chunk(k)).start()

    def line_down(k):
        c_next(k, 1, first_chunk(k)).start()

    up = both(z >= 1, z <= 3)
    down = z >= 6

    def line_relay(k):
        arrive(chunk(k), c_recv.at[k])

        @pl.when(up)
        def _():
            c_next(k, 0, chunk(k)).start()

        @pl.when(down)
        def _():
            c_next(k, 1, chunk(k)).start()

        c_beside(k, chunk(k)).start()

    def w_copy(send, recv, row, col):
        return copy(wbuf.at[c], wbuf.at[c], send, recv, row, col)

    def w_scatter(p):
        return copy(wown.at[p], wbuf.at[p], w_send_a.at[p], w_piece, 1, p)

    def w_down(k):
        p = lax.rem(r + 2 * k, n)
        return w_copy(w_send_b.at[p], w_piece, p, c)

    def w_across(k):
        p = other(c, k)
        return w_copy(w_send_c.at[p], w_gather.at[c], r, p)

    def diagonal():
        return copy(upper.at[1], diag, diag_send, diag_recv, 1, 1)

    def w_beside(g):
        part = wbuf.at[pl.ds(4 * g, 4)]
        return copy(part, part, w_pair_send.at[g], w_pair.at[g], pair, c)

    def pass_w():
        arrive(wbuf.at[c], w_piece)

        @pl.when(r == 1)
        def _():
            pl.semaphore_wait(go_line, 1)
            span(1, n // 2, lambda k: w_down(k).start())

        each(lambda k: w_across(k).start())

    def hand(b):
        src = panel if b == 0 else xv.at[pl.ds(0, 512)]
        dst = handed if b == 0 else cbuf.at[0]
        return copy(src, dst, hand_send.at[b], hand_recv.at[b], 1, 0)

    def hand_scatter(p):
        return copy(
            handed.at[pl.ds(pl.multiple_of(p * 32, 32), 32)],
            rbuf.at[p, 0],
            hand_rows.at[p],
            r_piece.at[0],
            0,
            p,
        )

    def hand_next(k, way):
        at = cbuf.at[0, pl.ds(pl.multiple_of(k * CHUNK, CHUNK), CHUNK)]
        return copy(at, at, hand_line.at[way, k], c_recv.at[k], 2 + way * (n - 4), 0)

    def middle():
        load_rest()
        arrive(lead.at[0], lead_recv.at[0])
        hand(0).start()
        hand(1).start()
        w0 = inverse[0]
        l10 = dot_nt(lead[0], w0)
        w10[...] = dot_nn(l10, w0)
        arrive(lead.at[1], lead_recv.at[1])
        work[...] = lead[1] - dot_nt(l10, l10)
        enter()
        signal(go_plane, 1, 0)

    @pl.when(no(corner))
    def _():
        enter()

        @pl.when(hub)
        def _():
            to_corner(0).start()

        @pl.when(last)
        def _():
            to_corner(1).start()

        @pl.when(r == 8)
        def _():
            signal(go_line, 1, c)

        @pl.when(z == door // 2)
        def _():
            signal(go_down, jnp.where(c == 0, 1, core), c)

        @pl.when(both(r == 0, c == 1))
        def _():
            signal(go_plane, 1, 1)

        @pl.when(z == 0)
        def _():
            span(0, CHUNKS, line_up)

        load_rest()

        @pl.when(both(r == 1, left))
        def _():
            pl.semaphore_wait(go_plane, 1)

        @pl.when(left)
        def _():
            plane_scatter()

        @pl.when(hub)
        def _():
            arrive(handed, hand_recv.at[0])
            each(lambda p: hand_scatter(p).start())
            arrive(cbuf.at[0], hand_recv.at[1])
            span(0, CHUNKS, lambda k: hand_next(k, 0).start())
            pl.semaphore_wait(go_down, 2)
            span(0, CHUNKS, lambda k: hand_next(k, 1).start())

        @pl.when(z == 0)
        def _():
            @pl.when(no(hub))
            def _():
                pl.semaphore_wait(go_down, 1)

            span(0, CHUNKS, line_down)

        def by_plane(counts):
            value = counts[0]
            for k in range(1, 8):
                value = jnp.where(z == k, counts[k], value)
            return value

        early = by_plane(EARLY)
        mid = by_plane(MID)

        @pl.when(z > 0)
        def _():
            span(0, early, line_relay)

        plane_gather()

        @pl.when(z > 0)
        def _():
            span(early, mid, line_relay)

        @pl.when(core == 1)
        def _():
            pass_w()

        @pl.when(z > 0)
        def _():
            span(mid, CHUNKS, line_relay)

        @pl.when(core == 1)
        def _():
            for g in range(4):
                for p in range(4 * g, 4 * g + 4):

                    @pl.when(c != p)
                    def _():
                        arrive(wbuf.at[p], w_gather.at[p])

                w_beside(g).start()

    @pl.when(corner)
    def _():
        work[...] = panel[0:NB, :]

        def block(b, carry):
            factor(work, solved_rows, upper.at[b], inverse.at[b])

            @pl.when(b == 0)
            def _():
                middle()

            return carry

        lax.fori_loop(0, 2, block, 0)
        wown[:, 0] = inverse[0].reshape(n, 8, NB)
        wown[:, 1] = -dot_nn(inverse[1], w10[...]).reshape(n, 8, NB)
        wown[:, 2] = inverse[1].reshape(n, 8, NB)
        span(0, n, lambda p: w_scatter(p).start())
        diagonal().start()
        rbuf[0, 0] = panel[0:32, :]
        plane_gather()
        diag[...] = upper[0]

    @pl.when(z == 0)
    def _():
        cbuf[core] = xv[0:512, :]

    def r_wait(k):
        p = other(c, k)
        arrive(rbuf.at[p], r_gather.at[p])

    def c_wait(k):
        arrive(cbuf.at[1 - core, pl.ds(pl.multiple_of(k * CHUNK, CHUNK), CHUNK)], c_pair.at[k])

    @pl.when(no(hub))
    def _():
        span(0, CHUNKS, c_wait)

    for h in range(2):
        for b in range(4):
            ac[h * NB : (h + 1) * NB, b * NB : (b + 1) * NB] = cbuf[h, pl.ds(b, NB, stride=4), :]
    each(r_wait)

    @pl.when(core == 0)
    def _():
        for g in range(4):
            arrive(wbuf.at[pl.ds(4 * g, 4)], w_pair.at[g])

    w00 = wbuf[:, 0].reshape(NB, NB)
    w01 = wbuf[:, 1].reshape(NB, NB)
    w11 = wbuf[:, 2].reshape(NB, NB)
    r0 = rbuf[:, 0].reshape(4 * NB, NB)
    r1 = rbuf[:, 1].reshape(4 * NB, NB)
    rows = jnp.concatenate([r0, r1], axis=1)
    lower = jnp.concatenate(
        [
            jnp.concatenate([w00, jnp.zeros((NB, NB), F32)], axis=1),
            jnp.concatenate([w01, w11], axis=1),
        ],
        axis=0,
    )
    pr[...] = dot_nt(rows, lower)
    pc[...] = dot_nn(lower, ac[...])

    @pl.when(last)
    def _():
        arrive(diag, diag_recv)

    @pl.when(corner)
    def _():
        span(0, n, lambda p: w_scatter(p).wait_send())
        diagonal().wait_send()
        hand(0).wait_send()
        hand(1).wait_send()

    @pl.when(hub)
    def _():
        to_corner(0).wait_send()
        each(lambda p: hand_scatter(p).wait_send())
        span(0, CHUNKS, lambda k: hand_next(k, 0).wait_send())
        span(0, CHUNKS, lambda k: hand_next(k, 1).wait_send())

    @pl.when(last)
    def _():
        to_corner(1).wait_send()

    @pl.when(both(left, no(corner)))
    def _():
        each(lambda k: r_scatter(k).wait_send())

    @pl.when(r == 1)
    def _():
        span(1, n // 2, lambda k: w_down(k).wait_send())

    @pl.when(either(both(z == 0, no(corner)), up))
    def _():
        span(0, CHUNKS, lambda k: c_next(k, 0, chunk(k)).wait_send())

    @pl.when(either(both(z == 0, no(corner)), down))
    def _():
        span(0, CHUNKS, lambda k: c_next(k, 1, chunk(k)).wait_send())

    @pl.when(no(corner))
    def _():
        span(0, CHUNKS, lambda k: c_beside(k, chunk(k)).wait_send())

    each(lambda k: r_across(k).wait_send())

    @pl.when(core == 1)
    def _():
        each(lambda k: w_across(k).wait_send())
        for g in range(4):
            w_beside(g).wait_send()


def update_kernel(x, pr, pc, diag, out, parts, sems):
    r = lax.axis_index("row")
    c = lax.axis_index("col")
    both = jnp.logical_and

    def store(a):
        return pltpu.make_async_copy(parts.at[a], out.at[pl.ds(a * 512, 512)], sems.at[a])

    for a in range(4):
        at = slice(a * NB, (a + 1) * NB)

        def put(b, value):
            parts[a, pl.ds(b, NB, stride=4), :] = value

        def update():
            delta = dot_nn(pr[at, :], pc[...])
            for b in range(4):
                put(b, x[pl.ds(a * 512 + b, NB, stride=4), :] - delta[:, b * NB : (b + 1) * NB])

            @pl.when(c == 0)
            def _():
                put(0, pr[at, 0:NB])

            @pl.when(c == 1)
            def _():
                put(0, pr[at, NB:])

        if a > 0:
            update()
        else:

            @pl.when(r < 2)
            def _():
                parts[0] = jnp.zeros((512, NB), F32)

                @pl.when(both(r == 1, c == 0))
                def _():
                    put(0, pr[at, 0:NB])

                @pl.when(both(r == c, c < 2))
                def _():
                    put(0, diag[...].T)

            @pl.when(r >= 2)
            def _():
                update()

        store(a).start()

    for a in range(4):
        store(a).wait()


def per_device(matrix):
    n = lax.axis_size("row")
    flat = matrix.reshape(2048, NB)
    dma = pltpu.SemaphoreType.DMA
    square = pltpu.VMEM((NB, NB), F32)
    whole = pl.BlockSpec(memory_space=pltpu.VMEM)
    flat = pltpu.with_memory_space_constraint(flat, pltpu.HBM)
    pr, pc, diag, x = pl.pallas_call(
        functools.partial(gather_kernel, n),
        out_shape=[
            pltpu.VMEM((4 * NB, 2 * NB), F32),
            pltpu.VMEM((2 * NB, 4 * NB), F32),
            square,
            pltpu.VMEM((2048, NB), F32),
        ],
        in_specs=[pl.BlockSpec(memory_space=pl.ANY)],
        out_specs=[whole] * 4,
        scratch_shapes=[
            pltpu.VMEM((512, NB), F32),
            pltpu.VMEM((2, NB, NB), F32),
            pltpu.VMEM((n, 2, 32, NB), F32),
            pltpu.VMEM((2, 512, NB), F32),
            pltpu.VMEM((n, 3, 8, NB), F32),
            pltpu.VMEM((n, 3, 8, NB), F32),
            pltpu.VMEM((2 * NB, 4 * NB), F32),
            square,
            square,
            pltpu.VMEM((2, NB, NB), F32),
            pltpu.VMEM((2, NB, NB), F32),
            square,
            pltpu.VMEM((512, NB), F32),
            dma((2,)),
            dma((2,)),
            dma,
            dma,
            dma,
            pltpu.SemaphoreType.REGULAR,
            pltpu.SemaphoreType.REGULAR,
            pltpu.SemaphoreType.REGULAR,
            dma((2,)),
            dma((2,)),
            dma((n,)),
            dma((2, CHUNKS)),
            dma((2,)),
            dma((n,)),
            dma((n,)),
            dma((n,)),
            dma((CHUNKS,)),
            dma((2, CHUNKS)),
            dma((CHUNKS,)),
            dma((CHUNKS,)),
            dma,
            dma((n,)),
            dma((n,)),
            dma((n,)),
            dma((n,)),
            dma((4,)),
            dma((4,)),
        ],
        compiler_params=pltpu.CompilerParams(
            collective_id=0, has_side_effects=True, vmem_limit_bytes=24 * 1024 * 1024
        ),
    )(flat)
    out = pl.pallas_call(
        update_kernel,
        out_shape=pltpu.HBM((2048, NB), F32),
        in_specs=[whole] * 4,
        out_specs=pl.BlockSpec(memory_space=pltpu.HBM),
        scratch_shapes=[pltpu.VMEM((4, 512, NB), F32), dma((4,))],
        compiler_params=pltpu.CompilerParams(vmem_limit_bytes=24 * 1024 * 1024),
    )(x, pr, pc, diag)
    return out.reshape(matrix.shape)


def solution(mesh):
    specs = P(None, "row", None, None, "col", None)
    return jax.shard_map(
        per_device, mesh=mesh, in_specs=(specs,), out_specs=specs, check_vma=False
    )
```

```python
import functools

import jax
import jax.numpy as jnp
from jax import lax
from jax.experimental import pallas as pl
from jax.experimental.pallas import tpu as pltpu
from jax.sharding import PartitionSpec as P

F32 = jnp.float32
MESH = pl.DeviceIdType.MESH
HIGHEST = lax.Precision.HIGHEST
NB = 128
LOOK = 2
CHUNK = 64
CHUNKS = 512 // CHUNK
EARLY = (0, 6, 4, 2, 0, 0, 0, 1)
MID = (0, 8, 8, 8, 6, 0, 2, 4)


def dot_nn(a, b):
    return jnp.dot(a, b, precision=HIGHEST, preferred_element_type=F32)


def dot_nt(a, b):
    return lax.dot_general(
        a, b, (((1,), (1,)), ((), ())), precision=HIGHEST, preferred_element_type=F32
    )


def row_splat(tile, k):
    return jnp.broadcast_to(tile[k : k + 1, :], (8, NB))


def lane_splat(tile, k):
    return jnp.broadcast_to(tile[:, k : k + 1], (8, NB))


def eliminate(rows, rows_identity, columns):
    sub = lax.broadcasted_iota(jnp.int32, (8, NB), 0)
    columns = list(columns)
    upper, inverse, solved = rows, rows_identity, rows_identity
    scale = jnp.ones((8, NB), F32)
    for k in range(8):
        pivot = row_splat(columns[k], k)
        over = 1.0 / pivot
        here = sub == k
        ratio = columns[k] * over
        below = jnp.where(sub > k, ratio, 0.0)
        for j in range(k + 1, 8):
            r = row_splat(columns[j], k)
            columns[j] = jnp.where(here, r * over, columns[j] - ratio * r)
        upper = upper - below * row_splat(upper, k)
        inverse = inverse - below * row_splat(inverse, k)
        r = row_splat(solved, k)
        solved = jnp.where(here, r * over, solved - ratio * r)
        scale = jnp.where(here, lax.rsqrt(pivot), scale)
    return upper * scale, inverse * scale, solved


def factor(work, solved_rows, upper, inverse):
    lane = lax.broadcasted_iota(jnp.int32, (8, NB), 1)
    sub = lax.broadcasted_iota(jnp.int32, (8, NB), 0)
    solved_rows[...] = jnp.zeros((NB, NB), F32)
    steps = NB // 8
    for t in range(steps):
        o = 8 * t
        rows = work[o : o + 8, :]
        columns = [lane_splat(rows, o + j) for j in range(8)]
        block = (lane >= o) & (lane < o + 8)
        rows_identity = jnp.where(block, (lane - o == sub).astype(F32), rows)
        up, inv, solved = eliminate(rows, rows_identity, columns)
        upper[o : o + 8, :] = jnp.where(lane >= o, up, 0.0)
        inverse[o : o + 8, :] = jnp.where(lane < o + 8, inv, 0.0)
        solved_rows[o : o + 8, :] = solved
        splats = [row_splat(solved, j) for j in range(8)]
        for i in range(t + 1, min(t + 1 + LOOK, steps)):
            tile = work[8 * i : 8 * i + 8, :]
            total = jnp.where(block, 0.0, tile)
            for j in range(8):
                total = total - lane_splat(tile, o + j) * splats[j]
            work[8 * i : 8 * i + 8, :] = total
        rest = 8 * (t + 1 + LOOK)
        if rest < NB:
            tiles = work[rest:, :]
            lanes = lax.broadcasted_iota(jnp.int32, (NB - rest, NB), 1)
            own = (lanes >= o) & (lanes < o + 8)
            work[rest:, :] = jnp.where(own, 0.0, tiles) - dot_nn(
                jnp.where(own, tiles, 0.0), solved_rows[...]
            )


def gather_kernel(
    n,
    x_hbm,
    pr,
    pc,
    diag,
    xv,
    panel,
    lead,
    rbuf,
    cbuf,
    wbuf,
    wown,
    ac,
    work,
    solved_rows,
    upper,
    inverse,
    w10,
    handed,
    load_sem,
    lead_recv,
    lead_send,
    diag_recv,
    diag_send,
    go_plane,
    go_line,
    go_down,
    hand_recv,
    hand_send,
    hand_rows,
    hand_line,
    r_piece,
    r_gather,
    r_send_a,
    r_send_b,
    c_recv,
    c_send,
    c_pair,
    c_pair_send,
    w_piece,
    w_gather,
    w_send_a,
    w_send_b,
    w_send_c,
    w_pair,
    w_pair_send,
):
    r = lax.axis_index("row")
    c = lax.axis_index("col")
    z = r // 2
    core = lax.rem(r, 2)
    pair = r + 1 - 2 * core
    both, either, no = jnp.logical_and, jnp.logical_or, jnp.logical_not
    left = c < 2
    corner = both(r == 0, c == 0)
    last = both(r == 1, c == 1)

    def span(first, end, body):
        def step(k, carry):
            body(k)
            return carry

        lax.fori_loop(first, end, step, 0)

    def each(body):
        span(1, n, body)

    def other(me, k):
        return lax.rem(me + k, n)

    def copy(src, dst, send, recv, row, col):
        return pltpu.make_async_remote_copy(
            src_ref=src,
            dst_ref=dst,
            send_sem=send,
            recv_sem=recv,
            device_id=(row, col),
            device_id_type=MESH,
        )

    def signal(sem, row, col):
        pl.semaphore_signal(sem, inc=1, device_id=(row, col), device_id_type=MESH)

    def arrive(buffer, sem):
        pltpu.make_async_copy(buffer, buffer, sem).wait()

    hub = both(r == 1, c == 0)
    barrier = pltpu.get_barrier_semaphore()
    door = jnp.where(left, 2, 12)
    before = jnp.where(z < 5, r - 2, jnp.where(z < 7, r + 2, door + core))
    signal(barrier, pair, c)

    @pl.when(z > 0)
    def _():
        signal(barrier, before, c)

    @pl.when(z != 4)
    def _():
        signal(barrier, 8, c)

    @pl.when(either(hub, both(z == 0, c != 0)))
    def _():
        signal(barrier, door + core, c)

    @pl.when(hub)
    def _():
        signal(barrier, door, c)

    for k in range(2):

        @pl.when(c != k)
        def _():
            signal(barrier, jnp.where(z > 0, r, 0), k)

    @pl.when(corner)
    def _():
        signal(barrier, 1, 1)

    top = pltpu.make_async_copy(x_hbm.at[pl.ds(0, 512)], xv.at[pl.ds(0, 512)], load_sem.at[0])
    below = pltpu.make_async_copy(
        x_hbm.at[pl.ds(512, 1536)], xv.at[pl.ds(512, 1536)], load_sem.at[1]
    )
    top.start()
    below.start()
    top.wait()

    @pl.when(left)
    def _():
        panel[0:NB, :] = xv[pl.ds(0, NB, stride=4), :]

    def load_rest():
        below.wait()

        @pl.when(left)
        def _():
            panel[NB:, :] = xv[pl.ds(512, 384, stride=4), :]

    def enter():
        after = jnp.where(either(z == 4, z == 5), 0, 1)
        heard = (
            1
            + after
            + jnp.where(z == door // 2, 2, 0)
            + jnp.where(r == 8, n - 2, 0)
            + jnp.where(both(z > 0, left), n - 1, 0)
            + jnp.where(both(r == 0, left), 2 * (n - 1), 0)
            + jnp.where(last, 1, 0)
        )
        pl.semaphore_wait(barrier, heard)

    def to_corner(b):
        return copy(panel.at[pl.ds(0, NB)], lead.at[b], lead_send, lead_recv.at[b], 0, 0)

    def r_scatter(k):
        p = other(c, k)
        return copy(
            panel.at[pl.ds(pl.multiple_of(p * 32, 32), 32)],
            rbuf.at[p, c],
            r_send_a.at[p],
            r_piece.at[c],
            r,
            p,
        )

    def r_across(k):
        p = other(c, k)
        return copy(rbuf.at[c], rbuf.at[c], r_send_b.at[p], r_gather.at[c], r, p)

    def plane_scatter():
        each(lambda k: r_scatter(k).start())
        rbuf[c, c] = panel[pl.ds(pl.multiple_of(c * 32, 32), 32), :]

    def r_batch(first):
        def send(k):
            p = other(c, k)
            early = either(p < 4, p >= 12)

            @pl.when(early if first else no(early))
            def _():
                r_across(k).start()

        each(send)

    def plane_gather():
        @pl.when(c != 0)
        def _():
            arrive(rbuf.at[c, 0], r_piece.at[0])

        @pl.when(c != 1)
        def _():
            arrive(rbuf.at[c, 1], r_piece.at[1])

        r_batch(True)

        @pl.when(core == 0)
        def _():
            r_batch(False)

    def chunk(k):
        return cbuf.at[core, pl.ds(pl.multiple_of(k * CHUNK, CHUNK), CHUNK)]

    def first_chunk(k):
        return xv.at[pl.ds(pl.multiple_of(k * CHUNK, CHUNK), CHUNK)]

    def c_next(k, way, src):
        there = lax.rem(r + 2 + way * (n - 4), n)
        return copy(src, chunk(k), c_send.at[way, k], c_recv.at[k], there, c)

    def c_beside(k, src):
        return copy(src, chunk(k), c_pair_send.at[k], c_pair.at[k], pair, c)

    def line_up(k):
        c_next(k, 0, first_chunk(k)).start()
        c_beside(k, first_chunk(k)).start()

    def line_down(k):
        c_next(k, 1, first_chunk(k)).start()

    up = both(z >= 1, z <= 3)
    down = z >= 6

    def line_relay(k):
        arrive(chunk(k), c_recv.at[k])

        @pl.when(up)
        def _():
            c_next(k, 0, chunk(k)).start()

        @pl.when(down)
        def _():
            c_next(k, 1, chunk(k)).start()

        c_beside(k, chunk(k)).start()

    def w_copy(send, recv, row, col):
        return copy(wbuf.at[c], wbuf.at[c], send, recv, row, col)

    def w_scatter(p):
        return copy(wown.at[p], wbuf.at[p], w_send_a.at[p], w_piece, 1, p)

    def w_down(k):
        p = lax.rem(r + 2 * k, n)
        return w_copy(w_send_b.at[p], w_piece, p, c)

    def w_across(k):
        p = other(c, k)
        return w_copy(w_send_c.at[p], w_gather.at[c], r, p)

    def diagonal():
        return copy(upper.at[1], diag, diag_send, diag_recv, 1, 1)

    def w_beside(g):
        part = wbuf.at[pl.ds(4 * g, 4)]
        return copy(part, part, w_pair_send.at[g], w_pair.at[g], pair, c)

    def pass_w():
        arrive(wbuf.at[c], w_piece)

        @pl.when(r == 1)
        def _():
            pl.semaphore_wait(go_line, 1)
            span(1, n // 2, lambda k: w_down(k).start())

        for near in (True, False):

            def send(k):
                @pl.when((other(c, k) < 4) == near)
                def _():
                    w_across(k).start()

            each(send)

        r_batch(False)

    def hand(b):
        src = panel if b == 0 else xv.at[pl.ds(0, 512)]
        dst = handed if b == 0 else cbuf.at[0]
        return copy(src, dst, hand_send.at[b], hand_recv.at[b], 1, 0)

    def hand_scatter(p):
        return copy(
            handed.at[pl.ds(pl.multiple_of(p * 32, 32), 32)],
            rbuf.at[p, 0],
            hand_rows.at[p],
            r_piece.at[0],
            0,
            p,
        )

    def hand_next(k, way):
        at = cbuf.at[0, pl.ds(pl.multiple_of(k * CHUNK, CHUNK), CHUNK)]
        return copy(at, at, hand_line.at[way, k], c_recv.at[k], 2 + way * (n - 4), 0)

    def middle():
        load_rest()
        arrive(lead.at[0], lead_recv.at[0])
        hand(0).start()
        hand(1).start()
        w0 = inverse[0]
        l10 = dot_nt(lead[0], w0)
        w10[...] = dot_nn(l10, w0)
        arrive(lead.at[1], lead_recv.at[1])
        work[...] = lead[1] - dot_nt(l10, l10)
        enter()
        signal(go_plane, 1, 0)

    @pl.when(no(corner))
    def _():
        enter()

        @pl.when(hub)
        def _():
            to_corner(0).start()

        @pl.when(last)
        def _():
            to_corner(1).start()

        @pl.when(r == 8)
        def _():
            signal(go_line, 1, c)

        @pl.when(z == door // 2)
        def _():
            signal(go_down, jnp.where(c == 0, 1, core), c)

        @pl.when(both(r == 0, c == 1))
        def _():
            signal(go_plane, 1, 1)

        @pl.when(z == 0)
        def _():
            span(0, CHUNKS, line_up)

        load_rest()

        @pl.when(both(r == 1, left))
        def _():
            pl.semaphore_wait(go_plane, 1)

        @pl.when(left)
        def _():
            plane_scatter()

        @pl.when(hub)
        def _():
            arrive(handed, hand_recv.at[0])
            each(lambda p: hand_scatter(p).start())
            arrive(cbuf.at[0], hand_recv.at[1])
            span(0, CHUNKS, lambda k: hand_next(k, 0).start())
            pl.semaphore_wait(go_down, 2)
            span(0, CHUNKS, lambda k: hand_next(k, 1).start())

        @pl.when(z == 0)
        def _():
            @pl.when(no(hub))
            def _():
                pl.semaphore_wait(go_down, 1)

            span(0, CHUNKS, line_down)

        def by_plane(counts):
            value = counts[0]
            for k in range(1, 8):
                value = jnp.where(z == k, counts[k], value)
            return value

        early = by_plane(EARLY)
        mid = by_plane(MID)

        @pl.when(z > 0)
        def _():
            span(0, early, line_relay)

        plane_gather()

        @pl.when(z > 0)
        def _():
            span(early, mid, line_relay)

        @pl.when(core == 1)
        def _():
            pass_w()

        @pl.when(z > 0)
        def _():
            span(mid, CHUNKS, line_relay)

        @pl.when(core == 1)
        def _():
            for g in range(4):
                for p in range(4 * g, 4 * g + 4):

                    @pl.when(c != p)
                    def _():
                        arrive(wbuf.at[p], w_gather.at[p])

                w_beside(g).start()

    @pl.when(corner)
    def _():
        work[...] = panel[0:NB, :]

        def block(b, carry):
            factor(work, solved_rows, upper.at[b], inverse.at[b])

            @pl.when(b == 0)
            def _():
                middle()

            return carry

        lax.fori_loop(0, 2, block, 0)
        wown[:, 0] = inverse[0].reshape(n, 8, NB)
        wown[:, 1] = -dot_nn(inverse[1], w10[...]).reshape(n, 8, NB)
        wown[:, 2] = inverse[1].reshape(n, 8, NB)
        for p in range(n):
            w_scatter((p + n // 2) % n).start()
        diagonal().start()
        rbuf[0, 0] = panel[0:32, :]
        plane_gather()
        diag[...] = upper[0]

    @pl.when(z == 0)
    def _():
        cbuf[core] = xv[0:512, :]

    def r_wait(k):
        p = other(c, k)
        arrive(rbuf.at[p], r_gather.at[p])

    def c_wait(k):
        arrive(cbuf.at[1 - core, pl.ds(pl.multiple_of(k * CHUNK, CHUNK), CHUNK)], c_pair.at[k])

    @pl.when(no(hub))
    def _():
        span(0, CHUNKS, c_wait)

    for h in range(2):
        for b in range(4):
            ac[h * NB : (h + 1) * NB, b * NB : (b + 1) * NB] = cbuf[h, pl.ds(b, NB, stride=4), :]
    each(r_wait)

    @pl.when(core == 0)
    def _():
        for g in range(4):
            arrive(wbuf.at[pl.ds(4 * g, 4)], w_pair.at[g])

    w00 = wbuf[:, 0].reshape(NB, NB)
    w01 = wbuf[:, 1].reshape(NB, NB)
    w11 = wbuf[:, 2].reshape(NB, NB)
    r0 = rbuf[:, 0].reshape(4 * NB, NB)
    r1 = rbuf[:, 1].reshape(4 * NB, NB)
    rows = jnp.concatenate([r0, r1], axis=1)
    lower = jnp.concatenate(
        [
            jnp.concatenate([w00, jnp.zeros((NB, NB), F32)], axis=1),
            jnp.concatenate([w01, w11], axis=1),
        ],
        axis=0,
    )
    pr[...] = dot_nt(rows, lower)
    pc[...] = dot_nn(lower, ac[...])

    @pl.when(last)
    def _():
        arrive(diag, diag_recv)

    @pl.when(corner)
    def _():
        span(0, n, lambda p: w_scatter(p).wait_send())
        diagonal().wait_send()
        hand(0).wait_send()
        hand(1).wait_send()

    @pl.when(hub)
    def _():
        to_corner(0).wait_send()
        each(lambda p: hand_scatter(p).wait_send())
        span(0, CHUNKS, lambda k: hand_next(k, 0).wait_send())
        span(0, CHUNKS, lambda k: hand_next(k, 1).wait_send())

    @pl.when(last)
    def _():
        to_corner(1).wait_send()

    @pl.when(both(left, no(corner)))
    def _():
        each(lambda k: r_scatter(k).wait_send())

    @pl.when(r == 1)
    def _():
        span(1, n // 2, lambda k: w_down(k).wait_send())

    @pl.when(either(both(z == 0, no(corner)), up))
    def _():
        span(0, CHUNKS, lambda k: c_next(k, 0, chunk(k)).wait_send())

    @pl.when(either(both(z == 0, no(corner)), down))
    def _():
        span(0, CHUNKS, lambda k: c_next(k, 1, chunk(k)).wait_send())

    @pl.when(no(corner))
    def _():
        span(0, CHUNKS, lambda k: c_beside(k, chunk(k)).wait_send())

    each(lambda k: r_across(k).wait_send())

    @pl.when(core == 1)
    def _():
        each(lambda k: w_across(k).wait_send())
        for g in range(4):
            w_beside(g).wait_send()


def update_kernel(x, pr, pc, diag, out, parts, sems):
    r = lax.axis_index("row")
    c = lax.axis_index("col")
    both = jnp.logical_and

    def store(a):
        return pltpu.make_async_copy(parts.at[a], out.at[pl.ds(a * 512, 512)], sems.at[a])

    for a in range(4):
        at = slice(a * NB, (a + 1) * NB)

        def put(b, value):
            parts[a, pl.ds(b, NB, stride=4), :] = value

        def update():
            delta = dot_nn(pr[at, :], pc[...])
            for b in range(4):
                put(b, x[pl.ds(a * 512 + b, NB, stride=4), :] - delta[:, b * NB : (b + 1) * NB])

            @pl.when(c == 0)
            def _():
                put(0, pr[at, 0:NB])

            @pl.when(c == 1)
            def _():
                put(0, pr[at, NB:])

        if a > 0:
            update()
        else:

            @pl.when(r < 2)
            def _():
                parts[0] = jnp.zeros((512, NB), F32)

                @pl.when(both(r == 1, c == 0))
                def _():
                    put(0, pr[at, 0:NB])

                @pl.when(both(r == c, c < 2))
                def _():
                    put(0, diag[...].T)

            @pl.when(r >= 2)
            def _():
                update()

        store(a).start()

    for a in range(4):
        store(a).wait()


def per_device(matrix):
    n = lax.axis_size("row")
    flat = matrix.reshape(2048, NB)
    dma = pltpu.SemaphoreType.DMA
    square = pltpu.VMEM((NB, NB), F32)
    whole = pl.BlockSpec(memory_space=pltpu.VMEM)
    flat = pltpu.with_memory_space_constraint(flat, pltpu.HBM)
    pr, pc, diag, x = pl.pallas_call(
        functools.partial(gather_kernel, n),
        out_shape=[
            pltpu.VMEM((4 * NB, 2 * NB), F32),
            pltpu.VMEM((2 * NB, 4 * NB), F32),
            square,
            pltpu.VMEM((2048, NB), F32),
        ],
        in_specs=[pl.BlockSpec(memory_space=pl.ANY)],
        out_specs=[whole] * 4,
        scratch_shapes=[
            pltpu.VMEM((512, NB), F32),
            pltpu.VMEM((2, NB, NB), F32),
            pltpu.VMEM((n, 2, 32, NB), F32),
            pltpu.VMEM((2, 512, NB), F32),
            pltpu.VMEM((n, 3, 8, NB), F32),
            pltpu.VMEM((n, 3, 8, NB), F32),
            pltpu.VMEM((2 * NB, 4 * NB), F32),
            square,
            square,
            pltpu.VMEM((2, NB, NB), F32),
            pltpu.VMEM((2, NB, NB), F32),
            square,
            pltpu.VMEM((512, NB), F32),
            dma((2,)),
            dma((2,)),
            dma,
            dma,
            dma,
            pltpu.SemaphoreType.REGULAR,
            pltpu.SemaphoreType.REGULAR,
            pltpu.SemaphoreType.REGULAR,
            dma((2,)),
            dma((2,)),
            dma((n,)),
            dma((2, CHUNKS)),
            dma((2,)),
            dma((n,)),
            dma((n,)),
            dma((n,)),
            dma((CHUNKS,)),
            dma((2, CHUNKS)),
            dma((CHUNKS,)),
            dma((CHUNKS,)),
            dma,
            dma((n,)),
            dma((n,)),
            dma((n,)),
            dma((n,)),
            dma((4,)),
            dma((4,)),
        ],
        compiler_params=pltpu.CompilerParams(
            collective_id=0, has_side_effects=True, vmem_limit_bytes=24 * 1024 * 1024
        ),
    )(flat)
    out = pl.pallas_call(
        update_kernel,
        out_shape=pltpu.HBM((2048, NB), F32),
        in_specs=[whole] * 4,
        out_specs=pl.BlockSpec(memory_space=pltpu.HBM),
        scratch_shapes=[pltpu.VMEM((4, 512, NB), F32), dma((4,))],
        compiler_params=pltpu.CompilerParams(vmem_limit_bytes=24 * 1024 * 1024),
    )(x, pr, pc, diag)
    return out.reshape(matrix.shape)


def solution(mesh):
    specs = P(None, "row", None, None, "col", None)
    return jax.shard_map(
        per_device, mesh=mesh, in_specs=(specs,), out_specs=specs, check_vma=False
    )
```

```python
import functools

import jax
import jax.numpy as jnp
from jax import lax
from jax.experimental import pallas as pl
from jax.experimental.pallas import tpu as pltpu
from jax.sharding import PartitionSpec as P

F32 = jnp.float32
MESH = pl.DeviceIdType.MESH
HIGHEST = lax.Precision.HIGHEST
NB = 128
LOOK = 2
CHUNK = 64
CHUNKS = 512 // CHUNK
EARLY = (0, 6, 4, 2, 0, 0, 0, 1)
MID = (0, 8, 8, 8, 6, 0, 2, 4)


def dot_nn(a, b):
    return jnp.dot(a, b, precision=HIGHEST, preferred_element_type=F32)


def dot_nt(a, b):
    return lax.dot_general(
        a, b, (((1,), (1,)), ((), ())), precision=HIGHEST, preferred_element_type=F32
    )


def row_splat(tile, k):
    return jnp.broadcast_to(tile[k : k + 1, :], (8, NB))


def lane_splat(tile, k):
    return jnp.broadcast_to(tile[:, k : k + 1], (8, NB))


def eliminate(rows, rows_identity, columns):
    sub = lax.broadcasted_iota(jnp.int32, (8, NB), 0)
    columns = list(columns)
    upper, inverse, solved = rows, rows_identity, rows_identity
    scale = jnp.ones((8, NB), F32)
    for k in range(8):
        pivot = row_splat(columns[k], k)
        over = 1.0 / pivot
        here = sub == k
        ratio = columns[k] * over
        below = jnp.where(sub > k, ratio, 0.0)
        for j in range(k + 1, 8):
            r = row_splat(columns[j], k)
            columns[j] = jnp.where(here, r * over, columns[j] - ratio * r)
        upper = upper - below * row_splat(upper, k)
        inverse = inverse - below * row_splat(inverse, k)
        r = row_splat(solved, k)
        solved = jnp.where(here, r * over, solved - ratio * r)
        scale = jnp.where(here, lax.rsqrt(pivot), scale)
    return upper * scale, inverse * scale, solved


def factor(work, solved_rows, upper, inverse):
    lane = lax.broadcasted_iota(jnp.int32, (8, NB), 1)
    sub = lax.broadcasted_iota(jnp.int32, (8, NB), 0)
    solved_rows[...] = jnp.zeros((NB, NB), F32)
    steps = NB // 8
    for t in range(steps):
        o = 8 * t
        rows = work[o : o + 8, :]
        columns = [lane_splat(rows, o + j) for j in range(8)]
        block = (lane >= o) & (lane < o + 8)
        rows_identity = jnp.where(block, (lane - o == sub).astype(F32), rows)
        up, inv, solved = eliminate(rows, rows_identity, columns)
        upper[o : o + 8, :] = jnp.where(lane >= o, up, 0.0)
        inverse[o : o + 8, :] = jnp.where(lane < o + 8, inv, 0.0)
        solved_rows[o : o + 8, :] = solved
        splats = [row_splat(solved, j) for j in range(8)]
        for i in range(t + 1, min(t + 1 + LOOK, steps)):
            tile = work[8 * i : 8 * i + 8, :]
            total = jnp.where(block, 0.0, tile)
            for j in range(8):
                total = total - lane_splat(tile, o + j) * splats[j]
            work[8 * i : 8 * i + 8, :] = total
        rest = 8 * (t + 1 + LOOK)
        if rest < NB:
            tiles = work[rest:, :]
            lanes = lax.broadcasted_iota(jnp.int32, (NB - rest, NB), 1)
            own = (lanes >= o) & (lanes < o + 8)
            work[rest:, :] = jnp.where(own, 0.0, tiles) - dot_nn(
                jnp.where(own, tiles, 0.0), solved_rows[...]
            )


def gather_kernel(
    n,
    x_hbm,
    pr,
    pc,
    diag,
    xv,
    panel,
    lead,
    rbuf,
    cbuf,
    wbuf,
    wown,
    ac,
    work,
    solved_rows,
    upper,
    inverse,
    w10,
    handed,
    load_sem,
    lead_recv,
    lead_send,
    diag_recv,
    diag_send,
    go_plane,
    go_line,
    go_down,
    hand_recv,
    hand_send,
    hand_rows,
    hand_line,
    r_piece,
    r_gather,
    r_send_a,
    r_send_b,
    c_recv,
    c_send,
    c_pair,
    c_pair_send,
    w_piece,
    w_gather,
    w_send_a,
    w_send_b,
    w_send_c,
    w_pair,
    w_pair_send,
):
    r = lax.axis_index("row")
    c = lax.axis_index("col")
    z = r // 2
    x = c // 4
    core = lax.rem(r, 2)
    pair = r + 1 - 2 * core
    both, either, no = jnp.logical_and, jnp.logical_or, jnp.logical_not
    left = c < 2
    corner = both(r == 0, c == 0)
    last = both(r == 1, c == 1)

    def span(first, end, body):
        def step(k, carry):
            body(k)
            return carry

        lax.fori_loop(first, end, step, 0)

    def each(body):
        span(1, n, body)

    def other(me, k):
        return lax.rem(me + k, n)

    def copy(src, dst, send, recv, row, col):
        return pltpu.make_async_remote_copy(
            src_ref=src,
            dst_ref=dst,
            send_sem=send,
            recv_sem=recv,
            device_id=(row, col),
            device_id_type=MESH,
        )

    def signal(sem, row, col):
        pl.semaphore_signal(sem, inc=1, device_id=(row, col), device_id_type=MESH)

    def arrive(buffer, sem):
        pltpu.make_async_copy(buffer, buffer, sem).wait()

    hub = both(r == 1, c == 0)
    barrier = pltpu.get_barrier_semaphore()
    door = jnp.where(left, 2, 12)
    before = jnp.where(z < 5, r - 2, jnp.where(z < 7, r + 2, door + core))
    signal(barrier, pair, c)

    @pl.when(z > 0)
    def _():
        signal(barrier, before, c)

    @pl.when(z != 4)
    def _():
        signal(barrier, 8, c)

    @pl.when(either(hub, both(z == 0, c != 0)))
    def _():
        signal(barrier, door + core, c)

    @pl.when(hub)
    def _():
        signal(barrier, door, c)

    for k in range(2):

        @pl.when(c != k)
        def _():
            signal(barrier, jnp.where(z > 0, r, 0), k)

    @pl.when(corner)
    def _():
        signal(barrier, 1, 1)

    top = pltpu.make_async_copy(x_hbm.at[pl.ds(0, 512)], xv.at[pl.ds(0, 512)], load_sem.at[0])
    below = pltpu.make_async_copy(
        x_hbm.at[pl.ds(512, 1536)], xv.at[pl.ds(512, 1536)], load_sem.at[1]
    )
    top.start()
    below.start()
    top.wait()

    @pl.when(left)
    def _():
        panel[0:NB, :] = xv[pl.ds(0, NB, stride=4), :]

    def load_rest():
        below.wait()

        @pl.when(left)
        def _():
            panel[NB:, :] = xv[pl.ds(512, 384, stride=4), :]

    def enter():
        after = jnp.where(either(z == 4, z == 5), 0, 1)
        heard = (
            1
            + after
            + jnp.where(z == door // 2, 2, 0)
            + jnp.where(r == 8, n - 2, 0)
            + jnp.where(both(z > 0, left), n - 1, 0)
            + jnp.where(both(r == 0, left), 2 * (n - 1), 0)
            + jnp.where(last, 1, 0)
        )
        pl.semaphore_wait(barrier, heard)

    def to_corner(b):
        return copy(panel.at[pl.ds(0, NB)], lead.at[b], lead_send, lead_recv.at[b], 0, 0)

    def r_scatter(k):
        p = other(c, k)
        return copy(
            panel.at[pl.ds(pl.multiple_of(p * 32, 32), 32)],
            rbuf.at[p, c],
            r_send_a,
            r_piece.at[c],
            r,
            p,
        )

    def r_across(k):
        p = other(c, k)
        return copy(rbuf.at[c], rbuf.at[c], r_send_b, r_gather, r, p)

    def plane_scatter():
        each(lambda k: r_scatter(lax.rem(k + n // 2 - 2, n - 1) + 1).start())
        rbuf[c, c] = panel[pl.ds(pl.multiple_of(c * 32, 32), 32), :]

    def r_batch(first):
        def send(k):
            p = other(c, k)
            early = either(p < 4, p >= 12)

            @pl.when(early if first else no(early))
            def _():
                r_across(k).start()

        each(send)

    def plane_gather():
        @pl.when(c != 0)
        def _():
            arrive(rbuf.at[c, 0], r_piece.at[0])

        @pl.when(c != 1)
        def _():
            arrive(rbuf.at[c, 1], r_piece.at[1])

        r_batch(True)

        @pl.when(core == 0)
        def _():
            r_batch(False)

    def chunk(k):
        return cbuf.at[core, pl.ds(pl.multiple_of(k * CHUNK, CHUNK), CHUNK)]

    def first_chunk(k):
        return xv.at[pl.ds(pl.multiple_of(k * CHUNK, CHUNK), CHUNK)]

    def c_next(k, way, src):
        there = lax.rem(r + 2 + way * (n - 4), n)
        return copy(src, chunk(k), c_send.at[way], c_recv.at[k], there, c)

    def c_beside(k, src):
        return copy(src, chunk(k), c_pair_send, c_pair, pair, c)

    def line_up(k):
        c_next(k, 0, first_chunk(k)).start()
        c_beside(k, first_chunk(k)).start()

    def line_down(k):
        c_next(k, 1, first_chunk(k)).start()

    up = both(z >= 1, z <= 3)
    down = z >= 6

    def line_relay(k):
        arrive(chunk(k), c_recv.at[k])

        @pl.when(up)
        def _():
            c_next(k, 0, chunk(k)).start()

        @pl.when(down)
        def _():
            c_next(k, 1, chunk(k)).start()

        c_beside(k, chunk(k)).start()

    def w_copy(send, recv, row, col):
        return copy(wbuf.at[c], wbuf.at[c], send, recv, row, col)

    def w_scatter(p):
        return copy(wown.at[p], wbuf.at[p], w_send_a, w_piece, 1, p)

    def w_down(k):
        p = lax.rem(r + 2 * k, n)
        return w_copy(w_send_b, w_piece, p, c)

    def w_across(k):
        p = other(c, k)
        return w_copy(w_send_c, w_gather.at[c // 4], r, p)

    def diagonal():
        return copy(upper.at[1], diag, diag_send, diag_recv, 1, 1)

    def w_beside(g):
        part = wbuf.at[pl.ds(4 * g, 4)]
        return copy(part, part, w_pair_send, w_pair, pair, c)

    def pass_w():
        arrive(wbuf.at[c], w_piece)

        @pl.when(r == 1)
        def _():
            pl.semaphore_wait(go_line, 1)
            span(1, n // 2, lambda k: w_down(k).start())

        for near in (True, False):

            def send(k):
                @pl.when((other(c, k) < 4) == near)
                def _():
                    w_across(k).start()

            each(send)

        r_batch(False)

    def hand(b):
        src = panel if b == 0 else xv.at[pl.ds(0, 512)]
        dst = handed if b == 0 else cbuf.at[0]
        return copy(src, dst, hand_send.at[b], hand_recv.at[b], 1, 0)

    def hand_scatter(p):
        return copy(
            handed.at[pl.ds(pl.multiple_of(p * 32, 32), 32)],
            rbuf.at[p, 0],
            hand_rows,
            r_piece.at[0],
            0,
            p,
        )

    def hand_next(k, way):
        at = cbuf.at[0, pl.ds(pl.multiple_of(k * CHUNK, CHUNK), CHUNK)]
        return copy(at, at, hand_line.at[way], c_recv.at[k], 2 + way * (n - 4), 0)

    def middle():
        load_rest()
        arrive(lead.at[0], lead_recv.at[0])
        hand(0).start()
        hand(1).start()
        w0 = inverse[0]
        l10 = dot_nt(lead[0], w0)
        w10[...] = dot_nn(l10, w0)
        arrive(lead.at[1], lead_recv.at[1])
        work[...] = lead[1] - dot_nt(l10, l10)
        enter()
        signal(go_plane, 1, 0)

    @pl.when(no(corner))
    def _():
        enter()

        @pl.when(hub)
        def _():
            to_corner(0).start()

        @pl.when(last)
        def _():
            to_corner(1).start()

        @pl.when(r == 8)
        def _():
            signal(go_line, 1, c)

        @pl.when(z == door // 2)
        def _():
            signal(go_down, jnp.where(c == 0, 1, core), c)

        @pl.when(both(r == 0, c == 1))
        def _():
            signal(go_plane, 1, 1)

        @pl.when(z == 0)
        def _():
            span(0, CHUNKS, line_up)

        load_rest()

        @pl.when(both(r == 1, left))
        def _():
            pl.semaphore_wait(go_plane, 1)

        @pl.when(left)
        def _():
            plane_scatter()

        @pl.when(hub)
        def _():
            arrive(handed, hand_recv.at[0])
            each(lambda p: hand_scatter(p).start())
            arrive(cbuf.at[0], hand_recv.at[1])
            span(0, CHUNKS, lambda k: hand_next(k, 0).start())
            pl.semaphore_wait(go_down, 2)
            span(0, CHUNKS, lambda k: hand_next(k, 1).start())

        @pl.when(z == 0)
        def _():
            @pl.when(no(hub))
            def _():
                pl.semaphore_wait(go_down, 1)

            span(0, CHUNKS, line_down)

        def by_plane(counts):
            value = counts[0]
            for k in range(1, 8):
                value = jnp.where(z == k, counts[k], value)
            return value

        early = by_plane(EARLY)
        mid = by_plane(MID)

        @pl.when(z > 0)
        def _():
            span(0, early, line_relay)

        plane_gather()

        @pl.when(z > 0)
        def _():
            span(early, mid, line_relay)

        @pl.when(core == 1)
        def _():
            pass_w()

        @pl.when(z > 0)
        def _():
            span(mid, CHUNKS, line_relay)

        @pl.when(core == 1)
        def _():
            for g in range(4):
                @pl.when(x == g)
                def _():
                    arrive(wbuf.at[pl.ds(4 * g, 3)], w_gather.at[g])

                @pl.when(x != g)
                def _():
                    arrive(wbuf.at[pl.ds(4 * g, 4)], w_gather.at[g])

                w_beside(g).start()

    @pl.when(corner)
    def _():
        work[...] = panel[0:NB, :]

        def block(b, carry):
            factor(work, solved_rows, upper.at[b], inverse.at[b])

            @pl.when(b == 0)
            def _():
                middle()

            return carry

        lax.fori_loop(0, 2, block, 0)
        wown[:, 0] = inverse[0].reshape(n, 8, NB)
        wown[:, 1] = -dot_nn(inverse[1], w10[...]).reshape(n, 8, NB)
        wown[:, 2] = inverse[1].reshape(n, 8, NB)
        for p in range(n):
            w_scatter((p + n // 2) % n).start()
        diagonal().start()
        rbuf[0, 0] = panel[0:32, :]
        plane_gather()
        diag[...] = upper[0]

    @pl.when(z == 0)
    def _():
        cbuf[core] = xv[0:512, :]

    @pl.when(no(hub))
    def _():
        arrive(cbuf.at[1 - core], c_pair)

    for h in range(2):
        for b in range(4):
            ac[h * NB : (h + 1) * NB, b * NB : (b + 1) * NB] = cbuf[h, pl.ds(b, NB, stride=4), :]

    @pl.when(core == 0)
    def _():
        arrive(wbuf, w_pair)

    w00 = wbuf[:, 0].reshape(NB, NB)
    w01 = wbuf[:, 1].reshape(NB, NB)
    w11 = wbuf[:, 2].reshape(NB, NB)
    lower = jnp.concatenate(
        [
            jnp.concatenate([w00, jnp.zeros((NB, NB), F32)], axis=1),
            jnp.concatenate([w01, w11], axis=1),
        ],
        axis=0,
    )
    pc[...] = dot_nn(lower, ac[...])
    arrive(rbuf.at[pl.ds(0, n - 1)], r_gather)
    r0 = rbuf[:, 0].reshape(4 * NB, NB)
    r1 = rbuf[:, 1].reshape(4 * NB, NB)
    pr[...] = dot_nt(jnp.concatenate([r0, r1], axis=1), lower)

    @pl.when(last)
    def _():
        arrive(diag, diag_recv)

    most = n - 1

    @pl.when(corner)
    def _():
        arrive(wown, w_send_a)
        diagonal().wait_send()
        hand(0).wait_send()
        hand(1).wait_send()

    @pl.when(hub)
    def _():
        to_corner(0).wait_send()
        arrive(handed.at[pl.ds(0, 32 * most)], hand_rows)
        arrive(cbuf.at[0], hand_line.at[0])
        arrive(cbuf.at[0], hand_line.at[1])

    @pl.when(last)
    def _():
        to_corner(1).wait_send()

    @pl.when(both(left, no(corner)))
    def _():
        arrive(panel.at[pl.ds(0, 32 * most)], r_send_a)

    @pl.when(r == 1)
    def _():
        arrive(wbuf.at[pl.ds(0, n // 2 - 1)], w_send_b)

    @pl.when(either(both(z == 0, no(corner)), up))
    def _():
        arrive(cbuf.at[core], c_send.at[0])

    @pl.when(either(both(z == 0, no(corner)), down))
    def _():
        arrive(cbuf.at[core], c_send.at[1])

    @pl.when(no(corner))
    def _():
        arrive(cbuf.at[core], c_pair_send)

    arrive(rbuf.at[pl.ds(0, most)], r_send_b)

    @pl.when(core == 1)
    def _():
        arrive(wbuf.at[pl.ds(0, most)], w_send_c)
        arrive(wbuf, w_pair_send)


def update_kernel(x, pr, pc, diag, out, parts, sems):
    r = lax.axis_index("row")
    c = lax.axis_index("col")
    both = jnp.logical_and

    def store(a):
        return pltpu.make_async_copy(parts.at[a], out.at[pl.ds(a * 512, 512)], sems.at[a])

    for a in range(4):
        at = slice(a * NB, (a + 1) * NB)

        def put(b, value):
            parts[a, pl.ds(b, NB, stride=4), :] = value

        def update():
            delta = dot_nn(pr[at, :], pc[...])
            for b in range(4):
                put(b, x[pl.ds(a * 512 + b, NB, stride=4), :] - delta[:, b * NB : (b + 1) * NB])

            @pl.when(c == 0)
            def _():
                put(0, pr[at, 0:NB])

            @pl.when(c == 1)
            def _():
                put(0, pr[at, NB:])

        if a > 0:
            update()
        else:

            @pl.when(r < 2)
            def _():
                parts[0] = jnp.zeros((512, NB), F32)

                @pl.when(both(r == 1, c == 0))
                def _():
                    put(0, pr[at, 0:NB])

                @pl.when(both(r == c, c < 2))
                def _():
                    put(0, diag[...].T)

            @pl.when(r >= 2)
            def _():
                update()

        store(a).start()

    for a in range(4):
        store(a).wait()


def per_device(matrix):
    n = lax.axis_size("row")
    flat = matrix.reshape(2048, NB)
    dma = pltpu.SemaphoreType.DMA
    square = pltpu.VMEM((NB, NB), F32)
    whole = pl.BlockSpec(memory_space=pltpu.VMEM)
    flat = pltpu.with_memory_space_constraint(flat, pltpu.HBM)
    pr, pc, diag, x = pl.pallas_call(
        functools.partial(gather_kernel, n),
        out_shape=[
            pltpu.VMEM((4 * NB, 2 * NB), F32),
            pltpu.VMEM((2 * NB, 4 * NB), F32),
            square,
            pltpu.VMEM((2048, NB), F32),
        ],
        in_specs=[pl.BlockSpec(memory_space=pl.ANY)],
        out_specs=[whole] * 4,
        scratch_shapes=[
            pltpu.VMEM((512, NB), F32),
            pltpu.VMEM((2, NB, NB), F32),
            pltpu.VMEM((n, 2, 32, NB), F32),
            pltpu.VMEM((2, 512, NB), F32),
            pltpu.VMEM((n, 3, 8, NB), F32),
            pltpu.VMEM((n, 3, 8, NB), F32),
            pltpu.VMEM((2 * NB, 4 * NB), F32),
            square,
            square,
            pltpu.VMEM((2, NB, NB), F32),
            pltpu.VMEM((2, NB, NB), F32),
            square,
            pltpu.VMEM((512, NB), F32),
            dma((2,)),
            dma((2,)),
            dma,
            dma,
            dma,
            pltpu.SemaphoreType.REGULAR,
            pltpu.SemaphoreType.REGULAR,
            pltpu.SemaphoreType.REGULAR,
            dma((2,)),
            dma((2,)),
            dma,
            dma((2,)),
            dma((2,)),
            dma,
            dma,
            dma,
            dma((CHUNKS,)),
            dma((2,)),
            dma,
            dma,
            dma,
            dma((4,)),
            dma,
            dma,
            dma,
            dma,
            dma,
        ],
        compiler_params=pltpu.CompilerParams(
            collective_id=0, has_side_effects=True, vmem_limit_bytes=24 * 1024 * 1024
        ),
    )(flat)
    out = pl.pallas_call(
        update_kernel,
        out_shape=pltpu.HBM((2048, NB), F32),
        in_specs=[whole] * 4,
        out_specs=pl.BlockSpec(memory_space=pltpu.HBM),
        scratch_shapes=[pltpu.VMEM((4, 512, NB), F32), dma((4,))],
        compiler_params=pltpu.CompilerParams(vmem_limit_bytes=24 * 1024 * 1024),
    )(x, pr, pc, diag)
    return out.reshape(matrix.shape)


def solution(mesh):
    specs = P(None, "row", None, None, "col", None)
    return jax.shard_map(
        per_device, mesh=mesh, in_specs=(specs,), out_specs=specs, check_vma=False
    )
```

```python
import functools

import jax
import jax.numpy as jnp
from jax import lax
from jax.experimental import pallas as pl
from jax.experimental.pallas import tpu as pltpu
from jax.sharding import PartitionSpec as P

F32 = jnp.float32
MESH = pl.DeviceIdType.MESH
HIGHEST = lax.Precision.HIGHEST
NB = 128
LOOK = 2
STARTS = (0, 128, 384, 512)
CHUNK = 64
CHUNKS = 512 // CHUNK
EARLY = (0, 6, 4, 2, 0, 0, 0, 1)
MID = (0, 8, 8, 8, 6, 0, 2, 4)
R_FIRST = (0, 3)
R_LATER = (1, 2)
W_ORDER = (0, 1, 2, 3)


def dot_nn(a, b):
    return jnp.dot(a, b, precision=HIGHEST, preferred_element_type=F32)


def dot_nt(a, b):
    return lax.dot_general(
        a, b, (((1,), (1,)), ((), ())), precision=HIGHEST, preferred_element_type=F32
    )


def row_splat(tile, k):
    return jnp.broadcast_to(tile[k : k + 1, :], (8, NB))


def lane_splat(tile, k):
    return jnp.broadcast_to(tile[:, k : k + 1], (8, NB))


def eliminate(rows, rows_identity, columns):
    sub = lax.broadcasted_iota(jnp.int32, (8, NB), 0)
    columns = list(columns)
    upper, inverse, solved = rows, rows_identity, rows_identity
    scale = jnp.ones((8, NB), F32)
    for k in range(8):
        pivot = row_splat(columns[k], k)
        over = 1.0 / pivot
        here = sub == k
        ratio = columns[k] * over
        below = jnp.where(sub > k, ratio, 0.0)
        for j in range(k + 1, 8):
            r = row_splat(columns[j], k)
            columns[j] = jnp.where(here, r * over, columns[j] - ratio * r)
        upper = upper - below * row_splat(upper, k)
        inverse = inverse - below * row_splat(inverse, k)
        r = row_splat(solved, k)
        solved = jnp.where(here, r * over, solved - ratio * r)
        scale = jnp.where(here, lax.rsqrt(pivot), scale)
    return upper * scale, inverse * scale, solved


def factor(work, solved_rows, upper, inverse):
    lane = lax.broadcasted_iota(jnp.int32, (8, NB), 1)
    sub = lax.broadcasted_iota(jnp.int32, (8, NB), 0)
    solved_rows[...] = jnp.zeros((NB, NB), F32)
    steps = NB // 8
    for t in range(steps):
        o = 8 * t
        rows = work[o : o + 8, :]
        columns = [lane_splat(rows, o + j) for j in range(8)]
        block = (lane >= o) & (lane < o + 8)
        rows_identity = jnp.where(block, (lane - o == sub).astype(F32), rows)
        up, inv, solved = eliminate(rows, rows_identity, columns)
        upper[o : o + 8, :] = jnp.where(lane >= o, up, 0.0)
        inverse[o : o + 8, :] = jnp.where(lane < o + 8, inv, 0.0)
        solved_rows[o : o + 8, :] = solved
        splats = [row_splat(solved, j) for j in range(8)]
        for i in range(t + 1, min(t + 1 + LOOK, steps)):
            tile = work[8 * i : 8 * i + 8, :]
            total = jnp.where(block, 0.0, tile)
            for j in range(8):
                total = total - lane_splat(tile, o + j) * splats[j]
            work[8 * i : 8 * i + 8, :] = total
        rest = 8 * (t + 1 + LOOK)
        if rest < NB:
            tiles = work[rest:, :]
            lanes = lax.broadcasted_iota(jnp.int32, (NB - rest, NB), 1)
            own = (lanes >= o) & (lanes < o + 8)
            work[rest:, :] = jnp.where(own, 0.0, tiles) - dot_nn(
                jnp.where(own, tiles, 0.0), solved_rows[...]
            )


def gather_kernel(
    n,
    x_hbm,
    pr,
    pc,
    diag,
    xv,
    panel,
    lead,
    rbuf,
    cbuf,
    wbuf,
    wown,
    ac,
    work,
    solved_rows,
    upper,
    inverse,
    w10,
    handed,
    load_sem,
    lead_recv,
    lead_send,
    diag_recv,
    diag_send,
    go_plane,
    go_line,
    go_down,
    hand_recv,
    hand_send,
    hand_rows,
    hand_line,
    r_piece,
    r_gather,
    r_send_a,
    r_send_b,
    c_recv,
    c_send,
    c_pair,
    c_pair_send,
    w_piece,
    w_gather,
    w_send_a,
    w_send_b,
    w_send_c,
    w_pair,
    w_pair_send,
):
    r = lax.axis_index("row")
    c = lax.axis_index("col")
    z = r // 2
    x = c // 4
    y = lax.rem(c, 4)
    ys = [lax.rem(y + j, 4) for j in range(4)]
    core = lax.rem(r, 2)
    pair = r + 1 - 2 * core
    both, either, no = jnp.logical_and, jnp.logical_or, jnp.logical_not
    left = c < 2
    corner = both(r == 0, c == 0)
    last = both(r == 1, c == 1)

    def span(first, end, body):
        def step(k, carry):
            body(k)
            return carry

        lax.fori_loop(first, end, step, 0)

    def each(body):
        span(1, n, body)

    def other(me, k):
        return lax.rem(me + k, n)

    def copy(src, dst, send, recv, row, col):
        return pltpu.make_async_remote_copy(
            src_ref=src,
            dst_ref=dst,
            send_sem=send,
            recv_sem=recv,
            device_id=(row, col),
            device_id_type=MESH,
        )

    def signal(sem, row, col):
        pl.semaphore_signal(sem, inc=1, device_id=(row, col), device_id_type=MESH)

    def arrive(buffer, sem):
        pltpu.make_async_copy(buffer, buffer, sem).wait()

    top = pltpu.make_async_copy(x_hbm.at[pl.ds(0, 512)], xv.at[pl.ds(0, 512)], load_sem.at[0])
    below = pltpu.make_async_copy(
        x_hbm.at[pl.ds(512, 1536)], xv.at[pl.ds(512, 1536)], load_sem.at[1]
    )
    top.start()
    below.start()

    hub = both(r == 1, c == 0)
    barrier = pltpu.get_barrier_semaphore()
    door = jnp.where(left, 2, 12)
    before = jnp.where(z < 5, r - 2, jnp.where(z < 7, r + 2, door + core))
    signal(barrier, pair, c)

    @pl.when(z > 0)
    def _():
        signal(barrier, before, c)

    @pl.when(z != 4)
    def _():
        signal(barrier, 8, c)

    @pl.when(either(hub, both(z == 0, c != 0)))
    def _():
        signal(barrier, door + core, c)

    @pl.when(hub)
    def _():
        signal(barrier, door, c)

    for k in range(2):

        @pl.when(c != k)
        def _():
            signal(barrier, jnp.where(z > 0, r, 0), k)

    @pl.when(corner)
    def _():
        signal(barrier, 1, 1)

    top.wait()

    @pl.when(left)
    def _():
        panel[0:NB, :] = xv[pl.ds(0, NB, stride=4), :]

    def load_rest():
        below.wait()

        @pl.when(left)
        def _():
            panel[NB:, :] = xv[pl.ds(512, 384, stride=4), :]

    def enter():
        after = jnp.where(either(z == 4, z == 5), 0, 1)
        heard = (
            1
            + after
            + jnp.where(z == door // 2, 2, 0)
            + jnp.where(r == 8, n - 2, 0)
            + jnp.where(both(z > 0, left), n - 1, 0)
            + jnp.where(both(r == 0, left), 2 * (n - 1), 0)
            + jnp.where(last, 1, 0)
        )
        pl.semaphore_wait(barrier, heard)

    def to_corner(b):
        return copy(panel.at[pl.ds(0, NB)], lead.at[b], lead_send, lead_recv.at[b], 0, 0)

    def r_scatter(p):
        return copy(
            panel.at[pl.ds(p * 32, 32)],
            rbuf.at[p, c],
            r_send_a,
            r_piece.at[c],
            r,
            p,
        )

    def r_across(p):
        return copy(rbuf.at[c], rbuf.at[c], r_send_b, r_gather, r, p)

    def plane_scatter():
        for p in (*range(n // 2, n), *range(2, n // 2)):
            r_scatter(p).start()
        for p in range(2):

            @pl.when(c != p)
            def _():
                r_scatter(p).start()

        rbuf[c, c] = panel[pl.ds(pl.multiple_of(c * 32, 32), 32), :]

    def columns(make, xs):
        for there in xs:
            for j in (2, 1, 3, 0):
                p = 4 * there + ys[j]

                @pl.when(p != c)
                def _():
                    make(p).start()

    def r_batch(first):
        def send(k):
            p = other(c, k)
            early = either(p < 4, p >= 12)

            @pl.when(early if first else no(early))
            def _():
                r_across(p).start()

        each(send)

    def plane_gather():
        @pl.when(c != 0)
        def _():
            arrive(rbuf.at[c, 0], r_piece.at[0])

        @pl.when(c != 1)
        def _():
            arrive(rbuf.at[c, 1], r_piece.at[1])

        r_batch(True)

        @pl.when(core == 0)
        def _():
            r_batch(False)

    def chunk(k):
        return cbuf.at[core, pl.ds(pl.multiple_of(k * CHUNK, CHUNK), CHUNK)]

    def first_chunk(k):
        return xv.at[pl.ds(pl.multiple_of(k * CHUNK, CHUNK), CHUNK)]

    def c_next(k, way, src):
        there = lax.rem(r + 2 + way * (n - 4), n)
        return copy(src, chunk(k), c_send.at[way], c_recv.at[k], there, c)

    def c_beside(k, src):
        return copy(src, chunk(k), c_pair_send, c_pair, pair, c)

    def line_up(k):
        c_next(k, 0, first_chunk(k)).start()
        c_beside(k, first_chunk(k)).start()

    def line_down(k):
        c_next(k, 1, first_chunk(k)).start()

    up = both(z >= 1, z <= 3)
    down = z >= 6

    def line_relay(k):
        arrive(chunk(k), c_recv.at[k])

        @pl.when(up)
        def _():
            c_next(k, 0, chunk(k)).start()

        @pl.when(down)
        def _():
            c_next(k, 1, chunk(k)).start()

        c_beside(k, chunk(k)).start()

    def w_copy(send, recv, row, col):
        return copy(wbuf.at[c], wbuf.at[c], send, recv, row, col)

    def w_scatter(p):
        return copy(wown.at[p], wbuf.at[p], w_send_a, w_piece, 1, p)

    def w_down(k):
        p = lax.rem(r + 2 * k, n)
        return w_copy(w_send_b, w_piece, p, c)

    def w_across(p):
        return w_copy(w_send_c, w_gather.at[c // 4], r, p)

    def diagonal():
        return copy(upper.at[1], diag, diag_send, diag_recv, 1, 1)

    def w_beside(g):
        part = wbuf.at[pl.ds(4 * g, 4)]
        return copy(part, part, w_pair_send, w_pair, pair, c)

    def pass_w():
        arrive(wbuf.at[c], w_piece)

        @pl.when(r == 1)
        def _():
            pl.semaphore_wait(go_line, 1)
            for k in range(1, n // 2):
                w_down(k).start()

        columns(w_across, W_ORDER)
        r_batch(False)

    def hand(b):
        src = panel if b == 0 else xv.at[pl.ds(0, 512)]
        dst = handed if b == 0 else cbuf.at[0]
        return copy(src, dst, hand_send.at[b], hand_recv.at[b], 1, 0)

    def hand_scatter(p):
        return copy(
            handed.at[pl.ds(p * 32, 32)],
            rbuf.at[p, 0],
            hand_rows,
            r_piece.at[0],
            0,
            p,
        )

    def hand_next(k, way):
        at = cbuf.at[0, pl.ds(pl.multiple_of(k * CHUNK, CHUNK), CHUNK)]
        return copy(at, at, hand_line.at[way], c_recv.at[k], 2 + way * (n - 4), 0)

    def middle():
        load_rest()
        arrive(lead.at[0], lead_recv.at[0])
        hand(0).start()
        hand(1).start()
        w0 = inverse[0]
        l10 = dot_nt(lead[0], w0)
        w10[...] = dot_nn(l10, w0)
        arrive(lead.at[1], lead_recv.at[1])
        work[...] = lead[1] - dot_nt(l10, l10)
        enter()
        signal(go_plane, 1, 0)

    @pl.when(no(corner))
    def _():
        enter()

        @pl.when(hub)
        def _():
            to_corner(0).start()

        @pl.when(last)
        def _():
            to_corner(1).start()

        @pl.when(r == 8)
        def _():
            signal(go_line, 1, c)

        @pl.when(z == door // 2)
        def _():
            signal(go_down, jnp.where(c == 0, 1, core), c)

        @pl.when(both(r == 0, c == 1))
        def _():
            signal(go_plane, 1, 1)

        @pl.when(z == 0)
        def _():
            span(0, CHUNKS, line_up)

        load_rest()

        @pl.when(both(r == 1, left))
        def _():
            pl.semaphore_wait(go_plane, 1)

        @pl.when(left)
        def _():
            plane_scatter()

        @pl.when(hub)
        def _():
            arrive(handed, hand_recv.at[0])
            for p in (*range(n // 2, n), *range(1, n // 2)):
                hand_scatter(p).start()
            arrive(cbuf.at[0], hand_recv.at[1])
            span(0, CHUNKS, lambda k: hand_next(k, 0).start())
            pl.semaphore_wait(go_down, 2)
            span(0, CHUNKS, lambda k: hand_next(k, 1).start())

        @pl.when(z == 0)
        def _():
            @pl.when(no(hub))
            def _():
                pl.semaphore_wait(go_down, 1)

            span(0, CHUNKS, line_down)

        def by_plane(counts):
            value = counts[0]
            for k in range(1, 8):
                value = jnp.where(z == k, counts[k], value)
            return value

        early = by_plane(EARLY)
        mid = by_plane(MID)

        @pl.when(z > 0)
        def _():
            span(0, early, line_relay)

        plane_gather()

        @pl.when(z > 0)
        def _():
            span(early, mid, line_relay)

        @pl.when(core == 1)
        def _():
            pass_w()

        @pl.when(z > 0)
        def _():
            span(mid, CHUNKS, line_relay)

        @pl.when(core == 1)
        def _():
            for g in range(4):
                @pl.when(x == g)
                def _():
                    arrive(wbuf.at[pl.ds(4 * g, 3)], w_gather.at[g])

                @pl.when(x != g)
                def _():
                    arrive(wbuf.at[pl.ds(4 * g, 4)], w_gather.at[g])

                w_beside(g).start()

    @pl.when(corner)
    def _():
        work[...] = panel[0:NB, :]

        def block(b, carry):
            factor(work, solved_rows, upper.at[b], inverse.at[b])

            @pl.when(b == 0)
            def _():
                middle()

            return carry

        lax.fori_loop(0, 2, block, 0)
        wown[:, 0] = inverse[0].reshape(n, 8, NB)
        wown[:, 1] = -dot_nn(inverse[1], w10[...]).reshape(n, 8, NB)
        wown[:, 2] = inverse[1].reshape(n, 8, NB)
        for p in range(n):
            w_scatter((p + n // 2) % n).start()
        diagonal().start()
        rbuf[0, 0] = panel[0:32, :]
        plane_gather()
        diag[...] = upper[0]

    @pl.when(z == 0)
    def _():
        cbuf[core] = xv[0:512, :]

    @pl.when(no(hub))
    def _():
        arrive(cbuf.at[1 - core], c_pair)

    for h in range(2):
        for b in range(4):
            ac[h * NB : (h + 1) * NB, b * NB : (b + 1) * NB] = cbuf[h, pl.ds(b, NB, stride=4), :]

    most = n - 1

    @pl.when(hub)
    def _():
        to_corner(0).wait_send()
        arrive(handed.at[pl.ds(0, 32 * most)], hand_rows)
        arrive(cbuf.at[0], hand_line.at[0])
        arrive(cbuf.at[0], hand_line.at[1])

    @pl.when(last)
    def _():
        to_corner(1).wait_send()

    @pl.when(both(left, no(corner)))
    def _():
        arrive(panel.at[pl.ds(0, 32 * most)], r_send_a)

    @pl.when(r == 1)
    def _():
        arrive(wbuf.at[pl.ds(0, n // 2 - 1)], w_send_b)

    @pl.when(either(both(z == 0, no(corner)), up))
    def _():
        arrive(cbuf.at[core], c_send.at[0])

    @pl.when(either(both(z == 0, no(corner)), down))
    def _():
        arrive(cbuf.at[core], c_send.at[1])

    @pl.when(no(corner))
    def _():
        arrive(cbuf.at[core], c_pair_send)

    @pl.when(core == 0)
    def _():
        arrive(wbuf, w_pair)

    w00 = wbuf[:, 0].reshape(NB, NB)
    w01 = wbuf[:, 1].reshape(NB, NB)
    w11 = wbuf[:, 2].reshape(NB, NB)
    lower = jnp.concatenate(
        [
            jnp.concatenate([w00, jnp.zeros((NB, NB), F32)], axis=1),
            jnp.concatenate([w01, w11], axis=1),
        ],
        axis=0,
    )
    pc[...] = dot_nn(lower, ac[...])
    arrive(rbuf.at[pl.ds(0, n - 1)], r_gather)
    r0 = rbuf[:, 0].reshape(4 * NB, NB)
    r1 = rbuf[:, 1].reshape(4 * NB, NB)
    pr[...] = dot_nt(jnp.concatenate([r0, r1], axis=1), lower)

    @pl.when(last)
    def _():
        arrive(diag, diag_recv)

    @pl.when(corner)
    def _():
        arrive(wown, w_send_a)
        diagonal().wait_send()
        hand(0).wait_send()
        hand(1).wait_send()

    arrive(rbuf.at[pl.ds(0, most)], r_send_b)

    @pl.when(core == 1)
    def _():
        arrive(wbuf.at[pl.ds(0, most)], w_send_c)
        arrive(wbuf, w_pair_send)


def update_kernel(x, pr, pc, diag, out, parts, sems):
    r = lax.axis_index("row")
    c = lax.axis_index("col")
    both = jnp.logical_and

    def store(a):
        whole = pl.ds(4 * STARTS[a], 4 * (STARTS[a + 1] - STARTS[a]))
        return pltpu.make_async_copy(parts.at[whole], out.at[whole], sems.at[a])

    for a in range(len(STARTS) - 1):
        at = slice(STARTS[a], STARTS[a + 1])
        count = STARTS[a + 1] - STARTS[a]

        def rows(b):
            return pl.ds(4 * STARTS[a] + b, count, stride=4)

        def put(b, value):
            parts[rows(b), :] = value

        def update():
            delta = dot_nn(pr[at, :], pc[...])
            for b in range(4):
                put(b, x[rows(b), :] - delta[:, b * NB : (b + 1) * NB])

            @pl.when(c == 0)
            def _():
                put(0, pr[at, 0:NB])

            @pl.when(c == 1)
            def _():
                put(0, pr[at, NB:])

        if a > 0:
            update()
        else:

            @pl.when(r < 2)
            def _():
                parts[0:512, :] = jnp.zeros((512, NB), F32)

                @pl.when(both(r == 1, c == 0))
                def _():
                    put(0, pr[at, 0:NB])

                @pl.when(both(r == c, c < 2))
                def _():
                    put(0, diag[...].T)

            @pl.when(r >= 2)
            def _():
                update()

        store(a).start()

    for a in range(len(STARTS) - 1):
        store(a).wait()


def per_device(matrix):
    n = lax.axis_size("row")
    flat = matrix.reshape(2048, NB)
    dma = pltpu.SemaphoreType.DMA
    square = pltpu.VMEM((NB, NB), F32)
    whole = pl.BlockSpec(memory_space=pltpu.VMEM)
    flat = pltpu.with_memory_space_constraint(flat, pltpu.HBM)
    pr, pc, diag, x = pl.pallas_call(
        functools.partial(gather_kernel, n),
        out_shape=[
            pltpu.VMEM((4 * NB, 2 * NB), F32),
            pltpu.VMEM((2 * NB, 4 * NB), F32),
            square,
            pltpu.VMEM((2048, NB), F32),
        ],
        in_specs=[pl.BlockSpec(memory_space=pl.ANY)],
        out_specs=[whole] * 4,
        scratch_shapes=[
            pltpu.VMEM((512, NB), F32),
            pltpu.VMEM((2, NB, NB), F32),
            pltpu.VMEM((n, 2, 32, NB), F32),
            pltpu.VMEM((2, 512, NB), F32),
            pltpu.VMEM((n, 3, 8, NB), F32),
            pltpu.VMEM((n, 3, 8, NB), F32),
            pltpu.VMEM((2 * NB, 4 * NB), F32),
            square,
            square,
            pltpu.VMEM((2, NB, NB), F32),
            pltpu.VMEM((2, NB, NB), F32),
            square,
            pltpu.VMEM((512, NB), F32),
            dma((2,)),
            dma((2,)),
            dma,
            dma,
            dma,
            pltpu.SemaphoreType.REGULAR,
            pltpu.SemaphoreType.REGULAR,
            pltpu.SemaphoreType.REGULAR,
            dma((2,)),
            dma((2,)),
            dma,
            dma((2,)),
            dma((2,)),
            dma,
            dma,
            dma,
            dma((CHUNKS,)),
            dma((2,)),
            dma,
            dma,
            dma,
            dma((4,)),
            dma,
            dma,
            dma,
            dma,
            dma,
        ],
        compiler_params=pltpu.CompilerParams(
            collective_id=0, has_side_effects=True, vmem_limit_bytes=24 * 1024 * 1024
        ),
    )(flat)
    out = pl.pallas_call(
        update_kernel,
        out_shape=pltpu.HBM((2048, NB), F32),
        in_specs=[whole] * 4,
        out_specs=pl.BlockSpec(memory_space=pltpu.HBM),
        scratch_shapes=[pltpu.VMEM((2048, NB), F32), dma((len(STARTS) - 1,))],
        compiler_params=pltpu.CompilerParams(vmem_limit_bytes=24 * 1024 * 1024),
    )(x, pr, pc, diag)
    return out.reshape(matrix.shape)


def solution(mesh):
    specs = P(None, "row", None, None, "col", None)
    return jax.shard_map(
        per_device, mesh=mesh, in_specs=(specs,), out_specs=specs, check_vma=False
    )
```

```python
import functools

import jax
import jax.numpy as jnp
from jax import lax
from jax.experimental import pallas as pl
from jax.experimental.pallas import tpu as pltpu
from jax.sharding import PartitionSpec as P

F32 = jnp.float32
MESH = pl.DeviceIdType.MESH
HIGHEST = lax.Precision.HIGHEST
NB = 128
LOOK = 2
STARTS = (0, 128, 512)
CHUNK = 64
CHUNKS = 512 // CHUNK
EARLY = (0, 6, 4, 2, 0, 0, 0, 1)
MID = (0, 8, 8, 8, 6, 0, 2, 4)
R_FIRST = (0, 3)
R_LATER = (1, 2)
W_ORDER = (0, 1, 2, 3)


def dot_nn(a, b):
    return jnp.dot(a, b, precision=HIGHEST, preferred_element_type=F32)


def dot_nt(a, b):
    return lax.dot_general(
        a, b, (((1,), (1,)), ((), ())), precision=HIGHEST, preferred_element_type=F32
    )


def row_splat(tile, k):
    return jnp.broadcast_to(tile[k : k + 1, :], (8, NB))


def lane_splat(tile, k):
    return jnp.broadcast_to(tile[:, k : k + 1], (8, NB))


def eliminate(rows, rows_identity, columns):
    sub = lax.broadcasted_iota(jnp.int32, (8, NB), 0)
    columns = list(columns)
    upper, inverse, solved = rows, rows_identity, rows_identity
    scale = jnp.ones((8, NB), F32)
    for k in range(8):
        pivot = row_splat(columns[k], k)
        over = 1.0 / pivot
        here = sub == k
        ratio = columns[k] * over
        below = jnp.where(sub > k, ratio, 0.0)
        for j in range(k + 1, 8):
            r = row_splat(columns[j], k)
            columns[j] = jnp.where(here, r * over, columns[j] - ratio * r)
        upper = upper - below * row_splat(upper, k)
        inverse = inverse - below * row_splat(inverse, k)
        r = row_splat(solved, k)
        solved = jnp.where(here, r * over, solved - ratio * r)
        scale = jnp.where(here, lax.rsqrt(pivot), scale)
    return upper * scale, inverse * scale, solved


def factor(work, solved_rows, upper, inverse):
    lane = lax.broadcasted_iota(jnp.int32, (8, NB), 1)
    sub = lax.broadcasted_iota(jnp.int32, (8, NB), 0)
    solved_rows[...] = jnp.zeros((NB, NB), F32)
    steps = NB // 8
    for t in range(steps):
        o = 8 * t
        rows = work[o : o + 8, :]
        columns = [lane_splat(rows, o + j) for j in range(8)]
        block = (lane >= o) & (lane < o + 8)
        rows_identity = jnp.where(block, (lane - o == sub).astype(F32), rows)
        up, inv, solved = eliminate(rows, rows_identity, columns)
        upper[o : o + 8, :] = jnp.where(lane >= o, up, 0.0)
        inverse[o : o + 8, :] = jnp.where(lane < o + 8, inv, 0.0)
        solved_rows[o : o + 8, :] = solved
        splats = [row_splat(solved, j) for j in range(8)]
        for i in range(t + 1, min(t + 1 + LOOK, steps)):
            tile = work[8 * i : 8 * i + 8, :]
            total = jnp.where(block, 0.0, tile)
            for j in range(8):
                total = total - lane_splat(tile, o + j) * splats[j]
            work[8 * i : 8 * i + 8, :] = total
        rest = 8 * (t + 1 + LOOK)
        if rest < NB:
            tiles = work[rest:, :]
            lanes = lax.broadcasted_iota(jnp.int32, (NB - rest, NB), 1)
            own = (lanes >= o) & (lanes < o + 8)
            work[rest:, :] = jnp.where(own, 0.0, tiles) - dot_nn(
                jnp.where(own, tiles, 0.0), solved_rows[...]
            )


def gather_kernel(
    n,
    x_hbm,
    pr,
    pc,
    diag,
    xv,
    panel,
    lead,
    rbuf,
    cbuf,
    wbuf,
    wown,
    ac,
    work,
    solved_rows,
    upper,
    inverse,
    w10,
    handed,
    load_sem,
    lead_recv,
    lead_send,
    diag_recv,
    diag_send,
    go_plane,
    go_line,
    go_down,
    hand_recv,
    hand_send,
    hand_rows,
    hand_line,
    r_piece,
    r_gather,
    r_send_a,
    r_send_b,
    c_recv,
    c_send,
    c_pair,
    c_pair_send,
    w_piece,
    w_gather,
    w_send_a,
    w_send_b,
    w_send_c,
    w_pair,
    w_pair_send,
):
    r = lax.axis_index("row")
    c = lax.axis_index("col")
    z = r // 2
    x = c // 4
    y = lax.rem(c, 4)
    ys = [lax.rem(y + j, 4) for j in range(4)]
    core = lax.rem(r, 2)
    pair = r + 1 - 2 * core
    both, either, no = jnp.logical_and, jnp.logical_or, jnp.logical_not
    left = c < 2
    corner = both(r == 0, c == 0)
    last = both(r == 1, c == 1)

    def span(first, end, body):
        def step(k, carry):
            body(k)
            return carry

        lax.fori_loop(first, end, step, 0)

    def each(body):
        span(1, n, body)

    def other(me, k):
        return lax.rem(me + k, n)

    def copy(src, dst, send, recv, row, col):
        return pltpu.make_async_remote_copy(
            src_ref=src,
            dst_ref=dst,
            send_sem=send,
            recv_sem=recv,
            device_id=(row, col),
            device_id_type=MESH,
        )

    def signal(sem, row, col):
        pl.semaphore_signal(sem, inc=1, device_id=(row, col), device_id_type=MESH)

    def arrive(buffer, sem):
        pltpu.make_async_copy(buffer, buffer, sem).wait()

    top = pltpu.make_async_copy(x_hbm.at[pl.ds(0, 512)], xv.at[pl.ds(0, 512)], load_sem.at[0])
    below = pltpu.make_async_copy(
        x_hbm.at[pl.ds(512, 1536)], xv.at[pl.ds(512, 1536)], load_sem.at[1]
    )
    top.start()
    below.start()

    hub = both(r == 1, c == 0)
    barrier = pltpu.get_barrier_semaphore()
    door = jnp.where(left, 2, 12)
    before = jnp.where(z < 5, r - 2, jnp.where(z < 7, r + 2, door + core))
    signal(barrier, pair, c)

    @pl.when(z > 0)
    def _():
        signal(barrier, before, c)

    @pl.when(z != 4)
    def _():
        signal(barrier, 8, c)

    @pl.when(either(hub, both(z == 0, c != 0)))
    def _():
        signal(barrier, door + core, c)

    @pl.when(hub)
    def _():
        signal(barrier, door, c)

    for k in range(2):

        @pl.when(c != k)
        def _():
            signal(barrier, jnp.where(z > 0, r, 0), k)

    @pl.when(corner)
    def _():
        signal(barrier, 1, 1)

    top.wait()

    @pl.when(left)
    def _():
        panel[0:NB, :] = xv[pl.ds(0, NB, stride=4), :]

    def load_rest():
        below.wait()

        @pl.when(left)
        def _():
            panel[NB:, :] = xv[pl.ds(512, 384, stride=4), :]

    def enter():
        after = jnp.where(either(z == 4, z == 5), 0, 1)
        heard = (
            1
            + after
            + jnp.where(z == door // 2, 2, 0)
            + jnp.where(r == 8, n - 2, 0)
            + jnp.where(both(z > 0, left), n - 1, 0)
            + jnp.where(both(r == 0, left), 2 * (n - 1), 0)
            + jnp.where(last, 1, 0)
        )
        pl.semaphore_wait(barrier, heard)

    def to_corner(b):
        return copy(panel.at[pl.ds(0, NB)], lead.at[b], lead_send, lead_recv.at[b], 0, 0)

    def r_scatter(p):
        return copy(
            panel.at[pl.ds(p * 32, 32)],
            rbuf.at[p, c],
            r_send_a,
            r_piece.at[c],
            r,
            p,
        )

    def r_across(p):
        return copy(rbuf.at[c], rbuf.at[c], r_send_b, r_gather, r, p)

    def plane_scatter():
        for p in (*range(n // 2, n), *range(2, n // 2)):
            r_scatter(p).start()
        for p in range(2):

            @pl.when(c != p)
            def _():
                r_scatter(p).start()

        rbuf[c, c] = panel[pl.ds(pl.multiple_of(c * 32, 32), 32), :]

    def columns(make, xs):
        for there in xs:
            for j in (2, 1, 3, 0):
                p = 4 * there + ys[j]

                @pl.when(p != c)
                def _():
                    make(p).start()

    def r_batch(first):
        def send(k):
            p = other(c, k)
            early = either(p < 4, p >= 12)

            @pl.when(early if first else no(early))
            def _():
                r_across(p).start()

        each(send)

    def plane_gather():
        @pl.when(c != 0)
        def _():
            arrive(rbuf.at[c, 0], r_piece.at[0])

        @pl.when(c != 1)
        def _():
            arrive(rbuf.at[c, 1], r_piece.at[1])

        r_batch(True)

        @pl.when(core == 0)
        def _():
            r_batch(False)

    def chunk(k):
        return cbuf.at[core, pl.ds(pl.multiple_of(k * CHUNK, CHUNK), CHUNK)]

    def first_chunk(k):
        return xv.at[pl.ds(pl.multiple_of(k * CHUNK, CHUNK), CHUNK)]

    def c_next(k, way, src):
        there = lax.rem(r + 2 + way * (n - 4), n)
        return copy(src, chunk(k), c_send.at[way], c_recv.at[k], there, c)

    def c_beside(k, src):
        return copy(src, chunk(k), c_pair_send, c_pair, pair, c)

    def line_up(k):
        c_next(k, 0, first_chunk(k)).start()
        c_beside(k, first_chunk(k)).start()

    def line_down(k):
        c_next(k, 1, first_chunk(k)).start()

    up = both(z >= 1, z <= 3)
    down = z >= 6

    def line_relay(k):
        arrive(chunk(k), c_recv.at[k])

        @pl.when(up)
        def _():
            c_next(k, 0, chunk(k)).start()

        @pl.when(down)
        def _():
            c_next(k, 1, chunk(k)).start()

        c_beside(k, chunk(k)).start()

    def w_copy(send, recv, row, col):
        return copy(wbuf.at[c], wbuf.at[c], send, recv, row, col)

    def w_scatter(p):
        return copy(wown.at[p], wbuf.at[p], w_send_a, w_piece, 1, p)

    def w_down(k):
        p = lax.rem(r + 2 * k, n)
        return w_copy(w_send_b, w_piece, p, c)

    def w_across(p):
        return w_copy(w_send_c, w_gather.at[c // 4], r, p)

    def diagonal():
        return copy(upper.at[1], diag, diag_send, diag_recv, 1, 1)

    def w_beside(g):
        part = wbuf.at[pl.ds(4 * g, 4)]
        return copy(part, part, w_pair_send, w_pair, pair, c)

    def pass_w():
        arrive(wbuf.at[c], w_piece)

        @pl.when(r == 1)
        def _():
            pl.semaphore_wait(go_line, 1)
            for k in range(1, n // 2):
                w_down(k).start()

        columns(w_across, W_ORDER)
        r_batch(False)

    def hand(b):
        src = panel if b == 0 else xv.at[pl.ds(0, 512)]
        dst = handed if b == 0 else cbuf.at[0]
        return copy(src, dst, hand_send.at[b], hand_recv.at[b], 1, 0)

    def hand_scatter(p):
        return copy(
            handed.at[pl.ds(p * 32, 32)],
            rbuf.at[p, 0],
            hand_rows,
            r_piece.at[0],
            0,
            p,
        )

    def hand_next(k, way):
        at = cbuf.at[0, pl.ds(pl.multiple_of(k * CHUNK, CHUNK), CHUNK)]
        return copy(at, at, hand_line.at[way], c_recv.at[k], 2 + way * (n - 4), 0)

    def middle():
        load_rest()
        arrive(lead.at[0], lead_recv.at[0])
        hand(0).start()
        hand(1).start()
        w0 = inverse[0]
        l10 = dot_nt(lead[0], w0)
        w10[...] = dot_nn(l10, w0)
        arrive(lead.at[1], lead_recv.at[1])
        work[...] = lead[1] - dot_nt(l10, l10)
        enter()
        signal(go_plane, 1, 0)

    @pl.when(no(corner))
    def _():
        enter()

        @pl.when(hub)
        def _():
            to_corner(0).start()

        @pl.when(last)
        def _():
            to_corner(1).start()

        @pl.when(r == 8)
        def _():
            signal(go_line, 1, c)

        @pl.when(z == door // 2)
        def _():
            signal(go_down, jnp.where(c == 0, 1, core), c)

        @pl.when(both(r == 0, c == 1))
        def _():
            signal(go_plane, 1, 1)

        @pl.when(z == 0)
        def _():
            span(0, CHUNKS, line_up)

        load_rest()

        @pl.when(both(r == 1, left))
        def _():
            pl.semaphore_wait(go_plane, 1)

        @pl.when(left)
        def _():
            plane_scatter()

        @pl.when(hub)
        def _():
            arrive(handed, hand_recv.at[0])
            for p in (*range(n // 2, n), *range(1, n // 2)):
                hand_scatter(p).start()
            arrive(cbuf.at[0], hand_recv.at[1])
            span(0, CHUNKS, lambda k: hand_next(k, 0).start())
            pl.semaphore_wait(go_down, 2)
            span(0, CHUNKS, lambda k: hand_next(k, 1).start())

        @pl.when(z == 0)
        def _():
            @pl.when(no(hub))
            def _():
                pl.semaphore_wait(go_down, 1)

            span(0, CHUNKS, line_down)

        def by_plane(counts):
            value = counts[0]
            for k in range(1, 8):
                value = jnp.where(z == k, counts[k], value)
            return value

        early = by_plane(EARLY)
        mid = by_plane(MID)

        @pl.when(z > 0)
        def _():
            span(0, early, line_relay)

        plane_gather()

        @pl.when(z > 0)
        def _():
            span(early, mid, line_relay)

        @pl.when(core == 1)
        def _():
            pass_w()

        @pl.when(z > 0)
        def _():
            span(mid, CHUNKS, line_relay)

        @pl.when(core == 1)
        def _():
            for g in range(4):
                @pl.when(x == g)
                def _():
                    arrive(wbuf.at[pl.ds(4 * g, 3)], w_gather.at[g])

                @pl.when(x != g)
                def _():
                    arrive(wbuf.at[pl.ds(4 * g, 4)], w_gather.at[g])

                w_beside(g).start()

    @pl.when(corner)
    def _():
        work[...] = panel[0:NB, :]

        def block(b, carry):
            factor(work, solved_rows, upper.at[b], inverse.at[b])

            @pl.when(b == 0)
            def _():
                middle()

            return carry

        lax.fori_loop(0, 2, block, 0)
        wown[:, 0] = inverse[0].reshape(n, 8, NB)
        wown[:, 1] = -dot_nn(inverse[1], w10[...]).reshape(n, 8, NB)
        wown[:, 2] = inverse[1].reshape(n, 8, NB)
        for p in range(n):
            w_scatter((p + n // 2) % n).start()
        diagonal().start()
        rbuf[0, 0] = panel[0:32, :]
        plane_gather()
        diag[...] = upper[0]

    @pl.when(z == 0)
    def _():
        cbuf[core] = xv[0:512, :]

    @pl.when(no(hub))
    def _():
        arrive(cbuf.at[1 - core], c_pair)

    for h in range(2):
        for b in range(4):
            ac[h * NB : (h + 1) * NB, b * NB : (b + 1) * NB] = cbuf[h, pl.ds(b, NB, stride=4), :]

    most = n - 1

    @pl.when(hub)
    def _():
        to_corner(0).wait_send()
        arrive(handed.at[pl.ds(0, 32 * most)], hand_rows)
        arrive(cbuf.at[0], hand_line.at[0])
        arrive(cbuf.at[0], hand_line.at[1])

    @pl.when(last)
    def _():
        to_corner(1).wait_send()

    @pl.when(both(left, no(corner)))
    def _():
        arrive(panel.at[pl.ds(0, 32 * most)], r_send_a)

    @pl.when(r == 1)
    def _():
        arrive(wbuf.at[pl.ds(0, n // 2 - 1)], w_send_b)

    @pl.when(either(both(z == 0, no(corner)), up))
    def _():
        arrive(cbuf.at[core], c_send.at[0])

    @pl.when(either(both(z == 0, no(corner)), down))
    def _():
        arrive(cbuf.at[core], c_send.at[1])

    @pl.when(no(corner))
    def _():
        arrive(cbuf.at[core], c_pair_send)

    @pl.when(core == 0)
    def _():
        arrive(wbuf, w_pair)

    w00 = wbuf[:, 0].reshape(NB, NB)
    w01 = wbuf[:, 1].reshape(NB, NB)
    w11 = wbuf[:, 2].reshape(NB, NB)
    lower = jnp.concatenate(
        [
            jnp.concatenate([w00, jnp.zeros((NB, NB), F32)], axis=1),
            jnp.concatenate([w01, w11], axis=1),
        ],
        axis=0,
    )
    pc[...] = dot_nn(lower, ac[...])
    arrive(rbuf.at[pl.ds(0, n - 1)], r_gather)
    r0 = rbuf[:, 0].reshape(4 * NB, NB)
    r1 = rbuf[:, 1].reshape(4 * NB, NB)
    pr[...] = dot_nt(jnp.concatenate([r0, r1], axis=1), lower)

    @pl.when(last)
    def _():
        arrive(diag, diag_recv)

    @pl.when(corner)
    def _():
        arrive(wown, w_send_a)
        diagonal().wait_send()
        hand(0).wait_send()
        hand(1).wait_send()

    arrive(rbuf.at[pl.ds(0, most)], r_send_b)

    @pl.when(core == 1)
    def _():
        arrive(wbuf.at[pl.ds(0, most)], w_send_c)
        arrive(wbuf, w_pair_send)


def update_kernel(x, pr, pc, diag, out, parts, sems):
    r = lax.axis_index("row")
    c = lax.axis_index("col")
    both = jnp.logical_and

    def store(a):
        whole = pl.ds(4 * STARTS[a], 4 * (STARTS[a + 1] - STARTS[a]))
        return pltpu.make_async_copy(parts.at[whole], out.at[whole], sems.at[a])

    for a in range(len(STARTS) - 1):
        at = slice(STARTS[a], STARTS[a + 1])
        count = STARTS[a + 1] - STARTS[a]

        def rows(b):
            return pl.ds(4 * STARTS[a] + b, count, stride=4)

        def put(b, value):
            parts[rows(b), :] = value

        def update():
            delta = dot_nn(pr[at, :], pc[...])
            for b in range(4):
                put(b, x[rows(b), :] - delta[:, b * NB : (b + 1) * NB])

            @pl.when(c == 0)
            def _():
                put(0, pr[at, 0:NB])

            @pl.when(c == 1)
            def _():
                put(0, pr[at, NB:])

        if a > 0:
            update()
        else:

            @pl.when(r < 2)
            def _():
                parts[0:512, :] = jnp.zeros((512, NB), F32)

                @pl.when(both(r == 1, c == 0))
                def _():
                    put(0, pr[at, 0:NB])

                @pl.when(both(r == c, c < 2))
                def _():
                    put(0, diag[...].T)

            @pl.when(r >= 2)
            def _():
                update()

        store(a).start()

    for a in range(len(STARTS) - 1):
        store(a).wait()


def per_device(matrix):
    n = lax.axis_size("row")
    flat = matrix.reshape(2048, NB)
    dma = pltpu.SemaphoreType.DMA
    square = pltpu.VMEM((NB, NB), F32)
    whole = pl.BlockSpec(memory_space=pltpu.VMEM)
    flat = pltpu.with_memory_space_constraint(flat, pltpu.HBM)
    pr, pc, diag, x = pl.pallas_call(
        functools.partial(gather_kernel, n),
        out_shape=[
            pltpu.VMEM((4 * NB, 2 * NB), F32),
            pltpu.VMEM((2 * NB, 4 * NB), F32),
            square,
            pltpu.VMEM((2048, NB), F32),
        ],
        in_specs=[pl.BlockSpec(memory_space=pl.ANY)],
        out_specs=[whole] * 4,
        scratch_shapes=[
            pltpu.VMEM((512, NB), F32),
            pltpu.VMEM((2, NB, NB), F32),
            pltpu.VMEM((n, 2, 32, NB), F32),
            pltpu.VMEM((2, 512, NB), F32),
            pltpu.VMEM((n, 3, 8, NB), F32),
            pltpu.VMEM((n, 3, 8, NB), F32),
            pltpu.VMEM((2 * NB, 4 * NB), F32),
            square,
            square,
            pltpu.VMEM((2, NB, NB), F32),
            pltpu.VMEM((2, NB, NB), F32),
            square,
            pltpu.VMEM((512, NB), F32),
            dma((2,)),
            dma((2,)),
            dma,
            dma,
            dma,
            pltpu.SemaphoreType.REGULAR,
            pltpu.SemaphoreType.REGULAR,
            pltpu.SemaphoreType.REGULAR,
            dma((2,)),
            dma((2,)),
            dma,
            dma((2,)),
            dma((2,)),
            dma,
            dma,
            dma,
            dma((CHUNKS,)),
            dma((2,)),
            dma,
            dma,
            dma,
            dma((4,)),
            dma,
            dma,
            dma,
            dma,
            dma,
        ],
        compiler_params=pltpu.CompilerParams(
            collective_id=0, has_side_effects=True, vmem_limit_bytes=24 * 1024 * 1024
        ),
    )(flat)
    out = pl.pallas_call(
        update_kernel,
        out_shape=pltpu.HBM((2048, NB), F32),
        in_specs=[whole] * 4,
        out_specs=pl.BlockSpec(memory_space=pltpu.HBM),
        scratch_shapes=[pltpu.VMEM((2048, NB), F32), dma((len(STARTS) - 1,))],
        compiler_params=pltpu.CompilerParams(vmem_limit_bytes=24 * 1024 * 1024),
    )(x, pr, pc, diag)
    return out.reshape(matrix.shape)


def solution(mesh):
    specs = P(None, "row", None, None, "col", None)
    return jax.shard_map(
        per_device, mesh=mesh, in_specs=(specs,), out_specs=specs, check_vma=False
    )
```

```python
import functools

import jax
import jax.numpy as jnp
from jax import lax
from jax.experimental import pallas as pl
from jax.experimental.pallas import tpu as pltpu
from jax.sharding import PartitionSpec as P

F32 = jnp.float32
MESH = pl.DeviceIdType.MESH
HIGHEST = lax.Precision.HIGHEST
NB = 128
LOOK = 2
STARTS = (0, 128, 512)
CHUNK = 64
CHUNKS = 512 // CHUNK
EARLY = (0, 6, 4, 2, 0, 0, 0, 1)
MID = (0, 8, 8, 8, 6, 0, 2, 4)
R_FIRST = (0, 3)
R_LATER = (1, 2)
W_ORDER = (0, 1, 2, 3)


def dot_nn(a, b):
    return jnp.dot(a, b, precision=HIGHEST, preferred_element_type=F32)


def dot_nt(a, b):
    return lax.dot_general(
        a, b, (((1,), (1,)), ((), ())), precision=HIGHEST, preferred_element_type=F32
    )


def row_splat(tile, k):
    return jnp.broadcast_to(tile[k : k + 1, :], (8, NB))


def lane_splat(tile, k):
    return jnp.broadcast_to(tile[:, k : k + 1], (8, NB))


def eliminate(rows, rows_identity, columns):
    sub = lax.broadcasted_iota(jnp.int32, (8, NB), 0)
    columns = list(columns)
    upper, inverse, solved = rows, rows_identity, rows_identity
    scale = jnp.ones((8, NB), F32)
    for k in range(8):
        pivot = row_splat(columns[k], k)
        over = 1.0 / pivot
        here = sub == k
        ratio = columns[k] * over
        below = jnp.where(sub > k, ratio, 0.0)
        for j in range(k + 1, 8):
            r = row_splat(columns[j], k)
            columns[j] = jnp.where(here, r * over, columns[j] - ratio * r)
        upper = upper - below * row_splat(upper, k)
        inverse = inverse - below * row_splat(inverse, k)
        r = row_splat(solved, k)
        solved = jnp.where(here, r * over, solved - ratio * r)
        scale = jnp.where(here, lax.rsqrt(pivot), scale)
    return upper * scale, inverse * scale, solved


def factor(work, solved_rows, upper, inverse):
    lane = lax.broadcasted_iota(jnp.int32, (8, NB), 1)
    sub = lax.broadcasted_iota(jnp.int32, (8, NB), 0)
    solved_rows[...] = jnp.zeros((NB, NB), F32)
    steps = NB // 8
    for t in range(steps):
        o = 8 * t
        rows = work[o : o + 8, :]
        columns = [lane_splat(rows, o + j) for j in range(8)]
        block = (lane >= o) & (lane < o + 8)
        rows_identity = jnp.where(block, (lane - o == sub).astype(F32), rows)
        up, inv, solved = eliminate(rows, rows_identity, columns)
        upper[o : o + 8, :] = jnp.where(lane >= o, up, 0.0)
        inverse[o : o + 8, :] = jnp.where(lane < o + 8, inv, 0.0)
        solved_rows[o : o + 8, :] = solved
        splats = [row_splat(solved, j) for j in range(8)]
        for i in range(t + 1, min(t + 1 + LOOK, steps)):
            tile = work[8 * i : 8 * i + 8, :]
            total = jnp.where(block, 0.0, tile)
            for j in range(8):
                total = total - lane_splat(tile, o + j) * splats[j]
            work[8 * i : 8 * i + 8, :] = total
        rest = 8 * (t + 1 + LOOK)
        if rest < NB:
            tiles = work[rest:, :]
            lanes = lax.broadcasted_iota(jnp.int32, (NB - rest, NB), 1)
            own = (lanes >= o) & (lanes < o + 8)
            work[rest:, :] = jnp.where(own, 0.0, tiles) - dot_nn(
                jnp.where(own, tiles, 0.0), solved_rows[...]
            )


def gather_kernel(
    n,
    x_hbm,
    pr,
    pc,
    diag,
    xv,
    panel,
    lead,
    rbuf,
    cbuf,
    wbuf,
    wown,
    ac,
    work,
    solved_rows,
    upper,
    inverse,
    w10,
    handed,
    load_sem,
    lead_recv,
    lead_send,
    diag_recv,
    diag_send,
    go_plane,
    go_line,
    go_down,
    hand_recv,
    hand_send,
    hand_rows,
    hand_line,
    r_piece,
    r_gather,
    r_send_a,
    r_send_b,
    c_recv,
    c_send,
    c_pair,
    c_pair_send,
    w_piece,
    w_gather,
    w_send_a,
    w_send_b,
    w_send_c,
    w_pair,
    w_pair_send,
):
    r = lax.axis_index("row")
    c = lax.axis_index("col")
    z = r // 2
    x = c // 4
    y = lax.rem(c, 4)
    ys = [lax.rem(y + j, 4) for j in range(4)]
    core = lax.rem(r, 2)
    pair = r + 1 - 2 * core
    both, either, no = jnp.logical_and, jnp.logical_or, jnp.logical_not
    left = c < 2
    corner = both(r == 0, c == 0)
    last = both(r == 1, c == 1)

    def span(first, end, body):
        def step(k, carry):
            body(k)
            return carry

        lax.fori_loop(first, end, step, 0)

    def each(body):
        span(1, n, body)

    def other(me, k):
        return lax.rem(me + k, n)

    def copy(src, dst, send, recv, row, col):
        return pltpu.make_async_remote_copy(
            src_ref=src,
            dst_ref=dst,
            send_sem=send,
            recv_sem=recv,
            device_id=(row, col),
            device_id_type=MESH,
        )

    def signal(sem, row, col):
        pl.semaphore_signal(sem, inc=1, device_id=(row, col), device_id_type=MESH)

    def arrive(buffer, sem):
        pltpu.make_async_copy(buffer, buffer, sem).wait()

    top = pltpu.make_async_copy(x_hbm.at[pl.ds(0, 512)], xv.at[pl.ds(0, 512)], load_sem.at[0])
    below = pltpu.make_async_copy(
        x_hbm.at[pl.ds(512, 1536)], xv.at[pl.ds(512, 1536)], load_sem.at[1]
    )
    top.start()
    below.start()

    hub = both(r == 1, c == 0)
    barrier = pltpu.get_barrier_semaphore()
    door = jnp.where(left, 2, 12)
    before = jnp.where(z < 5, r - 2, jnp.where(z < 7, r + 2, door + core))
    signal(barrier, pair, c)

    @pl.when(z > 0)
    def _():
        signal(barrier, before, c)

    @pl.when(z != 4)
    def _():
        signal(barrier, 8, c)

    @pl.when(either(hub, both(z == 0, c != 0)))
    def _():
        signal(barrier, door + core, c)

    @pl.when(hub)
    def _():
        signal(barrier, door, c)

    for k in range(2):

        @pl.when(c != k)
        def _():
            signal(barrier, jnp.where(z > 0, r, 0), k)

    @pl.when(corner)
    def _():
        signal(barrier, 1, 1)

    top.wait()

    @pl.when(left)
    def _():
        panel[0:NB, :] = xv[pl.ds(0, NB, stride=4), :]

    def load_rest():
        below.wait()

        @pl.when(left)
        def _():
            panel[NB:, :] = xv[pl.ds(512, 384, stride=4), :]

    def enter():
        after = jnp.where(either(z == 4, z == 5), 0, 1)
        heard = (
            1
            + after
            + jnp.where(z == door // 2, 2, 0)
            + jnp.where(r == 8, n - 2, 0)
            + jnp.where(both(z > 0, left), n - 1, 0)
            + jnp.where(both(r == 0, left), 2 * (n - 1), 0)
            + jnp.where(last, 1, 0)
        )
        pl.semaphore_wait(barrier, heard)

    def to_corner(b):
        return copy(panel.at[pl.ds(0, NB)], lead.at[b], lead_send, lead_recv.at[b], 0, 0)

    def r_scatter(p):
        return copy(
            panel.at[pl.ds(p * 32, 32)],
            rbuf.at[p, c],
            r_send_a,
            r_piece.at[c],
            r,
            p,
        )

    def r_across(p):
        return copy(rbuf.at[c], rbuf.at[c], r_send_b, r_gather, r, p)

    def plane_scatter():
        for p in (*range(n // 2, n), *range(2, n // 2)):
            r_scatter(p).start()
        for p in range(2):

            @pl.when(c != p)
            def _():
                r_scatter(p).start()

        rbuf[c, c] = panel[pl.ds(pl.multiple_of(c * 32, 32), 32), :]

    def columns(make, xs):
        for there in xs:
            for j in (2, 1, 3, 0):
                p = 4 * there + ys[j]

                @pl.when(p != c)
                def _():
                    make(p).start()

    def r_batch(first):
        def send(k):
            p = other(c, k)
            early = either(p < 4, p >= 12)

            @pl.when(early if first else no(early))
            def _():
                r_across(p).start()

        each(send)

    def plane_gather():
        @pl.when(c != 0)
        def _():
            arrive(rbuf.at[c, 0], r_piece.at[0])

        @pl.when(c != 1)
        def _():
            arrive(rbuf.at[c, 1], r_piece.at[1])

        r_batch(True)

        @pl.when(core == 0)
        def _():
            r_batch(False)

    def chunk(k):
        return cbuf.at[core, pl.ds(pl.multiple_of(k * CHUNK, CHUNK), CHUNK)]

    def first_chunk(k):
        return xv.at[pl.ds(pl.multiple_of(k * CHUNK, CHUNK), CHUNK)]

    def c_next(k, way, src):
        there = lax.rem(r + 2 + way * (n - 4), n)
        return copy(src, chunk(k), c_send.at[way], c_recv.at[k], there, c)

    def c_beside(k, src):
        return copy(src, chunk(k), c_pair_send, c_pair, pair, c)

    def line_up(k):
        c_next(k, 0, first_chunk(k)).start()
        c_beside(k, first_chunk(k)).start()

    def line_down(k):
        c_next(k, 1, first_chunk(k)).start()

    up = both(z >= 1, z <= 3)
    down = z >= 6

    def line_relay(k):
        arrive(chunk(k), c_recv.at[k])

        @pl.when(up)
        def _():
            c_next(k, 0, chunk(k)).start()

        @pl.when(down)
        def _():
            c_next(k, 1, chunk(k)).start()

        c_beside(k, chunk(k)).start()

    def w_copy(send, recv, row, col):
        return copy(wbuf.at[c], wbuf.at[c], send, recv, row, col)

    def w_scatter(p):
        return copy(wown.at[p], wbuf.at[p], w_send_a, w_piece, 1, p)

    def w_down(k):
        p = lax.rem(r + 2 * k, n)
        return w_copy(w_send_b, w_piece, p, c)

    def w_across(p):
        return w_copy(w_send_c, w_gather.at[c // 4], r, p)

    def diagonal():
        return copy(upper.at[1], diag, diag_send, diag_recv, 1, 1)

    def w_beside(g):
        part = wbuf.at[pl.ds(4 * g, 4)]
        return copy(part, part, w_pair_send, w_pair, pair, c)

    def pass_w():
        arrive(wbuf.at[c], w_piece)

        @pl.when(r == 1)
        def _():
            pl.semaphore_wait(go_line, 1)
            for k in range(1, n // 2):
                w_down(k).start()

        columns(w_across, W_ORDER)
        r_batch(False)

    def hand(b):
        src = panel if b == 0 else xv.at[pl.ds(0, 512)]
        dst = handed if b == 0 else cbuf.at[0]
        return copy(src, dst, hand_send.at[b], hand_recv.at[b], 1, 0)

    def hand_scatter(p):
        return copy(
            handed.at[pl.ds(p * 32, 32)],
            rbuf.at[p, 0],
            hand_rows,
            r_piece.at[0],
            0,
            p,
        )

    def hand_next(k, way):
        at = cbuf.at[0, pl.ds(pl.multiple_of(k * CHUNK, CHUNK), CHUNK)]
        return copy(at, at, hand_line.at[way], c_recv.at[k], 2 + way * (n - 4), 0)

    def middle():
        load_rest()
        arrive(lead.at[0], lead_recv.at[0])
        hand(0).start()
        hand(1).start()
        w0 = inverse[0]
        l10 = dot_nt(lead[0], w0)
        w10[...] = dot_nn(l10, w0)
        arrive(lead.at[1], lead_recv.at[1])
        work[...] = lead[1] - dot_nt(l10, l10)
        wown[:, 0] = inverse[0].reshape(n, 8, NB)
        enter()
        signal(go_plane, 1, 0)

    @pl.when(no(corner))
    def _():
        enter()

        @pl.when(hub)
        def _():
            to_corner(0).start()

        @pl.when(last)
        def _():
            to_corner(1).start()

        @pl.when(r == 8)
        def _():
            signal(go_line, 1, c)

        @pl.when(z == door // 2)
        def _():
            signal(go_down, jnp.where(c == 0, 1, core), c)

        @pl.when(both(r == 0, c == 1))
        def _():
            signal(go_plane, 1, 1)

        @pl.when(z == 0)
        def _():
            span(0, CHUNKS, line_up)

        load_rest()

        @pl.when(both(r == 1, left))
        def _():
            pl.semaphore_wait(go_plane, 1)

        @pl.when(left)
        def _():
            plane_scatter()

        @pl.when(hub)
        def _():
            arrive(handed, hand_recv.at[0])
            for p in (*range(n // 2, n), *range(1, n // 2)):
                hand_scatter(p).start()
            arrive(cbuf.at[0], hand_recv.at[1])
            span(0, CHUNKS, lambda k: hand_next(k, 0).start())
            pl.semaphore_wait(go_down, 2)
            span(0, CHUNKS, lambda k: hand_next(k, 1).start())

        @pl.when(z == 0)
        def _():
            @pl.when(no(hub))
            def _():
                pl.semaphore_wait(go_down, 1)

            span(0, CHUNKS, line_down)

        def by_plane(counts):
            value = counts[0]
            for k in range(1, 8):
                value = jnp.where(z == k, counts[k], value)
            return value

        early = by_plane(EARLY)
        mid = by_plane(MID)

        @pl.when(z > 0)
        def _():
            span(0, early, line_relay)

        plane_gather()

        @pl.when(z > 0)
        def _():
            span(early, mid, line_relay)

        @pl.when(core == 1)
        def _():
            pass_w()

        @pl.when(z > 0)
        def _():
            span(mid, CHUNKS, line_relay)

        @pl.when(core == 1)
        def _():
            for g in range(4):
                @pl.when(x == g)
                def _():
                    arrive(wbuf.at[pl.ds(4 * g, 3)], w_gather.at[g])

                @pl.when(x != g)
                def _():
                    arrive(wbuf.at[pl.ds(4 * g, 4)], w_gather.at[g])

                w_beside(g).start()

    @pl.when(corner)
    def _():
        work[...] = panel[0:NB, :]

        def block(b, carry):
            factor(work, solved_rows, upper.at[b], inverse.at[b])

            @pl.when(b == 0)
            def _():
                middle()

            return carry

        lax.fori_loop(0, 2, block, 0)
        wown[:, 1] = -dot_nn(inverse[1], w10[...]).reshape(n, 8, NB)
        wown[:, 2] = inverse[1].reshape(n, 8, NB)
        for p in range(n):
            w_scatter((p + n // 2) % n).start()
        diagonal().start()
        rbuf[0, 0] = panel[0:32, :]
        plane_gather()
        diag[...] = upper[0]

    @pl.when(z == 0)
    def _():
        cbuf[core] = xv[0:512, :]

    @pl.when(no(hub))
    def _():
        arrive(cbuf.at[1 - core], c_pair)

    for h in range(2):
        for b in range(4):
            ac[h * NB : (h + 1) * NB, b * NB : (b + 1) * NB] = cbuf[h, pl.ds(b, NB, stride=4), :]

    most = n - 1

    @pl.when(hub)
    def _():
        to_corner(0).wait_send()
        arrive(handed.at[pl.ds(0, 32 * most)], hand_rows)
        arrive(cbuf.at[0], hand_line.at[0])
        arrive(cbuf.at[0], hand_line.at[1])

    @pl.when(last)
    def _():
        to_corner(1).wait_send()

    @pl.when(both(left, no(corner)))
    def _():
        arrive(panel.at[pl.ds(0, 32 * most)], r_send_a)

    @pl.when(r == 1)
    def _():
        arrive(wbuf.at[pl.ds(0, n // 2 - 1)], w_send_b)

    @pl.when(either(both(z == 0, no(corner)), up))
    def _():
        arrive(cbuf.at[core], c_send.at[0])

    @pl.when(either(both(z == 0, no(corner)), down))
    def _():
        arrive(cbuf.at[core], c_send.at[1])

    @pl.when(no(corner))
    def _():
        arrive(cbuf.at[core], c_pair_send)

    @pl.when(core == 0)
    def _():
        arrive(wbuf, w_pair)

    w00 = wbuf[:, 0].reshape(NB, NB)
    w01 = wbuf[:, 1].reshape(NB, NB)
    w11 = wbuf[:, 2].reshape(NB, NB)
    lower = jnp.concatenate(
        [
            jnp.concatenate([w00, jnp.zeros((NB, NB), F32)], axis=1),
            jnp.concatenate([w01, w11], axis=1),
        ],
        axis=0,
    )
    pc[...] = dot_nn(lower, ac[...])
    arrive(rbuf.at[pl.ds(0, n - 1)], r_gather)
    r0 = rbuf[:, 0].reshape(4 * NB, NB)
    r1 = rbuf[:, 1].reshape(4 * NB, NB)
    pr[...] = dot_nt(jnp.concatenate([r0, r1], axis=1), lower)

    @pl.when(last)
    def _():
        arrive(diag, diag_recv)

    @pl.when(corner)
    def _():
        arrive(wown, w_send_a)
        diagonal().wait_send()
        hand(0).wait_send()
        hand(1).wait_send()

    arrive(rbuf.at[pl.ds(0, most)], r_send_b)

    @pl.when(core == 1)
    def _():
        arrive(wbuf.at[pl.ds(0, most)], w_send_c)
        arrive(wbuf, w_pair_send)


def update_kernel(x, pr, pc, diag, out, parts, sems):
    r = lax.axis_index("row")
    c = lax.axis_index("col")
    both = jnp.logical_and

    def store(a):
        whole = pl.ds(4 * STARTS[a], 4 * (STARTS[a + 1] - STARTS[a]))
        return pltpu.make_async_copy(parts.at[whole], out.at[whole], sems.at[a])

    for a in range(len(STARTS) - 1):
        at = slice(STARTS[a], STARTS[a + 1])
        count = STARTS[a + 1] - STARTS[a]

        def rows(b):
            return pl.ds(4 * STARTS[a] + b, count, stride=4)

        def put(b, value):
            parts[rows(b), :] = value

        def update():
            delta = dot_nn(pr[at, :], pc[...])
            for b in range(4):
                put(b, x[rows(b), :] - delta[:, b * NB : (b + 1) * NB])

            @pl.when(c == 0)
            def _():
                put(0, pr[at, 0:NB])

            @pl.when(c == 1)
            def _():
                put(0, pr[at, NB:])

        if a > 0:
            update()
        else:

            @pl.when(r < 2)
            def _():
                parts[0:512, :] = jnp.zeros((512, NB), F32)

                @pl.when(both(r == 1, c == 0))
                def _():
                    put(0, pr[at, 0:NB])

                @pl.when(both(r == c, c < 2))
                def _():
                    put(0, diag[...].T)

            @pl.when(r >= 2)
            def _():
                update()

        store(a).start()

    for a in range(len(STARTS) - 1):
        store(a).wait()


def per_device(matrix):
    n = lax.axis_size("row")
    flat = matrix.reshape(2048, NB)
    dma = pltpu.SemaphoreType.DMA
    square = pltpu.VMEM((NB, NB), F32)
    whole = pl.BlockSpec(memory_space=pltpu.VMEM)
    flat = pltpu.with_memory_space_constraint(flat, pltpu.HBM)
    pr, pc, diag, x = pl.pallas_call(
        functools.partial(gather_kernel, n),
        out_shape=[
            pltpu.VMEM((4 * NB, 2 * NB), F32),
            pltpu.VMEM((2 * NB, 4 * NB), F32),
            square,
            pltpu.VMEM((2048, NB), F32),
        ],
        in_specs=[pl.BlockSpec(memory_space=pl.ANY)],
        out_specs=[whole] * 4,
        scratch_shapes=[
            pltpu.VMEM((512, NB), F32),
            pltpu.VMEM((2, NB, NB), F32),
            pltpu.VMEM((n, 2, 32, NB), F32),
            pltpu.VMEM((2, 512, NB), F32),
            pltpu.VMEM((n, 3, 8, NB), F32),
            pltpu.VMEM((n, 3, 8, NB), F32),
            pltpu.VMEM((2 * NB, 4 * NB), F32),
            square,
            square,
            pltpu.VMEM((2, NB, NB), F32),
            pltpu.VMEM((2, NB, NB), F32),
            square,
            pltpu.VMEM((512, NB), F32),
            dma((2,)),
            dma((2,)),
            dma,
            dma,
            dma,
            pltpu.SemaphoreType.REGULAR,
            pltpu.SemaphoreType.REGULAR,
            pltpu.SemaphoreType.REGULAR,
            dma((2,)),
            dma((2,)),
            dma,
            dma((2,)),
            dma((2,)),
            dma,
            dma,
            dma,
            dma((CHUNKS,)),
            dma((2,)),
            dma,
            dma,
            dma,
            dma((4,)),
            dma,
            dma,
            dma,
            dma,
            dma,
        ],
        compiler_params=pltpu.CompilerParams(
            collective_id=0, has_side_effects=True, vmem_limit_bytes=24 * 1024 * 1024
        ),
    )(flat)
    out = pl.pallas_call(
        update_kernel,
        out_shape=pltpu.HBM((2048, NB), F32),
        in_specs=[whole] * 4,
        out_specs=pl.BlockSpec(memory_space=pltpu.HBM),
        scratch_shapes=[pltpu.VMEM((2048, NB), F32), dma((len(STARTS) - 1,))],
        compiler_params=pltpu.CompilerParams(vmem_limit_bytes=24 * 1024 * 1024),
    )(x, pr, pc, diag)
    return out.reshape(matrix.shape)


def solution(mesh):
    specs = P(None, "row", None, None, "col", None)
    return jax.shard_map(
        per_device, mesh=mesh, in_specs=(specs,), out_specs=specs, check_vma=False
    )
```
